128 devices in a mesh: cache: 16 (over x, z_lo, core), head: 8 (over y, z_hi).
Axes of the slice: x: 4, y: 4, z: 4 (z_hi: 2, z_lo: 2; z = z_hi * 2 + z_lo), core: 2. Of those that a mesh axis runs over, the one named last changes fastest.
Arguments:
- hidden: bfloat16 [2, 2048, 8192], P(None, 'cache', 'head'), may hold values from -6 to 6
- norm_gain: bfloat16 [8192], replicated, may hold values from 0.25 to 1.75
- w_query: bfloat16 [8192, 4096], P(None, 'head'), may hold values from -0.109375 to 0.109375
- key_weight: bfloat16 [8192, 1024], P(None, 'head'), may hold values from -0.109375 to 0.109375
- value_weight: bfloat16 [8192, 1024], P(None, 'head'), may hold values from -0.0625 to 0.0625
- w_out: bfloat16 [4096, 8192], P('head'), may hold values from -0.09375 to 0.09375
- key_cache: bfloat16 [2048, 64, 8, 128], P('cache', None, 'head'), may hold values from -450 to 450
- value_cache: bfloat16 [2048, 64, 8, 128], P('cache', None, 'head'), may hold values from -6 to 6
- tree_pages: int32 [16, 128, 8], P('cache'), may hold values from 0 to 127
- page_fill: int32 [16, 128, 8], P('cache'), may hold values from 1 to 64, as said below
- row_depth: int32 [16, 2048], P('cache'), may hold values from 0 to 8, as said below
- row_length: int32 [2048], P('cache'), may hold values from 0 to 8192, as said below
Outputs:
- attn_out: bfloat16 [2, 2048, 8192], P(None, 'cache', 'head')
The draws below stay inside these ranges and needn't reach their ends.
Inputs may be any that keep to these rules, and one draw needn't show every extreme that they name: `page_fill`: slot 0 of every tree on every block holds 64 tokens, and so does every slot of tree 0 on every block. `row_depth`: the first row of every tree (r % 16 == 0) has depth 8 on every block. `row_length`: equals the sum over blocks c and slots s < row_depth[c, r] of page_fill[c, r // 16, s].
All inputs are finite; a program needn't handle non-finite values.
Results may differ from the reference program's by a relative error of at most 0.012.
The reference program's roundings to bfloat16 on the way count: a program that leaves them out, or rounds other values in their place, can miss the bound.
Values may be sent and summed in bfloat16 or wider, within the bound.
A program may use at most 128 MiB of HBM per device.

```python
import math
import jax
import jax.numpy as jnp
from jax import lax

MODEL_WIDTH = 8192
KEY_VALUE_HEADS = 8
HEAD_SIZE = 128
QUERY_HEADS = 32
NEW_POSITIONS = 2
PAGE_TOKENS = 64
TREE_SLOTS = 8
DEVICE_PAGES = 128
TREE_BRANCHES = 16
BRANCH_ROWS = 2048
TREE_TOTAL = 128
TOTAL_PAGES = 2048
N_CACHE = 16


def radix_tables(key):
    key_pages, key_fill, key_reach, key_depth = jax.random.split(key, 4)
    page_numbers = jax.random.randint(key_pages, (N_CACHE, TREE_TOTAL, TREE_SLOTS), 0, DEVICE_PAGES, dtype=jnp.int32)
    slot_index = jnp.arange(TREE_SLOTS, dtype=jnp.int32)
    tree_index = jnp.arange(TREE_TOTAL, dtype=jnp.int32)
    tokens_used = jax.random.randint(key_fill, (N_CACHE, TREE_TOTAL, TREE_SLOTS), 1, PAGE_TOKENS + 1, dtype=jnp.int32)
    full_slot = (slot_index[None, None, :] == 0) | (tree_index[None, :, None] == 0)
    tokens_used = jnp.where(full_slot, PAGE_TOKENS, tokens_used)
    depth_reach = jax.random.randint(key_reach, (N_CACHE, 1), TREE_SLOTS // 4, TREE_SLOTS + 1, dtype=jnp.int32)
    depths = jax.random.randint(key_depth, (N_CACHE, BRANCH_ROWS), 0, depth_reach + 1, dtype=jnp.int32)
    row_index = jnp.arange(BRANCH_ROWS, dtype=jnp.int32)
    depths = jnp.where((row_index % TREE_BRANCHES == 0)[None, :], TREE_SLOTS, depths)
    tree_of = row_index // TREE_BRANCHES
    per_row = tokens_used[:, tree_of, :]
    used_slots = slot_index[None, None, :] < depths[:, :, None]
    lengths = jnp.sum(jnp.where(used_slots, per_row, 0), axis=(0, 2)).astype(jnp.int32)
    return (page_numbers, tokens_used, depths, lengths)


def draw_tree_pages(key, part):
    shared = radix_tables(key)
    return shared[0]


def draw_page_fill(key, part):
    shared = radix_tables(key)
    return shared[1]


def draw_row_depth(key, part):
    shared = radix_tables(key)
    return shared[2]


def draw_row_length(key, part):
    shared = radix_tables(key)
    return shared[3]


def draw_key_cache(key, part):
    key = jax.random.fold_in(key, 7)
    rotary_base = jnp.clip(jax.random.normal(key, (TOTAL_PAGES, PAGE_TOKENS, KEY_VALUE_HEADS, HEAD_SIZE), jnp.float32), -3.0, 3.0)
    return (1.6 * rotary_base).astype(jnp.bfloat16)


def block_levels(rng, extent, pieces, low, top_value):
    level = 1.0
    for dim, shards_of in pieces:
        heights = jax.random.uniform(jax.random.fold_in(jax.random.fold_in(rng, 6), dim), (shards_of,), jnp.float32, low / len(pieces), top_value / len(pieces))
        level = level * jnp.repeat(jnp.exp(heights), extent[dim] // shards_of).reshape((-1,) + (1,) * (len(extent) - 1 - dim))
    return level


def gaussian(rng, shape, deviation, bound, shards=(), held_as=jnp.bfloat16):
    values = deviation * jax.random.normal(rng, shape, jnp.float32)
    if shards:
        values = values * block_levels(rng, shape, shards, -0.22, 0.18)
    return jnp.clip(values, -bound, bound).astype(held_as)


def setup_inputs(seed: int = 0) -> dict:
    seeds = jax.random.split(jax.random.key(seed), 13)
    hidden = gaussian(seeds[0], (NEW_POSITIONS, BRANCH_ROWS, MODEL_WIDTH), 1.0, 6.0, ((1, 16), (2, 8)))
    norm_gain = jnp.clip(1.0 + 0.15 * jax.random.normal(seeds[1], (MODEL_WIDTH,), jnp.float32), 0.25, 1.75).astype(jnp.bfloat16)
    w_query = gaussian(seeds[2], (MODEL_WIDTH, QUERY_HEADS * HEAD_SIZE), (MODEL_WIDTH * 25 // 64) ** -0.5, 0.109375, ((1, 8),))
    key_weight = gaussian(seeds[3], (MODEL_WIDTH, KEY_VALUE_HEADS * HEAD_SIZE), (MODEL_WIDTH * 25 // 64) ** -0.5, 0.109375, ((1, 8),))
    value_weight = gaussian(seeds[4], (MODEL_WIDTH, KEY_VALUE_HEADS * HEAD_SIZE), MODEL_WIDTH ** -0.5, 0.0625, ((1, 8),))
    w_out = gaussian(seeds[5], (QUERY_HEADS * HEAD_SIZE, MODEL_WIDTH), (QUERY_HEADS * HEAD_SIZE) ** -0.5, 0.09375, ((0, 8),))
    key_cache = draw_key_cache(jax.random.fold_in(seeds[12], 71), 0)
    value_cache = gaussian(seeds[7], (TOTAL_PAGES, PAGE_TOKENS, KEY_VALUE_HEADS, HEAD_SIZE), 1.0, 6.0, ((0, 16), (2, 8)))
    tree_pages = draw_tree_pages(jax.random.fold_in(seeds[12], 71), 0)
    page_fill = draw_page_fill(jax.random.fold_in(seeds[12], 71), 0)
    row_depth = draw_row_depth(jax.random.fold_in(seeds[12], 71), 0)
    row_length = draw_row_length(jax.random.fold_in(seeds[12], 71), 0)
    return dict(hidden=hidden, norm_gain=norm_gain, w_query=w_query, key_weight=key_weight, value_weight=value_weight, w_out=w_out, key_cache=key_cache, value_cache=value_cache, tree_pages=tree_pages, page_fill=page_fill, row_depth=row_depth, row_length=row_length)


ROPE_BASE = 500000.0
EPSILON = 1e-05
LOW_SCORE = -1e+30

def apply_rotary(vectors, position_list):
    half_width = vectors.shape[-1] // 2
    ladder = jnp.arange(half_width, dtype=jnp.float32) * (2.0 / vectors.shape[-1])
    frequency = jnp.power(jnp.float32(ROPE_BASE), -ladder)
    angles = position_list.astype(jnp.float32)[..., None] * frequency
    cosine = jnp.cos(angles)
    sine_part = jnp.sin(angles)
    front_half = vectors[..., :half_width]
    back_half = vectors[..., half_width:]
    return jnp.concatenate([front_half * cosine - back_half * sine_part, back_half * cosine + front_half * sine_part], axis=-1)

def reference(hidden, norm_gain, w_query, key_weight, value_weight, w_out, key_cache, value_cache, tree_pages, page_fill, row_depth, row_length):
    widened = hidden.astype(jnp.float32)
    mean_square = lax.optimization_barrier(jnp.mean(widened * widened, axis=-1, keepdims=True))
    normalized_input = (widened * lax.rsqrt(mean_square + EPSILON) * norm_gain.astype(jnp.float32)).astype(jnp.bfloat16)
    position_list = row_length[None, :] + jnp.arange(NEW_POSITIONS, dtype=jnp.int32)[:, None]
    query = apply_rotary(jnp.dot(normalized_input, w_query, preferred_element_type=jnp.float32).reshape(NEW_POSITIONS, BRANCH_ROWS, QUERY_HEADS, HEAD_SIZE), position_list[:, :, None]).astype(jnp.bfloat16)
    fresh_key = apply_rotary(jnp.dot(normalized_input, key_weight, preferred_element_type=jnp.float32).reshape(NEW_POSITIONS, BRANCH_ROWS, KEY_VALUE_HEADS, HEAD_SIZE), position_list[:, :, None]).astype(jnp.bfloat16)
    fresh_value = jnp.dot(normalized_input, value_weight, preferred_element_type=jnp.float32).astype(jnp.bfloat16).reshape(NEW_POSITIONS, BRANCH_ROWS, KEY_VALUE_HEADS, HEAD_SIZE)
    group_width = QUERY_HEADS // KEY_VALUE_HEADS
    score_scale = 1.0 / math.sqrt(HEAD_SIZE)
    key_block_list = key_cache.reshape(N_CACHE, DEVICE_PAGES, PAGE_TOKENS, KEY_VALUE_HEADS, HEAD_SIZE)
    value_block_list = value_cache.reshape(N_CACHE, DEVICE_PAGES, PAGE_TOKENS, KEY_VALUE_HEADS, HEAD_SIZE)
    block_number = jnp.arange(N_CACHE, dtype=jnp.int32)[:, None]
    column = jnp.arange(TREE_SLOTS * PAGE_TOKENS, dtype=jnp.int32)
    slot_of = column // PAGE_TOKENS
    token_of = column % PAGE_TOKENS
    causal = (jnp.arange(NEW_POSITIONS)[:, None] >= jnp.arange(NEW_POSITIONS)[None, :]).reshape(NEW_POSITIONS, 1, 1, 1, NEW_POSITIONS)

    def tree_attention(inputs):
        query_per_tree, tree_keys, tree_values, page_numbers, page_tokens, depths = inputs
        grouped_queries = query_per_tree.astype(jnp.float32).reshape(NEW_POSITIONS, TREE_BRANCHES, KEY_VALUE_HEADS, group_width, HEAD_SIZE)
        paged_keys = key_block_list[block_number, page_numbers].reshape(N_CACHE, TREE_SLOTS * PAGE_TOKENS, KEY_VALUE_HEADS, HEAD_SIZE).astype(jnp.float32)
        paged_values = value_block_list[block_number, page_numbers].reshape(N_CACHE, TREE_SLOTS * PAGE_TOKENS, KEY_VALUE_HEADS, HEAD_SIZE).astype(jnp.float32)
        scores = jnp.einsum('prkgd,cnkd->prkgcn', grouped_queries, paged_keys) * score_scale
        visible = (slot_of[None, None, :] < depths[:, :, None]) & (token_of[None, None, :] < page_tokens[:, slot_of][:, None, :])
        visible = jnp.transpose(visible, (1, 0, 2))[None, :, None, None, :, :]
        block_max = lax.optimization_barrier(jnp.max(jnp.where(visible, scores, LOW_SCORE), axis=-1))
        rounded = jnp.where(visible, jnp.exp(scores - block_max[..., None]), 0.0).astype(jnp.bfloat16)
        weights = lax.optimization_barrier(rounded).astype(jnp.float32)
        block_total = lax.optimization_barrier(jnp.sum(weights, axis=-1))
        block_out = jnp.einsum('prkgcn,cnkd->prkgcd', weights, paged_values)
        new_scores = jnp.einsum('prkgd,qrkd->prkgq', grouped_queries, tree_keys.astype(jnp.float32)) * score_scale
        new_max = lax.optimization_barrier(jnp.max(jnp.where(causal, new_scores, LOW_SCORE), axis=-1))
        new_rounded = jnp.where(causal, jnp.exp(new_scores - new_max[..., None]), 0.0).astype(jnp.bfloat16)
        new_weights = lax.optimization_barrier(new_rounded).astype(jnp.float32)
        new_total = lax.optimization_barrier(jnp.sum(new_weights, axis=-1))
        new_out = jnp.einsum('prkgq,qrkd->prkgd', new_weights, tree_values.astype(jnp.float32))
        highest = jnp.maximum(new_max, lax.optimization_barrier(jnp.max(block_max, axis=-1)))
        new_scale = jnp.exp(new_max - highest)
        block_scale = jnp.exp(block_max - highest[..., None])
        summed = new_scale * new_total + lax.optimization_barrier(jnp.sum(block_scale * block_total, axis=-1))
        merged = new_scale[..., None] * new_out + lax.optimization_barrier(jnp.sum(block_scale[..., None] * block_out, axis=-2))
        return (merged / summed[..., None]).astype(jnp.bfloat16).reshape(NEW_POSITIONS, TREE_BRANCHES, QUERY_HEADS * HEAD_SIZE)
    query_trees = query.reshape(NEW_POSITIONS, TREE_TOTAL, TREE_BRANCHES, QUERY_HEADS, HEAD_SIZE).transpose(1, 0, 2, 3, 4)
    key_per_tree = fresh_key.reshape(NEW_POSITIONS, TREE_TOTAL, TREE_BRANCHES, KEY_VALUE_HEADS, HEAD_SIZE).transpose(1, 0, 2, 3, 4)
    value_per_tree = fresh_value.reshape(NEW_POSITIONS, TREE_TOTAL, TREE_BRANCHES, KEY_VALUE_HEADS, HEAD_SIZE).transpose(1, 0, 2, 3, 4)
    page_trees = jnp.transpose(tree_pages, (1, 0, 2))
    token_trees = jnp.transpose(page_fill, (1, 0, 2))
    depth_trees = row_depth.reshape(N_CACHE, TREE_TOTAL, TREE_BRANCHES).transpose(1, 0, 2)
    attention = lax.map(tree_attention, (query_trees, key_per_tree, value_per_tree, page_trees, token_trees, depth_trees))
    attention = attention.transpose(1, 0, 2, 3).reshape(NEW_POSITIONS, BRANCH_ROWS, QUERY_HEADS * HEAD_SIZE)
    return jnp.dot(attention, w_out, preferred_element_type=jnp.float32).astype(jnp.bfloat16)
```

```python
import math

import jax
import jax.numpy as jnp
from jax import lax
from jax.experimental import pallas as pl
from jax.experimental.pallas import tpu as pltpu
from jax.sharding import PartitionSpec as P

ROPE_BASE = 500000.0
EPSILON = 1e-05


def apply_rotary(vectors, position_list):
    half_width = vectors.shape[-1] // 2
    ladder = jnp.arange(half_width, dtype=jnp.float32) * (2.0 / vectors.shape[-1])
    frequency = jnp.power(jnp.float32(ROPE_BASE), -ladder)
    angles = position_list.astype(jnp.float32)[..., None] * frequency
    cosine = jnp.cos(angles)
    sine_part = jnp.sin(angles)
    front_half = vectors[..., :half_width]
    back_half = vectors[..., half_width:]
    return jnp.concatenate(
        [front_half * cosine - back_half * sine_part, back_half * cosine + front_half * sine_part],
        axis=-1,
    )


MESH = pl.DeviceIdType.MESH
LOW_SCORE = -1e30
LOW_MAX = -1e29
EXP_SCALE = math.log2(math.e) / math.sqrt(128.0)


def place():
    c = lax.axis_index("cache")
    h = lax.axis_index("head")
    return c // 4, lax.rem(c // 2, 2), lax.rem(c, 2), h


def attention_kernel(
    pages, q_own, key_new, value_new, lim, keys, values,
    out,
    q_all, part, part_stat, got, got_stat, relay, relay_stat, rowed, rowed_stat, fresh, fresh_stat,
    lhs, send_sem, recv_sem,
):
    x, zl, core, h = place()

    def at(dx, dz):
        return (lax.rem(x + dx, 4) * 4 + (zl if dz == 0 else 1 - zl) * 2 + core, h)

    ahead, behind, across = at(1, 0), at(3, 0), at(0, 1)
    barrier = pltpu.get_barrier_semaphore()
    for device in (ahead, behind, across):
        pl.semaphore_signal(barrier, inc=1, device_id=device, device_id_type=MESH)
    pl.semaphore_wait(barrier, 3)

    made = {}

    def send(name, src, dst, device):
        number = len(made)
        copy = pltpu.make_async_remote_copy(
            src_ref=src, dst_ref=dst, send_sem=send_sem.at[number], recv_sem=recv_sem.at[number],
            device_id=device, device_id_type=MESH,
        )
        made[name] = copy
        copy.start()

    def arrived(*names):
        for name in names:
            made[name].wait_recv()

    lhs[128:144, :] = jnp.ones((16, 1024), jnp.bfloat16)
    token = lax.broadcasted_iota(jnp.int32, (1024, 128), 0) % 64
    low_lanes = lax.broadcasted_iota(jnp.int32, (128, 128), 1) < 64

    def block(dx, dz):
        owner = lax.rem(x + dx, 4) * 2 + (zl if dz == 0 else 1 - zl)

        def half_loop(half):
            def tree_step(u, _):
                tree = half * 4 + u
                base = (owner * 8 + tree) * 16
                numbers = [pages[base + i] for i in range(16)]
                k = jnp.concatenate([keys[n] for n in numbers], axis=0)
                q = q_all[dx, dz, half, u]
                s = lax.dot_general(k, q, (((1,), (1,)), ((), ())), preferred_element_type=jnp.float32)
                limits = lim[owner, tree]
                limits = jnp.concatenate(
                    [jnp.broadcast_to(limits[i : i + 1], (64, 128)) for i in range(16)], axis=0
                )
                s = jnp.where(token < limits, s, LOW_SCORE)
                m = jnp.maximum(jnp.max(s, axis=0, keepdims=True), LOW_MAX)
                p = jnp.exp2((s - m) * EXP_SCALE).astype(jnp.bfloat16)
                for i in range(8):
                    lhs[0:128, i * 128 : (i + 1) * 128] = jnp.where(
                        low_lanes, values[numbers[2 * i]], values[numbers[2 * i + 1]]
                    )
                o = jnp.dot(lhs[...], p, preferred_element_type=jnp.float32)
                part[dx, dz, half, u] = o[0:128].astype(jnp.bfloat16)
                part_stat[dx, dz, half, pl.ds(u, 1), :] = m
                part_stat[dx, dz, half, pl.ds(u + 4, 1), :] = o[128:129]
                return 0

            lax.fori_loop(0, 4, tree_step, 0)

        for half in (0, 1):
            half_loop(half)
            if dx in (1, 3):
                to, slot = (ahead, 0) if dx == 1 else (behind, 1)
                send(f"o{dx}{dz}{half}", part.at[dx, dz, half], got.at[slot, dz, half], to)
                send(f"s{dx}{dz}{half}", part_stat.at[dx, dz, half], got_stat.at[slot, dz, half], to)
            if dx == 2:
                to = ahead if half == 0 else behind
                send(f"o2{dz}{half}", part.at[dx, dz, half], relay.at[dz, half], to)
                send(f"s2{dz}{half}", part_stat.at[dx, dz, half], relay_stat.at[dz, half], to)

    def pass_on(dz):
        for half in (0, 1):
            to = ahead if half == 0 else behind
            arrived(f"o2{dz}{half}", f"s2{dz}{half}")
            send(f"or{dz}{half}", relay.at[dz, half], got.at[2, dz, half], to)
            send(f"sr{dz}{half}", relay_stat.at[dz, half], got_stat.at[2, dz, half], to)

    def merged(pieces, u):
        tops = [stat[pl.ds(u, 1), :] for _, stat in pieces]
        top = tops[0]
        for other in tops[1:]:
            top = jnp.maximum(top, other)
        total = jnp.zeros((1, 128), jnp.float32)
        sums = jnp.zeros((128, 128), jnp.float32)
        for (o, stat), m in zip(pieces, tops):
            w = jnp.exp2((m - top) * EXP_SCALE)
            total += w * stat[pl.ds(u + 4, 1), :]
            sums += w * o[u].astype(jnp.float32)
        return top, total, sums

    q_all[0, 0] = q_own[...]
    send("q30", q_all.at[0, 0], q_all.at[3, 0], ahead)
    send("q10", q_all.at[0, 0], q_all.at[1, 0], behind)
    send("q01", q_all.at[0, 0], q_all.at[0, 1], across)

    spot_k = lax.broadcasted_iota(jnp.int32, (32, 128), 0)
    spot_q = lax.broadcasted_iota(jnp.int32, (32, 128), 1)
    seen = (spot_k % 16 == spot_q % 16) & (spot_k // 16 <= spot_q // 64)
    for half in (0, 1):
        def new_step(u, _):
            q = q_all[0, 0, half, u]
            s = lax.dot_general(
                key_new[half * 4 + u], q, (((1,), (1,)), ((), ())), preferred_element_type=jnp.float32
            )
            s = jnp.where(seen, s, LOW_SCORE)
            m = jnp.max(s, axis=0, keepdims=True)
            p = jnp.exp2((s - m) * EXP_SCALE).astype(jnp.bfloat16)
            o = lax.dot_general(
                value_new[half * 4 + u], p, (((0,), (0,)), ((), ())), preferred_element_type=jnp.float32
            )
            fresh[half, u] = o.astype(jnp.bfloat16)
            fresh_stat[half, pl.ds(u, 1), :] = m
            fresh_stat[half, pl.ds(u + 4, 1), :] = jnp.sum(p.astype(jnp.float32), axis=0, keepdims=True)
            return 0

        lax.fori_loop(0, 4, new_step, 0)

    block(0, 0)
    arrived("q30")
    send("q20a", q_all.at[3, 0, 0], q_all.at[2, 0, 0], ahead)
    arrived("q10")
    send("q20b", q_all.at[1, 0, 1], q_all.at[2, 0, 1], behind)
    arrived("q01")
    send("q31", q_all.at[0, 1], q_all.at[3, 1], ahead)
    send("q11", q_all.at[0, 1], q_all.at[1, 1], behind)
    block(1, 0)
    block(3, 0)
    arrived("q20a")
    send("q21a", q_all.at[2, 0, 0], q_all.at[2, 1, 0], across)
    arrived("q20b")
    send("q21b", q_all.at[2, 0, 1], q_all.at[2, 1, 1], across)
    block(2, 0)
    arrived("q11", "q31")
    block(1, 1)
    block(3, 1)
    pass_on(0)
    arrived("q21a", "q21b")
    block(2, 1)
    block(0, 1)
    pass_on(1)
    for half in (0, 1):
        arrived(*[f"{a}{b}1{half}" for a in "os" for b in (1, 3)], f"or1{half}", f"sr1{half}")
        pieces = [(part.at[0, 1, half], part_stat.at[0, 1, half])]
        pieces += [(got.at[i, 1, half], got_stat.at[i, 1, half]) for i in range(3)]

        def row_step(u, _):
            top, total, sums = merged(pieces, u)
            rowed[0, half, u] = sums.astype(jnp.bfloat16)
            rowed_stat[0, half, pl.ds(u, 1), :] = top
            rowed_stat[0, half, pl.ds(u + 4, 1), :] = total
            return 0

        lax.fori_loop(0, 4, row_step, 0)
        send(f"oz{half}", rowed.at[0, half], rowed.at[1, half], across)
        send(f"sz{half}", rowed_stat.at[0, half], rowed_stat.at[1, half], across)
    for half in (0, 1):
        arrived(*[f"{a}{b}0{half}" for a in "os" for b in (1, 3)], f"or0{half}", f"sr0{half}")
        arrived(f"oz{half}", f"sz{half}")
        pieces = [(part.at[0, 0, half], part_stat.at[0, 0, half])]
        pieces += [(got.at[i, 0, half], got_stat.at[i, 0, half]) for i in range(3)]
        pieces += [(rowed.at[1, half], rowed_stat.at[1, half]), (fresh.at[half], fresh_stat.at[half])]

        def last_step(u, _):
            top, total, sums = merged(pieces, u)
            out[half * 4 + u] = jnp.transpose(sums / total).astype(jnp.bfloat16)
            return 0

        lax.fori_loop(0, 4, last_step, 0)
    for copy in made.values():
        copy.wait_send()


def attention_call(pages, q_own, key_new, value_new, lim, keys, values):
    blk = (2, 4, 128, 128)
    st = (2, 8, 128)
    bf, f32 = jnp.bfloat16, jnp.float32
    vm = pl.BlockSpec(memory_space=pltpu.VMEM)
    return pl.pallas_call(
        attention_kernel,
        out_shape=jax.ShapeDtypeStruct((8, 128, 128), bf),
        in_specs=[pl.BlockSpec(memory_space=pltpu.SMEM)] + [vm] * 6,
        out_specs=vm,
        scratch_shapes=[
            pltpu.VMEM((4, 2) + blk, bf),
            pltpu.VMEM((4, 2) + blk, bf),
            pltpu.VMEM((4, 2) + st, f32),
            pltpu.VMEM((3, 2) + blk, bf),
            pltpu.VMEM((3, 2) + st, f32),
            pltpu.VMEM((2,) + blk, bf),
            pltpu.VMEM((2,) + st, f32),
            pltpu.VMEM((2,) + blk, bf),
            pltpu.VMEM((2,) + st, f32),
            pltpu.VMEM(blk, bf),
            pltpu.VMEM(st, f32),
            pltpu.VMEM((144, 1024), bf),
            pltpu.SemaphoreType.DMA((48,)),
            pltpu.SemaphoreType.DMA((48,)),
        ],
        compiler_params=pltpu.CompilerParams(
            collective_id=2, has_side_effects=True, vmem_limit_bytes=50 * 2**20
        ),
        cost_estimate=pl.CostEstimate(flops=9 * 10**9, bytes_accessed=16 * 2**20, transcendentals=10**7),
    )(pages, q_own.reshape((2, 4, 128, 128)), key_new, value_new, lim, keys, values)


def sibling(array):
    return lax.ppermute(array, "cache", [(i, i ^ 1) for i in range(16)])


def tables(tree_pages, page_fill, row_depth):
    core = lax.rem(lax.axis_index("cache"), 2)
    pages = tree_pages[0].reshape(8, 2, 8, 8)
    fill = page_fill[0].reshape(8, 2, 8, 8)
    depth = row_depth[0].reshape(8, 2, 8, 16)
    packed = jnp.concatenate([pages, fill, depth], axis=-1)
    mine = lax.dynamic_index_in_dim(packed, core, 1, keepdims=False)
    theirs = sibling(lax.dynamic_index_in_dim(packed, 1 - core, 1, keepdims=False))

    def limits(t):
        lanes = jnp.tile(t[..., None, 16:32], (1, 1, 1, 8))
        slot = jnp.arange(8, dtype=jnp.int32)[:, None]
        return jnp.where(slot < lanes, t[..., 8:16, None], 0)

    numbers = jnp.concatenate([mine[..., :8], theirs[..., :8] + 128], axis=-1)
    lim = jnp.concatenate([limits(mine), limits(theirs)], axis=2)
    return numbers.reshape(-1), lim


def body(
    hidden,
    norm_gain,
    w_query,
    key_weight,
    value_weight,
    w_out,
    key_cache,
    value_cache,
    tree_pages,
    page_fill,
    row_depth,
    row_length,
):
    positions_n = hidden.shape[0]
    local_rows = hidden.shape[1]
    page_size = key_cache.shape[1]
    kv_local = key_cache.shape[2]
    head_dim = key_cache.shape[3]
    query_local = w_query.shape[1] // head_dim
    full_rows = lax.all_gather(hidden, "head", axis=2, tiled=True)
    widened = full_rows.astype(jnp.float32)
    mean_square = jnp.mean(widened * widened, axis=-1, keepdims=True)
    normalized_input = (
        widened * lax.rsqrt(mean_square + EPSILON) * norm_gain.astype(jnp.float32)
    ).astype(jnp.bfloat16)
    position_list = row_length[None, :] + jnp.arange(positions_n, dtype=jnp.int32)[:, None]
    query = apply_rotary(
        jnp.dot(normalized_input, w_query, preferred_element_type=jnp.float32).reshape(
            positions_n, local_rows, query_local, head_dim
        ),
        position_list[:, :, None],
    ).astype(jnp.bfloat16)
    fresh_key = apply_rotary(
        jnp.dot(normalized_input, key_weight, preferred_element_type=jnp.float32).reshape(
            positions_n, local_rows, kv_local, head_dim
        ),
        position_list[:, :, None],
    ).astype(jnp.bfloat16)
    fresh_value = (
        jnp.dot(normalized_input, value_weight, preferred_element_type=jnp.float32)
        .astype(jnp.bfloat16)
        .reshape(positions_n, local_rows, kv_local, head_dim)
    )
    trees = local_rows // 16
    own = query.reshape(positions_n, trees, 16, query_local, head_dim).transpose(1, 0, 3, 2, 4)
    own = own.reshape(trees, 128, head_dim)
    new_k = fresh_key.reshape(positions_n, trees, 16, head_dim).transpose(1, 0, 2, 3).reshape(trees, 32, head_dim)
    new_v = fresh_value.reshape(positions_n, trees, 16, head_dim).transpose(1, 0, 2, 3).reshape(trees, 32, head_dim)
    keys = key_cache.reshape(128, page_size, head_dim)
    values = jnp.transpose(value_cache.reshape(128, page_size, head_dim), (0, 2, 1))
    keys = jnp.concatenate([keys, sibling(keys)], axis=0)
    values = jnp.concatenate([values, sibling(values)], axis=0)
    values = jnp.concatenate([values, values], axis=2)
    numbers, lim = tables(tree_pages, page_fill, row_depth)
    attention = attention_call(numbers, own, new_k, new_v, lim, keys, values)
    attention = attention.reshape(trees, positions_n, query_local, 16, head_dim).transpose(1, 0, 3, 2, 4)
    flat_attention = attention.reshape(positions_n * local_rows, query_local * head_dim)
    out_rows = w_out.shape[1] // lax.axis_size("head")
    reduced = lax.psum_scatter(
        lax.dot_general(
            w_out, flat_attention, (((0,), (1,)), ((), ())), preferred_element_type=jnp.float32
        ),
        "head",
        scatter_dimension=0,
        tiled=True,
    )
    return (
        reduced.reshape(out_rows, positions_n, local_rows).transpose(1, 2, 0).astype(jnp.bfloat16)
    )


def solution(mesh):
    in_specs = (
        P(None, "cache", "head"),
        P(),
        P(None, "head"),
        P(None, "head"),
        P(None, "head"),
        P("head", None),
        P("cache", None, "head", None),
        P("cache", None, "head", None),
        P("cache", None, None),
        P("cache", None, None),
        P("cache", None),
        P("cache"),
    )
    out_specs = P(None, "cache", "head")
    return jax.shard_map(body, mesh=mesh, in_specs=in_specs, out_specs=out_specs, check_vma=False)
```

```python
import math

import jax
import jax.numpy as jnp
from jax import lax
from jax.experimental import pallas as pl
from jax.experimental.pallas import tpu as pltpu
from jax.sharding import PartitionSpec as P


MESH = pl.DeviceIdType.MESH
ROPE_BASE = 500000.0
EPSILON = 1e-05
LOW_SCORE = -1e30
LOW_MAX = -1e29
EXP_SCALE = math.log2(math.e) / math.sqrt(128.0)


def place():
    c = lax.axis_index("cache")
    h = lax.axis_index("head")
    return c // 4, lax.rem(c // 2, 2), lax.rem(c, 2), h


def column_place():
    h = lax.axis_index("head")
    return lax.axis_index("cache"), h // 2, lax.rem(h, 2)


def sender(send_sem, recv_sem):
    made = {}

    def send(name, src, dst, device):
        number = len(made)
        copy = pltpu.make_async_remote_copy(
            src_ref=src, dst_ref=dst, send_sem=send_sem.at[number], recv_sem=recv_sem.at[number],
            device_id=device, device_id_type=MESH,
        )
        made[name] = copy
        copy.start()

    def arrived(*names):
        for name in names:
            made[name].wait_recv()

    return made, send, arrived


def project_kernel(
    hidden, gain, cosine, sine, w_query, key_weight, value_weight,
    query, key_new, value_new,
    held, stat, weight, total, send_sem, recv_sem, weight_sem,
):
    c, y, zh = column_place()
    me = y * 2 + zh

    def at(dy, dz):
        return (c, lax.rem(y + dy, 4) * 2 + (zh if dz == 0 else 1 - zh))

    spots = [(dy, dz) for dy in range(4) for dz in range(2)]
    order = [(0, 0), (1, 0), (3, 0), (0, 1), (2, 0), (1, 1), (3, 1), (2, 1)]
    loads = {}
    for number, (dy, dz) in enumerate(order):
        rows = pl.ds(pl.multiple_of(at(dy, dz)[1] * 1024, 1024), 1024)
        for part, (array, low, width) in enumerate(
            ((w_query, 0, 512), (key_weight, 512, 128), (value_weight, 640, 128))
        ):
            load = pltpu.make_async_copy(
                array.at[rows], weight.at[number, :, pl.ds(low, width)], weight_sem.at[number * 3 + part]
            )
            load.start()
            loads[number, part] = load
    barrier = pltpu.get_barrier_semaphore()
    for spot in spots[1:]:
        pl.semaphore_signal(barrier, inc=1, device_id=at(*spot), device_id_type=MESH)
    pl.semaphore_wait(barrier, 7)
    made, send, arrived = sender(send_sem, recv_sem)
    ahead, behind, across = at(1, 0), at(3, 0), at(0, 1)

    for p in range(2):
        send(f"{p}30", hidden.at[p], held.at[p, 3, 0], ahead)
        send(f"{p}10", hidden.at[p], held.at[p, 1, 0], behind)
        send(f"{p}01", hidden.at[p], held.at[p, 0, 1], across)
    for p in range(2):
        wide = hidden[p].astype(jnp.float32)
        squares = jnp.sum(wide * wide, axis=-1, keepdims=True)
        stat[0, 0, pl.ds(p, 1)] = jnp.transpose(jnp.broadcast_to(squares, (128, 128)))[0:1]
    for dy, dz in spots[1:]:
        send(f"t{dy}{dz}", stat.at[0, 0], stat.at[(4 - dy) % 4, dz], at(dy, dz))

    def forward(p, dz):
        arrived(f"{p}3{dz}")
        send(f"{p}2{dz}a", held.at[p, 3, dz, pl.ds(0, 64)], held.at[p, 2, dz, pl.ds(0, 64)], ahead)
        arrived(f"{p}1{dz}")
        send(f"{p}2{dz}b", held.at[p, 1, dz, pl.ds(64, 64)], held.at[p, 2, dz, pl.ds(64, 64)], behind)

    scales = {}

    def multiply(p, dy, dz):
        number = order.index((dy, dz))
        if p == 0 or (dy, dz) not in multiply.loaded:
            if (dy, dz) not in multiply.loaded:
                for part in range(3):
                    loads[number, part].wait()
                multiply.loaded.add((dy, dz))
        block = hidden.at[p] if (dy, dz) == (0, 0) else held.at[p, dy, dz]
        columns = pl.ds(pl.multiple_of(at(dy, dz)[1] * 1024, 1024), 1024)
        normed = block[...].astype(jnp.float32) * scales[p] * gain[:, columns].astype(jnp.float32)
        product = jnp.dot(
            normed.astype(jnp.bfloat16), weight[number], preferred_element_type=jnp.float32
        )
        if (dy, dz) == (0, 0):
            total[p] = product
        else:
            total[p] += product

    multiply.loaded = set()
    arrived(*[f"t{dy}{dz}" for dy, dz in spots[1:]])
    for p in range(2):
        sums = stat[0, 0, pl.ds(p, 1)]
        for dy, dz in spots[1:]:
            sums = sums + stat[dy, dz, pl.ds(p, 1)]
        scale = lax.rsqrt(sums * (1.0 / 8192) + EPSILON)
        scales[p] = jnp.transpose(jnp.broadcast_to(scale, (128, 128)))[:, 0:1]
        multiply(p, 0, 0)
    arrived("001")
    send("031", held.at[0, 0, 1], held.at[0, 3, 1], ahead)
    send("011", held.at[0, 0, 1], held.at[0, 1, 1], behind)
    forward(0, 0)
    forward(1, 0)
    send("111", held.at[1, 1, 0], held.at[1, 1, 1], across)
    send("131", held.at[1, 3, 0], held.at[1, 3, 1], across)
    for spot in ((1, 0), (3, 0), (0, 1)):
        for p in range(2):
            if spot == (0, 1) and p == 1:
                arrived("101")
            multiply(p, *spot)
    forward(0, 1)
    for p in range(2):
        for n, low in (("a", 0), ("b", 64)):
            arrived(f"{p}20{n}")
            if p == 1:
                rows = pl.ds(low, 64)
                send(f"121{n}", held.at[1, 2, 0, rows], held.at[1, 2, 1, rows], across)
    multiply(1, 2, 0)
    multiply(0, 2, 0)
    multiply(0, 1, 1)
    multiply(0, 3, 1)
    arrived("111", "131")
    multiply(1, 1, 1)
    multiply(1, 3, 1)
    arrived("021a", "021b")
    multiply(0, 2, 1)

    def finish(p):
        cos, sin = cosine[p], sine[p]

        def turned(u):
            return (u * cos + pltpu.roll(u, 64, 1) * sin).astype(jnp.bfloat16)

        for head in range(4):
            q = turned(total[p, :, head * 128 : (head + 1) * 128])
            for tree in range(8):
                low = (p * 4 + head) * 16
                query[tree, low : low + 16] = q[tree * 16 : tree * 16 + 16]
        k = turned(total[p, :, 512:640])
        v = total[p, :, 640:768].astype(jnp.bfloat16)
        for tree in range(8):
            key_new[tree, p * 16 : p * 16 + 16] = k[tree * 16 : tree * 16 + 16]
            value_new[tree, p * 16 : p * 16 + 16] = v[tree * 16 : tree * 16 + 16]

    finish(0)
    arrived("121a", "121b")
    multiply(1, 2, 1)
    finish(1)
    for copy in made.values():
        copy.wait_send()


def project_call(hidden, gain, cosine, sine, w_query, key_weight, value_weight):
    bf, f32 = jnp.bfloat16, jnp.float32
    vm = pl.BlockSpec(memory_space=pltpu.VMEM)
    anywhere = pl.BlockSpec(memory_space=pl.ANY)
    return pl.pallas_call(
        project_kernel,
        out_shape=(
            jax.ShapeDtypeStruct((8, 128, 128), bf),
            jax.ShapeDtypeStruct((8, 32, 128), bf),
            jax.ShapeDtypeStruct((8, 32, 128), bf),
        ),
        in_specs=[vm] * 4 + [anywhere] * 3,
        out_specs=(vm, vm, vm),
        scratch_shapes=[
            pltpu.VMEM((2, 4, 2, 128, 1024), bf),
            pltpu.VMEM((4, 2, 8, 128), f32),
            pltpu.VMEM((8, 1024, 768), bf),
            pltpu.VMEM((2, 128, 768), f32),
            pltpu.SemaphoreType.DMA((40,)),
            pltpu.SemaphoreType.DMA((40,)),
            pltpu.SemaphoreType.DMA((24,)),
        ],
        compiler_params=pltpu.CompilerParams(
            collective_id=1, has_side_effects=True, vmem_limit_bytes=50 * 2**20
        ),
        cost_estimate=pl.CostEstimate(flops=4 * 10**9, bytes_accessed=16 * 2**20, transcendentals=0),
    )(hidden, gain, cosine, sine, w_query, key_weight, value_weight)


def rope_tables(row_length):
    spots = row_length[None, :] + jnp.arange(2, dtype=jnp.int32)[:, None]
    ladder = jnp.arange(64, dtype=jnp.float32) * (2.0 / 128)
    frequency = jnp.power(jnp.float32(ROPE_BASE), -ladder)
    angles = spots.astype(jnp.float32)[..., None] * frequency
    cosine, sine = jnp.cos(angles), jnp.sin(angles)
    return jnp.concatenate([cosine, cosine], axis=-1), jnp.concatenate([-sine, sine], axis=-1)


def attention_kernel(
    pages, q_own, key_new, value_new, lim, keys, values,
    out,
    q_all, part, part_stat, got, got_stat, relay, relay_stat, rowed, rowed_stat, fresh, fresh_stat,
    lhs, send_sem, recv_sem,
):
    x, zl, core, h = place()

    def at(dx, dz):
        return (lax.rem(x + dx, 4) * 4 + (zl if dz == 0 else 1 - zl) * 2 + core, h)

    ahead, behind, across = at(1, 0), at(3, 0), at(0, 1)
    barrier = pltpu.get_barrier_semaphore()
    for device in (ahead, behind, across):
        pl.semaphore_signal(barrier, inc=1, device_id=device, device_id_type=MESH)
    pl.semaphore_wait(barrier, 3)

    made, send, arrived = sender(send_sem, recv_sem)
    lhs[128:144, :] = jnp.ones((16, 1024), jnp.bfloat16)
    token = lax.broadcasted_iota(jnp.int32, (1024, 128), 0) % 64
    low_lanes = lax.broadcasted_iota(jnp.int32, (128, 128), 1) < 64

    def block(dx, dz):
        owner = lax.rem(x + dx, 4) * 2 + (zl if dz == 0 else 1 - zl)

        def half_loop(half):
            def tree_step(u, _):
                tree = half * 4 + u
                base = (owner * 8 + tree) * 16
                numbers = [pages[base + i] for i in range(16)]
                k = jnp.concatenate([keys[n] for n in numbers], axis=0)
                q = q_all[dx, dz, half, u]
                s = lax.dot_general(k, q, (((1,), (1,)), ((), ())), preferred_element_type=jnp.float32)
                limits = lim[owner, tree]
                limits = jnp.concatenate(
                    [jnp.broadcast_to(limits[i : i + 1], (64, 128)) for i in range(16)], axis=0
                )
                s = jnp.where(token < limits, s, LOW_SCORE)
                m = jnp.maximum(jnp.max(s, axis=0, keepdims=True), LOW_MAX)
                p = jnp.exp2((s - m) * EXP_SCALE).astype(jnp.bfloat16)
                for i in range(8):
                    lhs[0:128, i * 128 : (i + 1) * 128] = jnp.where(
                        low_lanes, values[numbers[2 * i]], values[numbers[2 * i + 1]]
                    )
                o = jnp.dot(lhs[...], p, preferred_element_type=jnp.float32)
                part[dx, dz, half, u] = o[0:128].astype(jnp.bfloat16)
                part_stat[dx, dz, half, pl.ds(u, 1), :] = m
                part_stat[dx, dz, half, pl.ds(u + 4, 1), :] = o[128:129]
                return 0

            lax.fori_loop(0, 4, tree_step, 0)

        for half in (0, 1):
            half_loop(half)
            if dx in (1, 3):
                to, slot = (ahead, 0) if dx == 1 else (behind, 1)
                send(f"o{dx}{dz}{half}", part.at[dx, dz, half], got.at[slot, dz, half], to)
                send(f"s{dx}{dz}{half}", part_stat.at[dx, dz, half], got_stat.at[slot, dz, half], to)
            if dx == 2:
                to = ahead if half == 0 else behind
                send(f"o2{dz}{half}", part.at[dx, dz, half], relay.at[dz, half], to)
                send(f"s2{dz}{half}", part_stat.at[dx, dz, half], relay_stat.at[dz, half], to)

    def pass_on(dz):
        for half in (0, 1):
            to = ahead if half == 0 else behind
            arrived(f"o2{dz}{half}", f"s2{dz}{half}")
            send(f"or{dz}{half}", relay.at[dz, half], got.at[2, dz, half], to)
            send(f"sr{dz}{half}", relay_stat.at[dz, half], got_stat.at[2, dz, half], to)

    def merged(pieces, u):
        tops = [stat[pl.ds(u, 1), :] for _, stat in pieces]
        top = tops[0]
        for other in tops[1:]:
            top = jnp.maximum(top, other)
        total = jnp.zeros((1, 128), jnp.float32)
        sums = jnp.zeros((128, 128), jnp.float32)
        for (o, stat), m in zip(pieces, tops):
            w = jnp.exp2((m - top) * EXP_SCALE)
            total += w * stat[pl.ds(u + 4, 1), :]
            sums += w * o[u].astype(jnp.float32)
        return top, total, sums

    q_all[0, 0] = q_own[...]
    send("q30", q_all.at[0, 0], q_all.at[3, 0], ahead)
    send("q10", q_all.at[0, 0], q_all.at[1, 0], behind)
    send("q01", q_all.at[0, 0], q_all.at[0, 1], across)

    spot_k = lax.broadcasted_iota(jnp.int32, (32, 128), 0)
    spot_q = lax.broadcasted_iota(jnp.int32, (32, 128), 1)
    seen = (spot_k % 16 == spot_q % 16) & (spot_k // 16 <= spot_q // 64)
    for half in (0, 1):
        def new_step(u, _):
            q = q_all[0, 0, half, u]
            s = lax.dot_general(
                key_new[half * 4 + u], q, (((1,), (1,)), ((), ())), preferred_element_type=jnp.float32
            )
            s = jnp.where(seen, s, LOW_SCORE)
            m = jnp.max(s, axis=0, keepdims=True)
            p = jnp.exp2((s - m) * EXP_SCALE).astype(jnp.bfloat16)
            o = lax.dot_general(
                value_new[half * 4 + u], p, (((0,), (0,)), ((), ())), preferred_element_type=jnp.float32
            )
            fresh[half, u] = o.astype(jnp.bfloat16)
            fresh_stat[half, pl.ds(u, 1), :] = m
            fresh_stat[half, pl.ds(u + 4, 1), :] = jnp.sum(p.astype(jnp.float32), axis=0, keepdims=True)
            return 0

        lax.fori_loop(0, 4, new_step, 0)

    block(0, 0)
    arrived("q30")
    send("q20a", q_all.at[3, 0, 0], q_all.at[2, 0, 0], ahead)
    arrived("q10")
    send("q20b", q_all.at[1, 0, 1], q_all.at[2, 0, 1], behind)
    arrived("q01")
    send("q31", q_all.at[0, 1], q_all.at[3, 1], ahead)
    send("q11", q_all.at[0, 1], q_all.at[1, 1], behind)
    block(1, 0)
    block(3, 0)
    arrived("q20a")
    send("q21a", q_all.at[2, 0, 0], q_all.at[2, 1, 0], across)
    arrived("q20b")
    send("q21b", q_all.at[2, 0, 1], q_all.at[2, 1, 1], across)
    block(2, 0)
    arrived("q11", "q31")
    block(1, 1)
    block(3, 1)
    pass_on(0)
    arrived("q21a", "q21b")
    block(2, 1)
    block(0, 1)
    pass_on(1)
    for half in (0, 1):
        arrived(*[f"{a}{b}1{half}" for a in "os" for b in (1, 3)], f"or1{half}", f"sr1{half}")
        pieces = [(part.at[0, 1, half], part_stat.at[0, 1, half])]
        pieces += [(got.at[i, 1, half], got_stat.at[i, 1, half]) for i in range(3)]

        def row_step(u, _):
            top, total, sums = merged(pieces, u)
            rowed[0, half, u] = sums.astype(jnp.bfloat16)
            rowed_stat[0, half, pl.ds(u, 1), :] = top
            rowed_stat[0, half, pl.ds(u + 4, 1), :] = total
            return 0

        lax.fori_loop(0, 4, row_step, 0)
        send(f"oz{half}", rowed.at[0, half], rowed.at[1, half], across)
        send(f"sz{half}", rowed_stat.at[0, half], rowed_stat.at[1, half], across)
    for half in (0, 1):
        arrived(*[f"{a}{b}0{half}" for a in "os" for b in (1, 3)], f"or0{half}", f"sr0{half}")
        arrived(f"oz{half}", f"sz{half}")
        pieces = [(part.at[0, 0, half], part_stat.at[0, 0, half])]
        pieces += [(got.at[i, 0, half], got_stat.at[i, 0, half]) for i in range(3)]
        pieces += [(rowed.at[1, half], rowed_stat.at[1, half]), (fresh.at[half], fresh_stat.at[half])]

        def last_step(u, _):
            top, total, sums = merged(pieces, u)
            out[half * 4 + u] = jnp.transpose(sums / total).astype(jnp.bfloat16)
            return 0

        lax.fori_loop(0, 4, last_step, 0)
    for copy in made.values():
        copy.wait_send()


def attention_call(pages, q_own, key_new, value_new, lim, keys, values):
    blk = (2, 4, 128, 128)
    st = (2, 8, 128)
    bf, f32 = jnp.bfloat16, jnp.float32
    vm = pl.BlockSpec(memory_space=pltpu.VMEM)
    return pl.pallas_call(
        attention_kernel,
        out_shape=jax.ShapeDtypeStruct((8, 128, 128), bf),
        in_specs=[pl.BlockSpec(memory_space=pltpu.SMEM)] + [vm] * 6,
        out_specs=vm,
        scratch_shapes=[
            pltpu.VMEM((4, 2) + blk, bf),
            pltpu.VMEM((4, 2) + blk, bf),
            pltpu.VMEM((4, 2) + st, f32),
            pltpu.VMEM((3, 2) + blk, bf),
            pltpu.VMEM((3, 2) + st, f32),
            pltpu.VMEM((2,) + blk, bf),
            pltpu.VMEM((2,) + st, f32),
            pltpu.VMEM((2,) + blk, bf),
            pltpu.VMEM((2,) + st, f32),
            pltpu.VMEM(blk, bf),
            pltpu.VMEM(st, f32),
            pltpu.VMEM((144, 1024), bf),
            pltpu.SemaphoreType.DMA((48,)),
            pltpu.SemaphoreType.DMA((48,)),
        ],
        compiler_params=pltpu.CompilerParams(
            collective_id=2, has_side_effects=True, vmem_limit_bytes=50 * 2**20
        ),
        cost_estimate=pl.CostEstimate(flops=9 * 10**9, bytes_accessed=16 * 2**20, transcendentals=10**7),
    )(pages, q_own.reshape((2, 4, 128, 128)), key_new, value_new, lim, keys, values)


def sibling(array):
    return lax.ppermute(array, "cache", [(i, i ^ 1) for i in range(16)])


def tables(tree_pages, page_fill, row_depth):
    core = lax.rem(lax.axis_index("cache"), 2)
    pages = tree_pages[0].reshape(8, 2, 8, 8)
    fill = page_fill[0].reshape(8, 2, 8, 8)
    depth = row_depth[0].reshape(8, 2, 8, 16)
    packed = jnp.concatenate([pages, fill, depth], axis=-1)
    mine = lax.dynamic_index_in_dim(packed, core, 1, keepdims=False)
    theirs = sibling(lax.dynamic_index_in_dim(packed, 1 - core, 1, keepdims=False))

    def limits(t):
        lanes = jnp.tile(t[..., None, 16:32], (1, 1, 1, 8))
        slot = jnp.arange(8, dtype=jnp.int32)[:, None]
        return jnp.where(slot < lanes, t[..., 8:16, None], 0)

    numbers = jnp.concatenate([mine[..., :8], theirs[..., :8] + 128], axis=-1)
    lim = jnp.concatenate([limits(mine), limits(theirs)], axis=2)
    return numbers.reshape(-1), lim


def out_kernel(att, w_out, out, sent, got_y, got_z, send_sem, recv_sem):
    c, y, zh = column_place()

    def at(dy, dz):
        return (c, lax.rem(y + dy, 4) * 2 + (zh if dz == 0 else 1 - zh))

    ahead, behind, across = at(1, 0), at(3, 0), at(0, 1)
    barrier = pltpu.get_barrier_semaphore()
    for device in (ahead, behind, across):
        pl.semaphore_signal(barrier, inc=1, device_id=device, device_id_type=MESH)
    pl.semaphore_wait(barrier, 3)
    made, send, arrived = sender(send_sem, recv_sem)

    def product(dy, dz, p, low, rows):
        features = pl.ds(pl.multiple_of(at(dy, dz)[1] * 1024, 1024), 1024)
        return jnp.dot(
            att[pl.ds(p * 128 + low, rows)], w_out[:, features], preferred_element_type=jnp.float32
        )

    def ring(p, dz, name, extra):
        buf, box = sent.at[p, dz], got_y.at[p, dz]

        def term(dy, low, rows):
            r = product(dy, dz, p, low, rows)
            return r if extra is None else r + extra[dy, pl.ds(low, rows)].astype(jnp.float32)

        def far():
            if extra is not None:
                arrived(f"z{p}2")
            for low, to, n in ((0, ahead, "a"), (64, behind, "b")):
                buf[2, pl.ds(low, 64)] = term(2, low, 64).astype(jnp.bfloat16)
                send(name + "f" + n, buf.at[2, pl.ds(low, 64)], box.at[2, pl.ds(low, 64)], to)

        def near():
            if extra is not None:
                arrived(f"z{p}1", f"z{p}3")
            for dy, low, to, n in ((1, 64, ahead, "a"), (3, 0, behind, "b")):
                buf[dy, pl.ds(low, 64)] = term(dy, low, 64).astype(jnp.bfloat16)
                send(name + "n" + n, buf.at[dy, pl.ds(low, 64)], box.at[4 - dy, pl.ds(low, 64)], to)

        def join():
            for dy, low, to, n in ((1, 0, ahead, "a"), (3, 64, behind, "b")):
                arrived(name + "f" + n)
                summed = term(dy, low, 64) + box[2, pl.ds(low, 64)].astype(jnp.float32)
                buf[dy, pl.ds(low, 64)] = summed.astype(jnp.bfloat16)
                send(name + "j" + n, buf.at[dy, pl.ds(low, 64)], box.at[4 - dy, pl.ds(low, 64)], to)

        def end():
            if extra is not None:
                arrived(f"z{p}0")
            r = term(0, 0, 128)
            arrived(*[name + s + n for s in "nj" for n in "ab"])
            return r + box[1].astype(jnp.float32) + box[3].astype(jnp.float32)

        return far, near, join, end

    first_other = ring(0, 1, "p", None)
    first_own = ring(0, 0, "q", None)
    second = ring(1, 0, "r", got_z.at[1])
    first_other[0]()
    for dy in (2,):
        sent[1, 1, dy] = product(dy, 1, 1, 0, 128).astype(jnp.bfloat16)
        send(f"z1{dy}", sent.at[1, 1, dy], got_z.at[1, dy], across)
    first_own[0]()
    for dy in (1, 3, 0):
        sent[1, 1, dy] = product(dy, 1, 1, 0, 128).astype(jnp.bfloat16)
        send(f"z1{dy}", sent.at[1, 1, dy], got_z.at[1, dy], across)
    first_other[1]()
    first_own[1]()
    first_other[2]()
    first_own[2]()
    second[0]()
    sent[0, 1, 0] = first_other[3]().astype(jnp.bfloat16)
    send("z0", sent.at[0, 1, 0], got_z.at[0, 0], across)
    second[1]()
    second[2]()
    half = first_own[3]()
    arrived("z0")
    out[0] = (half + got_z[0, 0].astype(jnp.float32)).astype(jnp.bfloat16)
    out[1] = second[3]().astype(jnp.bfloat16)
    for copy in made.values():
        copy.wait_send()


def out_call(att, w_out):
    bf = jnp.bfloat16
    vm = pl.BlockSpec(memory_space=pltpu.VMEM)
    return pl.pallas_call(
        out_kernel,
        out_shape=jax.ShapeDtypeStruct((2, 128, 1024), bf),
        in_specs=[vm, vm],
        out_specs=vm,
        scratch_shapes=[
            pltpu.VMEM((2, 2, 4, 128, 1024), bf),
            pltpu.VMEM((2, 2, 4, 128, 1024), bf),
            pltpu.VMEM((2, 4, 128, 1024), bf),
            pltpu.SemaphoreType.DMA((32,)),
            pltpu.SemaphoreType.DMA((32,)),
        ],
        compiler_params=pltpu.CompilerParams(
            collective_id=3, has_side_effects=True, vmem_limit_bytes=50 * 2**20
        ),
        cost_estimate=pl.CostEstimate(flops=2 * 10**9, bytes_accessed=10 * 2**20, transcendentals=0),
    )(att, w_out)


def body(
    hidden,
    norm_gain,
    w_query,
    key_weight,
    value_weight,
    w_out,
    key_cache,
    value_cache,
    tree_pages,
    page_fill,
    row_depth,
    row_length,
):
    keys = key_cache.reshape(128, 64, 128)
    values = jnp.transpose(value_cache.reshape(128, 64, 128), (0, 2, 1))
    keys = jnp.concatenate([keys, sibling(keys)], axis=0)
    values = jnp.concatenate([values, sibling(values)], axis=0)
    values = jnp.concatenate([values, values], axis=2)
    numbers, lim = tables(tree_pages, page_fill, row_depth)
    cosine, sine = rope_tables(row_length)
    query, key_new, value_new = project_call(
        hidden, norm_gain[None, :], cosine, sine, w_query, key_weight, value_weight
    )
    attention = attention_call(numbers, query, key_new, value_new, lim, keys, values)
    attention = attention.reshape(8, 2, 4, 16, 128).transpose(1, 0, 3, 2, 4).reshape(256, 512)
    return out_call(attention, w_out)


def solution(mesh):
    in_specs = (
        P(None, "cache", "head"),
        P(),
        P(None, "head"),
        P(None, "head"),
        P(None, "head"),
        P("head", None),
        P("cache", None, "head", None),
        P("cache", None, "head", None),
        P("cache", None, None),
        P("cache", None, None),
        P("cache", None),
        P("cache"),
    )
    out_specs = P(None, "cache", "head")
    return jax.shard_map(body, mesh=mesh, in_specs=in_specs, out_specs=out_specs, check_vma=False)
```

```python
import math

import jax
import jax.numpy as jnp
from jax import lax
from jax.experimental import pallas as pl
from jax.experimental.pallas import tpu as pltpu
from jax.sharding import PartitionSpec as P

MESH = pl.DeviceIdType.MESH
ROPE_BASE = 500000.0
EPSILON = 1e-05
LOW_SCORE = -1e30
LOW_MAX = -1e29
EXP_SCALE = math.log2(math.e) / math.sqrt(128.0)
BF, F32 = jnp.bfloat16, jnp.float32
SPOTS = [(dy, dz) for dy in range(4) for dz in range(2)]
ORDER = [(0, 0), (1, 0), (3, 0), (0, 1), (2, 0), (1, 1), (3, 1), (2, 1)]


def kernel(
    hidden, gain, cosine, sine, pages_in, fill, depth, w_query, key_weight, value_weight, w_out_hbm, key_hbm, value_hbm,
    out,
    held, sums, scale, weight, total, w_out, keys, values, filled, bias, bias_away, pages_away, pages,
    q_all, key_new, value_new, part, part_stat, got, got_stat, relay, relay_stat, rowed, rowed_stat, fresh, fresh_stat,
    vals, att, sent, got_y, got_z,
    send_sem, recv_sem, load_sem,
):
    c, h = lax.axis_index("cache"), lax.axis_index("head")
    x, zl, core = c // 4, lax.rem(c // 2, 2), lax.rem(c, 2)
    y, zh = h // 2, lax.rem(h, 2)

    def in_head(dy, dz):
        return lax.rem(y + dy, 4) * 2 + (zh if dz == 0 else 1 - zh)

    def in_cache(dx, dz):
        return lax.rem(x + dx, 4) * 4 + (zl if dz == 0 else 1 - zl) * 2 + core

    y_up, y_down, z_far = (c, in_head(1, 0)), (c, in_head(3, 0)), (c, in_head(0, 1))
    x_up, x_down, z_near = (in_cache(1, 0), h), (in_cache(3, 0), h), (in_cache(0, 1), h)
    twin = (c + 1 - 2 * core, h)

    loads = {}

    def load(name, src, dst):
        loads[name] = pltpu.make_async_copy(src, dst, load_sem.at[len(loads)])
        loads[name].start()

    load("pages", pages_in.at[core], pages.at[0])
    for number, spot in enumerate(ORDER):
        rows = pl.ds(pl.multiple_of(in_head(*spot) * 1024, 1024), 1024)
        load(("q", number), w_query.at[rows], weight.at[number, :, pl.ds(0, 512)])
        load(("k", number), key_weight.at[rows], weight.at[number, :, pl.ds(512, 128)])
        load(("v", number), value_weight.at[rows], weight.at[number, :, pl.ds(640, 128)])
    load("keys", key_hbm, keys.at[pl.ds(0, 128)])
    load("values", value_hbm, values.at[pl.ds(0, 128)])
    load("out", w_out_hbm, w_out)

    barrier = pltpu.get_barrier_semaphore()
    others = [(c, in_head(*spot)) for spot in SPOTS[1:]] + [x_up, x_down, z_near, twin]
    for device in others:
        pl.semaphore_signal(barrier, inc=1, device_id=device, device_id_type=MESH)
    pl.semaphore_wait(barrier, len(others))

    made = {}

    def send(name, src, dst, device):
        number = len(made)
        made[name] = pltpu.make_async_remote_copy(
            src_ref=src, dst_ref=dst, send_sem=send_sem.at[number], recv_sem=recv_sem.at[number],
            device_id=device, device_id_type=MESH,
        )
        made[name].start()

    def arrived(*names):
        for name in names:
            made[name].wait_recv()


    def gather_start(half):
        rows = pl.ds(half * 64, 64)
        for p in range(2):
            for name, to, dy, dz in (("30", y_up, 3, 0), ("10", y_down, 1, 0), ("01", z_far, 0, 1)):
                send(f"a{half}{p}{name}", hidden.at[p, rows], held.at[half, dy, dz, p], to)

    low_rows, high_rows = pl.ds(0, 32), pl.ds(32, 32)

    def gather_forward(half, p, dz):
        a = f"a{half}{p}"
        arrived(f"{a}3{dz}")
        send(f"{a}2{dz}u", held.at[half, 3, dz, p, low_rows], held.at[half, 2, dz, p, low_rows], y_up)
        arrived(f"{a}1{dz}")
        send(f"{a}2{dz}d", held.at[half, 1, dz, p, high_rows], held.at[half, 2, dz, p, high_rows], y_down)

    def gather_second(half):
        arrived(f"a{half}001")
        send(f"a{half}031", held.at[half, 0, 1, 0], held.at[half, 3, 1, 0], y_up)
        send(f"a{half}011", held.at[half, 0, 1, 0], held.at[half, 1, 1, 0], y_down)
        gather_forward(half, 0, 0)
        gather_forward(half, 1, 0)
        send(f"a{half}111", held.at[half, 1, 0, 1], held.at[half, 1, 1, 1], z_far)
        send(f"a{half}131", held.at[half, 3, 0, 1], held.at[half, 3, 1, 1], z_far)

    def gather_third(half):
        gather_forward(half, 0, 1)
        for n, rows in (("u", low_rows), ("d", high_rows)):
            arrived(f"a{half}120{n}")
            send(f"a{half}121{n}", held.at[half, 2, 0, 1, rows], held.at[half, 2, 1, 1, rows], z_far)

    ready = set()

    def multiply(half, dy, dz):
        number = ORDER.index((dy, dz))
        if number not in ready:
            for array in "qkv":
                loads[array, number].wait()
            ready.add(number)
        if (dy, dz) == (0, 0):
            rows = pl.ds(half * 64, 64)
            block = jnp.concatenate([hidden[0, rows], hidden[1, rows]], axis=0)
        else:
            block = held[half, dy, dz].reshape(128, 1024)
        columns = pl.ds(pl.multiple_of(in_head(dy, dz) * 1024, 1024), 1024)
        normed = block.astype(F32) * scale[half][:, 0:1] * gain[:, columns].astype(F32)
        product = jnp.dot(normed.astype(BF), weight[number], preferred_element_type=F32)
        if (dy, dz) == (0, 0):
            total[half] = product
        else:
            total[half] += product

    def multiply_near(half):
        arrived(f"a{half}101")
        for spot in ((1, 0), (3, 0), (0, 1)):
            multiply(half, *spot)

    def multiply_mid(half):
        arrived(f"a{half}020u", f"a{half}020d")
        multiply(half, 2, 0)
        arrived(f"a{half}111", f"a{half}131")
        multiply(half, 1, 1)
        multiply(half, 3, 1)

    def multiply_far(half):
        arrived(*[f"a{half}{p}21{n}" for p in range(2) for n in "ud"])
        multiply(half, 2, 1)

    def project_end(half):
        rows = pl.ds(half * 64, 64)
        cos = jnp.concatenate([cosine[0, rows], cosine[1, rows]], axis=0)
        sin = jnp.concatenate([sine[0, rows], sine[1, rows]], axis=0)

        def turned(u):
            return (u * cos + pltpu.roll(u, 64, 1) * sin).astype(BF)

        k = turned(total[half, :, 512:640])
        v = total[half, :, 640:768].astype(BF)
        for head in range(4):
            q = turned(total[half, :, head * 128 : (head + 1) * 128])
            for p in range(2):
                for u in range(4):
                    low = (p * 4 + head) * 16
                    q_all[0, 0, half, u, low : low + 16] = q[p * 64 + u * 16 : p * 64 + u * 16 + 16]
        for p in range(2):
            for u in range(4):
                low, there = p * 64 + u * 16, u * 32 + p * 16
                key_new[half, there : there + 16] = k[low : low + 16]
                value_new[half, there : there + 16, 0:128] = v[low : low + 16]


    def query_start(half):
        q = f"q{half}"
        send(q + "30", q_all.at[0, 0, half], q_all.at[3, 0, half], x_up)
        send(q + "10", q_all.at[0, 0, half], q_all.at[1, 0, half], x_down)
        send(q + "01", q_all.at[0, 0, half], q_all.at[0, 1, half], z_near)

    def query_forward(half, dz):
        q = f"q{half}"
        lows, highs = pl.ds(0, 2), pl.ds(2, 2)
        arrived(f"{q}3{dz}")
        send(f"{q}2{dz}u", q_all.at[3, dz, half, lows], q_all.at[2, dz, half, lows], x_up)
        arrived(f"{q}1{dz}")
        send(f"{q}2{dz}d", q_all.at[1, dz, half, highs], q_all.at[2, dz, half, highs], x_down)

    def query_second(half):
        q = f"q{half}"
        arrived(q + "01")
        send(q + "31", q_all.at[0, 1, half], q_all.at[3, 1, half], x_up)
        send(q + "11", q_all.at[0, 1, half], q_all.at[1, 1, half], x_down)
        query_forward(half, 0)


    lane = lax.broadcasted_iota(jnp.int32, (128, 128), 1)
    row = lax.broadcasted_iota(jnp.int32, (128, 128), 0)

    def fresh_tokens(half):
        stats = jnp.zeros((128, 128), F32)
        for u in range(4):
            seen = (lane // 32 == u) & (lane % 16 == row % 16) & ((lane % 32) // 16 <= row // 64)
            s = lax.dot_general(
                q_all[0, 0, half, u], key_new[half], (((1,), (1,)), ((), ())), preferred_element_type=F32
            )
            s = jnp.where(seen, s, LOW_SCORE)
            m = jnp.max(s, axis=1, keepdims=True)
            p = jnp.exp2((s - m) * EXP_SCALE).astype(BF)
            o = jnp.dot(p, value_new[half], preferred_element_type=F32)
            fresh[half, u] = o[:, 0:128].astype(BF)
            stats = jnp.where(lane == u, m, stats)
            stats = jnp.where(lane == u + 4, o[:, 128:256], stats)
        fresh_stat[half] = jnp.transpose(stats)[0:8]

    def block(half, dx, dz):
        owner = lax.rem(x + dx, 4) * 2 + (zl if dz == 0 else 1 - zl)
        stats = jnp.zeros((128, 128), F32)
        for u in range(4):
            tree = owner * 8 + half * 4 + u
            base = tree * 8
            numbers = []
            for b in range(2):
                numbers += [pages[b, base // 128, lax.rem(base, 128) + i] + b * 128 for i in range(8)]
            k = jnp.concatenate([keys[n] for n in numbers], axis=0)
            s = lax.dot_general(
                q_all[dx, dz, half, u], k, (((1,), (1,)), ((), ())), preferred_element_type=F32
            )
            hide = jnp.concatenate([bias[0, tree], bias[1, tree]], axis=1).astype(F32)
            s = jnp.concatenate([s[i * 16 : (i + 1) * 16] + hide for i in range(8)], axis=0)
            m = jnp.maximum(jnp.max(s, axis=1, keepdims=True), LOW_MAX)
            p = jnp.exp2((s - m) * EXP_SCALE).astype(BF)
            for i in range(16):
                vals[u, i * 64 : (i + 1) * 64, 0:128] = values[numbers[i]]
            o = jnp.dot(p, vals[u], preferred_element_type=F32)
            part[dx, dz, half, u] = o[:, 0:128].astype(BF)
            stats = jnp.where(lane == u, m, stats)
            stats = jnp.where(lane == u + 4, o[:, 128:256], stats)
        part_stat[dx, dz, half] = jnp.transpose(stats)[0:8]
        n = f"{half}{dx}{dz}"
        if dx in (1, 3):
            to, slot = (x_up, 0) if dx == 1 else (x_down, 1)
            send("o" + n, part.at[dx, dz, half], got.at[slot, dz, half], to)
            send("s" + n, part_stat.at[dx, dz, half], got_stat.at[slot, dz, half], to)
        if dx == 2:
            to = x_up if dz == 0 else x_down
            send("o" + n, part.at[dx, dz, half], relay.at[dz, half], to)
            send("s" + n, part_stat.at[dx, dz, half], relay_stat.at[dz, half], to)

    def pass_on(half, dz):
        n = f"{half}2{dz}"
        to = x_up if dz == 0 else x_down
        arrived("o" + n, "s" + n)
        send("ro" + n, relay.at[dz, half], got.at[2, dz, half], to)
        send("rs" + n, relay_stat.at[dz, half], got_stat.at[2, dz, half], to)

    def weigh(stats):
        tops = [s[0:4] for s in stats]
        top = tops[0]
        for other in tops[1:]:
            top = jnp.maximum(top, other)
        weights = [jnp.exp2((m - top) * EXP_SCALE) for m in tops]
        summed = jnp.zeros((4, 128), F32)
        for w, s in zip(weights, stats):
            summed = summed + w * s[4:8]
        return top, weights, summed

    def columns_of(weights):
        stacked = jnp.concatenate(weights + [jnp.zeros((128 - 4 * len(weights), 128), F32)], axis=0)
        return jnp.transpose(stacked)

    def received(half, dz):
        n = f"{half}{{}}{dz}"
        for a in "os":
            arrived(a + n.format(1), a + n.format(3), "r" + a + n.format(2))

    def plane_merge(half):
        received(half, 1)
        outs = [part.at[0, 1, half]] + [got.at[i, 1, half] for i in range(3)]
        top, weights, summed = weigh([part_stat[0, 1, half]] + [got_stat[i, 1, half] for i in range(3)])
        columns = columns_of(weights)
        for u in range(4):
            o = jnp.zeros((128, 128), F32)
            for i, ref in enumerate(outs):
                o = o + columns[:, i * 4 + u : i * 4 + u + 1] * ref[u].astype(F32)
            rowed[0, half, u] = o.astype(BF)
        rowed_stat[0, half] = jnp.concatenate([top, summed], axis=0)
        send(f"zo{half}", rowed.at[0, half], rowed.at[1, half], z_near)
        send(f"zs{half}", rowed_stat.at[0, half], rowed_stat.at[1, half], z_near)

    def last_merge(half):
        received(half, 0)
        arrived(f"zo{half}", f"zs{half}")
        outs = [part.at[0, 0, half]] + [got.at[i, 0, half] for i in range(3)] + [rowed.at[1, half], fresh.at[half]]
        stats = [part_stat[0, 0, half]] + [got_stat[i, 0, half] for i in range(3)]
        stats += [rowed_stat[1, half], fresh_stat[half]]
        top, weights, summed = weigh(stats)
        columns = columns_of([w / summed for w in weights])
        for u in range(4):
            o = jnp.zeros((128, 128), F32)
            for i, ref in enumerate(outs):
                o = o + columns[:, i * 4 + u : i * 4 + u + 1] * ref[u].astype(F32)
            o = o.astype(BF)
            for p in range(2):
                for head in range(4):
                    low = (p * 4 + head) * 16
                    att[half, p * 64 + u * 16 : p * 64 + u * 16 + 16, head * 128 : (head + 1) * 128] = o[low : low + 16]


    rings = {"p": (0, 0, 1), "q": (1, 0, 0), "r": (2, 1, 0)}

    def product(half, dy, dz):
        features = pl.ds(pl.multiple_of(in_head(dy, dz) * 1024, 1024), 1024)
        r = jnp.dot(att[half], w_out[:, features], preferred_element_type=F32).astype(BF)
        sent[half, dz, dy] = r.reshape(2, 64, 1024)

    def over_z(half, dy):
        send(f"z{half}{dy}", sent.at[half, 1, dy, 1], got_z.at[half, dy], z_far)

    def add_z(half, dy):
        arrived(f"z{half}{dy}")
        sent[half, 0, dy, 1] = (sent[half, 0, dy, 1].astype(F32) + got_z[half, dy].astype(F32)).astype(BF)

    def ring_far(half, name):
        ring, p, dz = rings[name]
        for rows, to, n in ((low_rows, y_up, "u"), (high_rows, y_down, "d")):
            send(f"{name}f{half}{n}", sent.at[half, dz, 2, p, rows], got_y.at[half, ring, 0, rows], to)

    def ring_near(half, name):
        ring, p, dz = rings[name]
        for dy, rows, to, n, slot in ((1, high_rows, y_up, "u", 2), (3, low_rows, y_down, "d", 1)):
            send(f"{name}n{half}{n}", sent.at[half, dz, dy, p, rows], got_y.at[half, ring, slot, rows], to)

    def ring_join(half, name):
        ring, p, dz = rings[name]
        for dy, rows, to, n, slot in ((1, low_rows, y_up, "u", 2), (3, high_rows, y_down, "d", 1)):
            arrived(f"{name}f{half}{n}")
            summed = sent[half, dz, dy, p, rows].astype(F32) + got_y[half, ring, 0, rows].astype(F32)
            sent[half, dz, dy, p, rows] = summed.astype(BF)
            send(f"{name}j{half}{n}", sent.at[half, dz, dy, p, rows], got_y.at[half, ring, slot, rows], to)

    def ring_end(half, name):
        ring, p, dz = rings[name]
        arrived(*[f"{name}{s}{half}{n}" for s in "nj" for n in "ud"])
        r = sent[half, dz, 0, p].astype(F32)
        return r + got_y[half, ring, 1].astype(F32) + got_y[half, ring, 2].astype(F32)

    def out_start(half):
        product(half, 2, 1)
        ring_far(half, "p")
        over_z(half, 2)
        product(half, 2, 0)
        ring_far(half, "q")
        product(half, 1, 1)
        over_z(half, 1)
        product(half, 3, 1)
        over_z(half, 3)
        ring_near(half, "p")
        product(half, 0, 1)
        over_z(half, 0)
        product(half, 1, 0)
        product(half, 3, 0)
        ring_near(half, "q")
        product(half, 0, 0)

    def out_join(half):
        ring_join(half, "p")
        ring_join(half, "q")

    def out_second(half):
        add_z(half, 2)
        ring_far(half, "r")
        add_z(half, 1)
        add_z(half, 3)
        ring_near(half, "r")

    def out_cross(half):
        sent[half, 1, 0, 0] = ring_end(half, "p").astype(BF)
        send(f"y{half}", sent.at[half, 1, 0, 0], got_z.at[half, 4], z_far)

    def out_third(half):
        ring_join(half, "r")
        add_z(half, 0)

    def out_end(half):
        rows = pl.ds(half * 64, 64)
        first = ring_end(half, "q")
        arrived(f"y{half}")
        out[0, rows] = (first + got_z[half, 4].astype(F32)).astype(BF)
        out[1, rows] = ring_end(half, "r").astype(BF)


    def exchange_start():
        send("pages", pages_in.at[1 - core], pages_away, twin)
        send("keys", key_hbm, keys.at[pl.ds(128, 128)], twin)
        send("values", value_hbm, values.at[pl.ds(128, 128)], twin)

    def squares_start():
        for p in range(2):
            wide = hidden[p].astype(F32)
            squares = jnp.sum(wide * wide, axis=-1, keepdims=True)
            sums[0, 0, pl.ds(p, 1)] = jnp.transpose(jnp.broadcast_to(squares, (128, 128)))[0:1]
        for dy, dz in SPOTS[1:]:
            send(f"t{dy}{dz}", sums.at[0, 0], sums.at[(4 - dy) % 4, dz], (c, in_head(dy, dz)))

    def squares_end():
        arrived(*[f"t{dy}{dz}" for dy, dz in SPOTS[1:]])
        for p in range(2):
            s = sums[0, 0, pl.ds(p, 1)]
            for dy, dz in SPOTS[1:]:
                s = s + sums[dy, dz, pl.ds(p, 1)]
            s = jnp.transpose(jnp.broadcast_to(lax.rsqrt(s * (1.0 / 8192) + EPSILON), (128, 128)))
            for half in range(2):
                scale[half, p * 64 : p * 64 + 64] = s[half * 64 : half * 64 + 64]

    def visibility():
        slot_row = lax.broadcasted_iota(jnp.int32, (128, 512), 0)
        slot_lane = lax.broadcasted_iota(jnp.int32, (128, 512), 1) // 64
        spread = jnp.where(slot_row == slot_lane, 1.0, 0.0).astype(BF)
        filled[...] = jnp.dot(fill[...], spread, preferred_element_type=F32)
        column = lax.broadcasted_iota(jnp.int32, (16, 512), 1)
        slot_of, token_of = (column // 64).astype(F32), (column % 64).astype(F32)

        def group(target, j, e):
            depths = jnp.transpose(jnp.broadcast_to(depth[pl.ds(e, 1)], (128, 128)))
            fills = filled[pl.ds(pl.multiple_of(e * 8, 8), 8)]
            for t in range(8):
                d = jnp.concatenate([depths[t * 16 : t * 16 + 16]] * 4, axis=1)
                visible = (slot_of < d) & (token_of < fills[t : t + 1])
                target[j * 8 + t] = jnp.where(visible, 0.0, LOW_SCORE).astype(BF)

        def away(j, _):
            group(bias_away, j, j * 2 + 1 - core)
            return 0

        def here(j, _):
            group(bias.at[0], j, j * 2 + core)
            return 0

        lax.fori_loop(0, 8, away, 0)
        send("bias", bias_away, bias.at[1], twin)
        lax.fori_loop(0, 8, here, 0)

    def exchange_end():
        arrived("pages")
        load("pages_away", pages_away, pages.at[1])
        for u in range(4):
            vals[u, :, 128:256] = jnp.ones((1024, 128), BF)
        for half in range(2):
            value_new[half, :, 128:256] = jnp.ones((128, 128), BF)
        for name in ("pages", "pages_away", "keys", "values", "out"):
            loads[name].wait()
        arrived("keys", "values", "bias")

    gather_start(0)
    squares_start()
    exchange_start()
    visibility()
    squares_end()
    multiply(0, 0, 0)
    gather_second(0)
    gather_start(1)
    multiply(1, 0, 0)
    multiply_near(0)
    gather_third(0)
    multiply_mid(0)
    gather_second(1)
    exchange_end()
    multiply_far(0)
    project_end(0)
    query_start(0)
    gather_third(1)
    fresh_tokens(0)
    block(0, 0, 0)
    multiply_near(1)
    query_second(0)
    multiply_mid(1)
    block(0, 1, 0)
    block(0, 3, 0)
    multiply_far(1)
    project_end(1)
    query_start(1)
    fresh_tokens(1)
    arrived("q020u", "q020d")
    block(0, 2, 0)
    query_forward(0, 1)
    block(0, 1, 1)
    block(0, 3, 1)
    query_second(1)
    pass_on(0, 0)
    arrived("q021u", "q021d")
    block(0, 2, 1)
    block(0, 0, 1)
    block(1, 0, 0)
    query_forward(1, 1)
    pass_on(0, 1)
    block(1, 1, 0)
    block(1, 3, 0)
    plane_merge(0)
    arrived("q120u", "q120d")
    block(1, 2, 0)
    block(1, 1, 1)
    last_merge(0)
    out_start(0)
    block(1, 3, 1)
    pass_on(1, 0)
    arrived("q121u", "q121d")
    block(1, 2, 1)
    out_join(0)
    block(1, 0, 1)
    out_second(0)
    pass_on(1, 1)
    out_cross(0)
    plane_merge(1)
    out_third(0)
    last_merge(1)
    out_start(1)
    out_end(0)
    out_join(1)
    out_second(1)
    out_cross(1)
    out_third(1)
    out_end(1)
    for copy in made.values():
        copy.wait_send()


def call(*operands):
    vm = pl.BlockSpec(memory_space=pltpu.VMEM)
    anywhere = pl.BlockSpec(memory_space=pl.ANY)
    trees, tile = (4, 128, 128), (8, 128)
    shapes = [
        ((2, 4, 2, 2, 64, 1024), BF), ((4, 2) + tile, F32), ((2, 128, 128), F32), ((8, 1024, 768), BF),
        ((2, 128, 768), F32), ((512, 8192), BF), ((256, 64, 128), BF), ((256, 64, 128), BF), ((128, 512), F32),
        ((2, 64, 16, 512), BF), ((64, 16, 512), BF), (tile, jnp.int32), None,
        ((4, 2, 2) + trees, BF), ((2, 128, 128), BF), ((2, 128, 256), BF),
        ((4, 2, 2) + trees, BF), ((4, 2, 2) + tile, F32), ((3, 2, 2) + trees, BF), ((3, 2, 2) + tile, F32),
        ((2, 2) + trees, BF), ((2, 2) + tile, F32), ((2, 2) + trees, BF), ((2, 2) + tile, F32),
        ((2,) + trees, BF), ((2,) + tile, F32),
        ((4, 1024, 256), BF), ((2, 128, 512), BF), ((2, 2, 4, 2, 64, 1024), BF), ((2, 3, 3, 64, 1024), BF),
        ((2, 5, 64, 1024), BF),
    ]
    scratch = [pltpu.VMEM(*s) if s else pltpu.SMEM((2, 8, 128), jnp.int32) for s in shapes]
    return pl.pallas_call(
        kernel,
        out_shape=jax.ShapeDtypeStruct((2, 128, 1024), BF),
        in_specs=[vm] * 7 + [anywhere] * 6,
        out_specs=vm,
        scratch_shapes=scratch
        + [pltpu.SemaphoreType.DMA((176,)), pltpu.SemaphoreType.DMA((176,)), pltpu.SemaphoreType.DMA((32,))],
        compiler_params=pltpu.CompilerParams(
            collective_id=1, has_side_effects=True, vmem_limit_bytes=61 * 2**20
        ),
        cost_estimate=pl.CostEstimate(flops=15 * 10**9, bytes_accessed=30 * 2**20, transcendentals=10**7),
    )(*operands)


def rope_tables(row_length):
    spots = row_length[None, :] + jnp.arange(2, dtype=jnp.int32)[:, None]
    ladder = jnp.arange(64, dtype=F32) * (2.0 / 128)
    frequency = jnp.power(jnp.float32(ROPE_BASE), -ladder)
    angles = spots.astype(F32)[..., None] * frequency
    cosine, sine = jnp.cos(angles), jnp.sin(angles)
    return jnp.concatenate([cosine, cosine], axis=-1), jnp.concatenate([-sine, sine], axis=-1)


def body(
    hidden,
    norm_gain,
    w_query,
    key_weight,
    value_weight,
    w_out,
    key_cache,
    value_cache,
    tree_pages,
    page_fill,
    row_depth,
    row_length,
):
    cosine, sine = rope_tables(row_length)
    pages = tree_pages.reshape(8, 2, 64).transpose(1, 0, 2).reshape(2, 4, 128)
    pages = jnp.pad(pages, ((0, 0), (0, 4), (0, 0)))
    fill = jnp.pad(page_fill[0].astype(BF), ((0, 0), (0, 120)))
    depth = row_depth.reshape(16, 128).astype(F32)
    return call(
        hidden, norm_gain[None, :], cosine, sine, pages, fill, depth, w_query, key_weight, value_weight, w_out,
        key_cache.reshape(128, 64, 128), value_cache.reshape(128, 64, 128),
    )


def solution(mesh):
    in_specs = (
        P(None, "cache", "head"),
        P(),
        P(None, "head"),
        P(None, "head"),
        P(None, "head"),
        P("head", None),
        P("cache", None, "head", None),
        P("cache", None, "head", None),
        P("cache", None, None),
        P("cache", None, None),
        P("cache", None),
        P("cache"),
    )
    out_specs = P(None, "cache", "head")
    return jax.shard_map(body, mesh=mesh, in_specs=in_specs, out_specs=out_specs, check_vma=False)
```

```python
import math

import jax
import jax.numpy as jnp
from jax import lax
from jax.experimental import pallas as pl
from jax.experimental.pallas import tpu as pltpu
from jax.sharding import PartitionSpec as P

MESH = pl.DeviceIdType.MESH
ROPE_BASE = 500000.0
EPSILON = 1e-05
LOW_SCORE = -1e30
LOW_MAX = -1e29
EXP_SCALE = math.log2(math.e) / math.sqrt(128.0)
BF, F32 = jnp.bfloat16, jnp.float32
CHUNKS = 2
ROWS = 128 // CHUNKS
TREES = 8 // CHUNKS
SPOTS = [(dy, dz) for dy in range(4) for dz in range(2)]
ORDER = [(0, 0), (1, 0), (3, 0), (0, 1), (2, 0), (1, 1), (3, 1), (2, 1)]


def kernel(
    hidden_hbm, gain_hbm, cosine_hbm, sine_hbm, pages_in, fill_hbm, depth_hbm, w_query, key_weight, value_weight,
    w_out_hbm, key_hbm, value_hbm,
    out,
    hidden, gain_in, gain, cosine, sine, fill, depth,
    held, sums, scale, weight, total, w_out, keys, values, filled, bias, bias_away, pages_away, pages,
    q_all, key_new, value_new, part, part_stat, got, got_stat, relay, relay_stat, rowed, rowed_stat, fresh, fresh_stat,
    vals, att, sent, got_y, got_z,
    send_sem, recv_sem, load_sem,
):
    c, h = lax.axis_index("cache"), lax.axis_index("head")
    x, zl, core = c // 4, lax.rem(c // 2, 2), lax.rem(c, 2)
    y, zh = h // 2, lax.rem(h, 2)

    def in_head(dy, dz):
        return lax.rem(y + dy, 4) * 2 + (zh if dz == 0 else 1 - zh)

    def in_cache(dx, dz):
        return lax.rem(x + dx, 4) * 4 + (zl if dz == 0 else 1 - zl) * 2 + core

    y_up, y_down, z_far = (c, in_head(1, 0)), (c, in_head(3, 0)), (c, in_head(0, 1))
    x_up, x_down, z_near = (in_cache(1, 0), h), (in_cache(3, 0), h), (in_cache(0, 1), h)
    twin = (c + 1 - 2 * core, h)

    loads = {}

    def load(name, src, dst):
        loads[name] = pltpu.make_async_copy(src, dst, load_sem.at[len(loads)])
        loads[name].start()

    def fetched(*names):
        for name in names:
            loads[name].wait()

    load("hidden", hidden_hbm, hidden)
    load("gain", gain_hbm, gain_in)
    load("pages", pages_in, pages.at[0])
    load("fill", fill_hbm, fill)
    load("depth", depth_hbm, depth)
    load("cosine", cosine_hbm, cosine)
    load("sine", sine_hbm, sine)
    for number, spot in enumerate(ORDER):
        rows = pl.ds(pl.multiple_of(in_head(*spot) * 1024, 1024), 1024)
        load(("q", number), w_query.at[rows], weight.at[number, :, pl.ds(0, 512)])
        load(("k", number), key_weight.at[rows], weight.at[number, :, pl.ds(512, 128)])
        load(("v", number), value_weight.at[rows], weight.at[number, :, pl.ds(640, 128)])
    load("keys", key_hbm, keys.at[pl.ds(0, 128)])
    load("values", value_hbm, values.at[pl.ds(0, 128)])
    load("out", w_out_hbm, w_out)

    barrier = pltpu.get_barrier_semaphore()
    others = [(c, in_head(*spot)) for spot in SPOTS[1:]] + [x_up, x_down, z_near, twin]
    for device in others:
        pl.semaphore_signal(barrier, inc=1, device_id=device, device_id_type=MESH)
    pl.semaphore_wait(barrier, len(others))

    made = {}

    def send(name, src, dst, device):
        number = len(made)
        made[name] = pltpu.make_async_remote_copy(
            src_ref=src, dst_ref=dst, send_sem=send_sem.at[number], recv_sem=recv_sem.at[number],
            device_id=device, device_id_type=MESH,
        )
        made[name].start()

    done = set()

    def arrived(*names):
        for name in names:
            if name not in done:
                done.add(name)
                made[name].wait_recv()


    def g_start(half, p):
        rows = pl.ds(half * ROWS, ROWS)
        for name, to, dy, dz in (("01", z_far, 0, 1), ("30", y_up, 3, 0), ("10", y_down, 1, 0)):
            send(f"a{half}{p}{name}", hidden_hbm.at[p, rows], held.at[half, dy, dz, p], to)

    low_rows, high_rows = pl.ds(0, ROWS // 2), pl.ds(ROWS // 2, ROWS // 2)

    def g_z(half):
        arrived(f"a{half}001")
        send(f"a{half}031", held.at[half, 0, 1, 0], held.at[half, 3, 1, 0], y_up)
        send(f"a{half}011", held.at[half, 0, 1, 0], held.at[half, 1, 1, 0], y_down)

    def g_up(half, p, dz):
        a = f"a{half}{p}"
        arrived(f"{a}3{dz}")
        if p == 1:
            send(f"a{half}131", held.at[half, 3, 0, 1], held.at[half, 3, 1, 1], z_far)
        send(f"{a}2{dz}u", held.at[half, 3, dz, p, low_rows], held.at[half, 2, dz, p, low_rows], y_up)

    def g_down(half, p, dz):
        a = f"a{half}{p}"
        arrived(f"{a}1{dz}")
        if p == 1:
            send(f"a{half}111", held.at[half, 1, 0, 1], held.at[half, 1, 1, 1], z_far)
        send(f"{a}2{dz}d", held.at[half, 1, dz, p, high_rows], held.at[half, 2, dz, p, high_rows], y_down)

    def g_far(half, n):
        rows = low_rows if n == "u" else high_rows
        arrived(f"a{half}120{n}")
        send(f"a{half}121{n}", held.at[half, 2, 0, 1, rows], held.at[half, 2, 1, 1, rows], z_far)

    ready = set()

    def multiply(half, dy, dz):
        number = ORDER.index((dy, dz))
        if number not in ready:
            for array in "qkv":
                fetched((array, number))
            ready.add(number)
        if (dy, dz) == (0, 0):
            rows = pl.ds(half * ROWS, ROWS)
            block = jnp.concatenate([hidden[0, rows], hidden[1, rows]], axis=0)
        else:
            for p in range(2):
                a = f"a{half}{p}{dy}{dz}"
                arrived(*([a + "u", a + "d"] if dy == 2 else [a]))
            block = held[half, dy, dz].reshape(2 * ROWS, 1024)
        normed = block.astype(F32) * scale[half][:, 0:1] * gain[in_head(dy, dz)]
        product = jnp.dot(normed.astype(BF), weight[number], preferred_element_type=F32)
        if (dy, dz) == (0, 0):
            total[half] = product
        else:
            total[half] += product

    def project_end(half):
        rows = pl.ds(half * ROWS, ROWS)
        cos = jnp.concatenate([cosine[0, rows], cosine[1, rows]], axis=0)
        sin = jnp.concatenate([sine[0, rows], sine[1, rows]], axis=0)
        cos, sin = jnp.concatenate([cos, cos], axis=1), jnp.concatenate([-sin, sin], axis=1)

        def turned(u):
            return (u * cos + pltpu.roll(u, 64, 1) * sin).astype(BF)

        k = turned(total[half, :, 512:640])
        v = total[half, :, 640:768].astype(BF)
        for head in range(4):
            q = turned(total[half, :, head * 128 : (head + 1) * 128])
            for p in range(2):
                for u in range(TREES):
                    low = (p * 4 + head) * 16
                    q_all[0, 0, half, u, low : low + 16] = q[p * ROWS + u * 16 : p * ROWS + u * 16 + 16]
        for p in range(2):
            for u in range(TREES):
                low, there = p * ROWS + u * 16, u * 32 + p * 16
                key_new[half, there : there + 16] = k[low : low + 16]
                value_new[half, there : there + 16, 0:128] = v[low : low + 16]
        name = f"q{half}"
        send(name + "30", q_all.at[0, 0, half], q_all.at[3, 0, half], x_up)
        send(name + "10", q_all.at[0, 0, half], q_all.at[1, 0, half], x_down)
        send(name + "01", q_all.at[0, 0, half], q_all.at[0, 1, half], z_near)


    def q_up(half, dz):
        q, trees = f"q{half}", pl.ds(0, TREES // 2)
        arrived(f"{q}3{dz}")
        send(f"{q}2{dz}u", q_all.at[3, dz, half, trees], q_all.at[2, dz, half, trees], x_up)

    def q_down(half, dz):
        q, trees = f"q{half}", pl.ds(TREES // 2, TREES // 2)
        arrived(f"{q}1{dz}")
        send(f"{q}2{dz}d", q_all.at[1, dz, half, trees], q_all.at[2, dz, half, trees], x_down)

    def q_z(half):
        q = f"q{half}"
        arrived(q + "01")
        send(q + "31", q_all.at[0, 1, half], q_all.at[3, 1, half], x_up)
        send(q + "11", q_all.at[0, 1, half], q_all.at[1, 1, half], x_down)


    lane = lax.broadcasted_iota(jnp.int32, (128, 128), 1)
    new_lane = lax.broadcasted_iota(jnp.int32, (128, TREES * 32), 1)
    new_row = lax.broadcasted_iota(jnp.int32, (128, TREES * 32), 0)

    def fresh_tokens(half):
        stats = jnp.zeros((128, 128), F32)
        for u in range(TREES):
            seen = (new_lane // 32 == u) & (new_lane % 16 == new_row % 16)
            seen = seen & ((new_lane % 32) // 16 <= new_row // 64)
            s = lax.dot_general(
                q_all[0, 0, half, u], key_new[half], (((1,), (1,)), ((), ())), preferred_element_type=F32
            )
            s = jnp.where(seen, s, LOW_SCORE)
            m = jnp.max(s, axis=1, keepdims=True)
            p = jnp.exp2((s - m) * EXP_SCALE).astype(BF)
            o = jnp.dot(p, value_new[half], preferred_element_type=F32)
            fresh[half, u] = o[:, 0:128].astype(BF)
            stats = jnp.where(lane == u, m, stats)
            stats = jnp.where(lane == u + 4, o[:, 128:256], stats)
        fresh_stat[half] = jnp.transpose(stats)[0:8]

    def block(half, dx, dz):
        owner = lax.rem(x + dx, 4) * 2 + (zl if dz == 0 else 1 - zl)
        if (dx, dz) != (0, 0):
            q = f"q{half}{dx}{dz}"
            arrived(*([q + "u", q + "d"] if dx == 2 else [q]))
        stats = jnp.zeros((128, 128), F32)
        for u in range(TREES):
            tree = owner * 8 + half * TREES + u
            among = (owner * 2 + core) * 8 + half * TREES + u
            numbers = [pages[b, i, among] + b * 128 for b in range(2) for i in range(8)]
            k = jnp.concatenate([keys[n] for n in numbers], axis=0)
            s = lax.dot_general(
                q_all[dx, dz, half, u], k, (((1,), (1,)), ((), ())), preferred_element_type=F32
            )
            hide = jnp.concatenate([bias[0, tree], bias[1, tree]], axis=1).astype(F32)
            s = jnp.concatenate([s[i * 16 : (i + 1) * 16] + hide for i in range(8)], axis=0)
            m = jnp.maximum(jnp.max(s, axis=1, keepdims=True), LOW_MAX)
            p = jnp.exp2((s - m) * EXP_SCALE).astype(BF)
            for i in range(16):
                vals[u, i * 64 : (i + 1) * 64, 0:128] = values[numbers[i]]
            o = jnp.dot(p, vals[u], preferred_element_type=F32)
            part[dx, dz, half, u] = o[:, 0:128].astype(BF)
            stats = jnp.where(lane == u, m, stats)
            stats = jnp.where(lane == u + 4, o[:, 128:256], stats)
        part_stat[dx, dz, half] = jnp.transpose(stats)[0:8]
        if dx == 2:
            send_part(half, 2, dz, relay.at[dz, half], relay_stat.at[dz, half], x_up if dz == 0 else x_down)
        if (dx, dz) == (1, 1):
            send_part(half, 1, 1, got.at[0, 1, half], got_stat.at[0, 1, half], x_up)
        if (dx, dz) == (3, 0):
            send_part(half, 3, 0, got.at[1, 0, half], got_stat.at[1, 0, half], x_down)

    def send_part(half, dx, dz, to, to_stat, device):
        send(f"o{half}{dx}{dz}", part.at[dx, dz, half], to, device)
        send(f"s{half}{dx}{dz}", part_stat.at[dx, dz, half], to_stat, device)

    def c_join(half, dz):
        arrived(f"o{half}2{dz}", f"s{half}2{dz}")
        dx = 1 if dz == 0 else 3
        outs = [part.at[dx, dz, half], relay.at[dz, half]]
        top, weights, summed = weigh([part_stat[dx, dz, half], relay_stat[dz, half]])
        columns = columns_of(weights)
        for u in range(TREES):
            part[dx, dz, half, u] = mixed(columns, outs, u).astype(BF)
        part_stat[dx, dz, half] = jnp.concatenate([top, summed], axis=0)
        slot = 0 if dz == 0 else 1
        send_part(half, dx, dz, got.at[slot, dz, half], got_stat.at[slot, dz, half], x_up if dz == 0 else x_down)

    def weigh(stats):
        tops = [s[0:4] for s in stats]
        top = tops[0]
        for other in tops[1:]:
            top = jnp.maximum(top, other)
        weights = [jnp.exp2((m - top) * EXP_SCALE) for m in tops]
        summed = jnp.zeros((4, 128), F32)
        for w, s in zip(weights, stats):
            summed = summed + w * s[4:8]
        return top, weights, summed

    def columns_of(weights):
        stacked = jnp.concatenate(weights + [jnp.zeros((128 - 4 * len(weights), 128), F32)], axis=0)
        return jnp.transpose(stacked)

    def mixed(columns, outs, u):
        o = jnp.zeros((128, 128), F32)
        for i, ref in enumerate(outs):
            o = o + columns[:, i * 4 + u : i * 4 + u + 1] * ref[u].astype(F32)
        return o

    def received(half, dz):
        arrived(*[f"{a}{half}{dx}{dz}" for a in "os" for dx in (1, 3)])
        outs = [part.at[0, dz, half]] + [got.at[i, dz, half] for i in range(2)]
        return outs, [part_stat[0, dz, half]] + [got_stat[i, dz, half] for i in range(2)]

    def plane_merge(half):
        outs, stats = received(half, 1)
        top, weights, summed = weigh(stats)
        columns = columns_of(weights)
        for u in range(TREES):
            rowed[0, half, u] = mixed(columns, outs, u).astype(BF)
        rowed_stat[0, half] = jnp.concatenate([top, summed], axis=0)
        send(f"zo{half}", rowed.at[0, half], rowed.at[1, half], z_near)
        send(f"zs{half}", rowed_stat.at[0, half], rowed_stat.at[1, half], z_near)

    def last_merge(half):
        outs, stats = received(half, 0)
        arrived(f"zo{half}", f"zs{half}")
        top, weights, summed = weigh(stats + [rowed_stat[1, half], fresh_stat[half]])
        columns = columns_of([w / summed for w in weights])
        for u in range(TREES):
            o = mixed(columns, outs + [rowed.at[1, half], fresh.at[half]], u).astype(BF)
            for p in range(2):
                for head in range(4):
                    low, there = (p * 4 + head) * 16, p * ROWS + u * 16
                    att[half, there : there + 16, head * 128 : (head + 1) * 128] = o[low : low + 16]


    rings = {"p": (0, 0, 1), "q": (1, 0, 0), "r": (2, 1, 0)}

    def product(half, dy, dz):
        if "out" not in done:
            done.add("out")
            fetched("out")
        features = pl.ds(pl.multiple_of(in_head(dy, dz) * 1024, 1024), 1024)
        r = jnp.dot(att[half], w_out[:, features], preferred_element_type=F32).astype(BF)
        sent[half, dz, dy] = r.reshape(2, ROWS, 1024)

    def over_z(half, dy):
        send(f"z{half}{dy}", sent.at[half, 1, dy, 1], got_z.at[half, dy], z_far)

    def add_z(half, dy):
        arrived(f"z{half}{dy}")
        sent[half, 0, dy, 1] = (sent[half, 0, dy, 1].astype(F32) + got_z[half, dy].astype(F32)).astype(BF)

    def ring_far(half, name):
        ring, p, dz = rings[name]
        for rows, to, n in ((low_rows, y_up, "u"), (high_rows, y_down, "d")):
            send(f"{name}f{half}{n}", sent.at[half, dz, 2, p, rows], got_y.at[half, ring, 0, rows], to)

    def ring_near(half, name, dy):
        ring, p, dz = rings[name]
        rows, to, n, slot = (high_rows, y_up, "u", 2) if dy == 1 else (low_rows, y_down, "d", 1)
        send(f"{name}n{half}{n}", sent.at[half, dz, dy, p, rows], got_y.at[half, ring, slot, rows], to)

    def d_join(half, name, dy):
        ring, p, dz = rings[name]
        rows, to, n, slot = (low_rows, y_up, "u", 2) if dy == 1 else (high_rows, y_down, "d", 1)
        arrived(f"{name}f{half}{n}")
        summed = sent[half, dz, dy, p, rows].astype(F32) + got_y[half, ring, 0, rows].astype(F32)
        sent[half, dz, dy, p, rows] = summed.astype(BF)
        send(f"{name}j{half}{n}", sent.at[half, dz, dy, p, rows], got_y.at[half, ring, slot, rows], to)

    def ring_end(half, name):
        ring, p, dz = rings[name]
        arrived(*[f"{name}{s}{half}{n}" for s in "nj" for n in "ud"])
        r = sent[half, dz, 0, p].astype(F32)
        return r + got_y[half, ring, 1].astype(F32) + got_y[half, ring, 2].astype(F32)

    def d_far(half, dz):
        product(half, 2, dz)
        ring_far(half, "p" if dz else "q")
        if dz:
            over_z(half, 2)

    def d_near(half, dy, dz):
        product(half, dy, dz)
        if dz:
            over_z(half, dy)
        ring_near(half, "p" if dz else "q", dy)

    def d_own(half, dz):
        product(half, 0, dz)
        if dz:
            over_z(half, 0)

    def r_far(half):
        add_z(half, 2)
        ring_far(half, "r")

    def r_near(half, dy):
        add_z(half, dy)
        ring_near(half, "r", dy)

    def d_cross(half):
        sent[half, 1, 0, 0] = ring_end(half, "p").astype(BF)
        send(f"y{half}", sent.at[half, 1, 0, 0], got_z.at[half, 4], z_far)

    def d_end(half, p):
        rows = pl.ds(half * ROWS, ROWS)
        if p == 0:
            first = ring_end(half, "q")
            arrived(f"y{half}")
            out[0, rows] = (first + got_z[half, 4].astype(F32)).astype(BF)
        else:
            add_z(half, 0)
            out[1, rows] = ring_end(half, "r").astype(BF)


    def exchange_start():
        send("pages", pages_in, pages_away, twin)
        send("keys", key_hbm, keys.at[pl.ds(128, 128)], twin)
        send("values", value_hbm, values.at[pl.ds(128, 128)], twin)

    def squares_start():
        fetched("hidden")
        fetched("gain")
        for i in range(64):
            gain[i // 8, :, i % 8 * 128 : i % 8 * 128 + 128] = gain_in[i : i + 1].astype(F32)
        for p in range(2):
            wide = hidden[p].astype(F32)
            squares = jnp.sum(wide * wide, axis=-1, keepdims=True)
            sums[0, 0, pl.ds(p, 1)] = jnp.transpose(jnp.broadcast_to(squares, (128, 128)))[0:1]
        for dy, dz in SPOTS[1:]:
            send(f"t{dy}{dz}", sums.at[0, 0], sums.at[(4 - dy) % 4, dz], (c, in_head(dy, dz)))

    def squares_end():
        arrived(*[f"t{dy}{dz}" for dy, dz in SPOTS[1:]])
        for p in range(2):
            s = sums[0, 0, pl.ds(p, 1)]
            for dy, dz in SPOTS[1:]:
                s = s + sums[dy, dz, pl.ds(p, 1)]
            s = jnp.transpose(jnp.broadcast_to(lax.rsqrt(s * (1.0 / 8192) + EPSILON), (128, 128)))
            for half in range(CHUNKS):
                scale[half, p * ROWS : (p + 1) * ROWS] = s[half * ROWS : (half + 1) * ROWS]

    def visibility():
        slot_row = lax.broadcasted_iota(jnp.int32, (128, 512), 0)
        slot_lane = lax.broadcasted_iota(jnp.int32, (128, 512), 1) // 64
        spread = jnp.where(slot_row == slot_lane, 1.0, 0.0).astype(BF)
        fetched("fill")
        fetched("depth")
        fills_t = jnp.concatenate([fill[...].astype(F32), jnp.zeros((120, 128), F32)], axis=0)
        filled[...] = jnp.dot(jnp.transpose(fills_t).astype(BF), spread, preferred_element_type=F32)
        column = lax.broadcasted_iota(jnp.int32, (16, 512), 1)
        slot_of, token_of = (column // 64).astype(F32), (column % 64).astype(F32)

        def group(target, j, e):
            depth_row = depth[:, pl.ds(pl.multiple_of(e * 128, 128), 128)].astype(F32)
            depths = jnp.transpose(jnp.broadcast_to(depth_row, (128, 128)))
            fills = filled[pl.ds(pl.multiple_of(e * 8, 8), 8)]
            for t in range(8):
                d = jnp.concatenate([depths[t * 16 : t * 16 + 16]] * 4, axis=1)
                visible = (slot_of < d) & (token_of < fills[t : t + 1])
                target[j * 8 + t] = jnp.where(visible, 0.0, LOW_SCORE).astype(BF)

        def away(j, _):
            group(bias_away, j, j * 2 + 1 - core)
            return 0

        def here(j, _):
            group(bias.at[0], j, j * 2 + core)
            return 0

        lax.fori_loop(0, 8, away, 0)
        send("bias", bias_away, bias.at[1], twin)
        lax.fori_loop(0, 8, here, 0)

    def exchange_end():
        arrived("pages")
        load("pages_away", pages_away, pages.at[1])
        for u in range(TREES):
            vals[u, :, 128:256] = jnp.ones((1024, 128), BF)
        for half in range(CHUNKS):
            value_new[half, :, 128:256] = jnp.ones((TREES * 32, 128), BF)
        fetched("pages", "pages_away", "keys", "values", "cosine", "sine")
        arrived("keys", "values", "bias")

    g_start(0, 1)
    g_start(0, 0)
    g_start(1, 0)
    g_down(0, 1, 0)
    g_up(0, 1, 0)
    g_z(0)
    squares_start()
    exchange_start()
    visibility()
    exchange_end()
    g_far(0, "u")
    g_up(0, 0, 0)
    g_far(0, "d")
    g_down(0, 0, 0)
    g_up(0, 0, 1)
    g_down(0, 0, 1)
    g_start(1, 1)
    g_z(1)
    squares_end()
    multiply(0, 0, 0)
    multiply(0, 3, 1)
    multiply(0, 0, 1)
    multiply(0, 2, 0)
    multiply(0, 1, 1)
    multiply(0, 1, 0)
    multiply(0, 3, 0)
    multiply(0, 2, 1)
    project_end(0)
    g_down(1, 1, 0)
    g_up(1, 1, 0)
    g_down(1, 0, 0)
    q_down(0, 0)
    q_z(0)
    g_up(1, 0, 0)
    g_down(1, 0, 1)
    g_far(1, "d")
    q_up(0, 0)
    block(0, 0, 0)
    g_up(1, 0, 1)
    block(0, 3, 0)
    g_far(1, "u")
    multiply(1, 0, 0)
    multiply(1, 3, 0)
    multiply(1, 2, 0)
    multiply(1, 1, 1)
    multiply(1, 1, 0)
    multiply(1, 3, 1)
    multiply(1, 0, 1)
    q_up(0, 1)
    q_down(0, 1)
    block(0, 2, 0)
    multiply(1, 2, 1)
    project_end(1)
    fresh_tokens(1)
    block(0, 2, 1)
    block(0, 1, 1)
    q_z(1)
    block(0, 3, 1)
    c_join(0, 1)
    block(0, 1, 0)
    c_join(0, 0)
    q_down(1, 0)
    q_up(1, 1)
    q_down(1, 1)
    q_up(1, 0)
    block(0, 0, 1)
    plane_merge(0)
    fresh_tokens(0)
    block(1, 1, 1)
    block(1, 2, 1)
    block(1, 2, 0)
    last_merge(0)
    d_near(0, 1, 1)
    d_near(0, 3, 0)
    d_far(0, 0)
    d_near(0, 1, 0)
    d_own(0, 0)
    d_near(0, 3, 1)
    d_far(0, 1)
    d_own(0, 1)
    block(1, 3, 1)
    c_join(1, 1)
    block(1, 1, 0)
    block(1, 0, 1)
    c_join(1, 0)
    d_join(0, "p", 1)
    d_join(0, "p", 3)
    block(1, 3, 0)
    plane_merge(1)
    r_far(0)
    d_join(0, "q", 1)
    d_cross(0)
    block(1, 0, 0)
    d_join(0, "q", 3)
    r_near(0, 1)
    d_join(0, "r", 1)
    r_near(0, 3)
    d_join(0, "r", 3)
    last_merge(1)
    d_far(1, 1)
    d_far(1, 0)
    d_near(1, 1, 0)
    d_near(1, 1, 1)
    d_near(1, 3, 1)
    d_join(1, "p", 3)
    d_join(1, "p", 1)
    d_near(1, 3, 0)
    r_far(1)
    d_join(1, "q", 3)
    d_join(1, "q", 1)
    d_own(1, 1)
    d_cross(1)
    r_near(1, 1)
    d_join(1, "r", 1)
    r_near(1, 3)
    d_join(1, "r", 3)
    d_end(0, 0)
    d_end(0, 1)
    d_own(1, 0)
    d_end(1, 0)
    d_end(1, 1)
    for copy in made.values():
        copy.wait_send()


def call(*operands):
    vm = pl.BlockSpec(memory_space=pltpu.VMEM)
    anywhere = pl.BlockSpec(memory_space=pl.ANY)
    n, r = CHUNKS, ROWS
    trees, tile = (n, TREES, 128, 128), (8, 128)
    stat = (n,) + tile
    shapes = [
        ((2, 128, 1024), BF), ((64, 128), BF), ((8, 1, 1024), F32), ((2, 128, 64), F32), ((2, 128, 64), F32),
        (tile, jnp.int32), ((1, 2048), jnp.int32),
        ((n, 4, 2, 2, r, 1024), BF), ((4, 2) + tile, F32), ((n, 2 * r, 128), F32), ((8, 1024, 768), BF),
        ((n, 2 * r, 768), F32), ((512, 8192), BF), ((256, 64, 128), BF), ((256, 64, 128), BF), ((128, 512), F32),
        ((2, 64, 16, 512), BF), ((64, 16, 512), BF), (tile, jnp.int32), None,
        ((4, 2) + trees, BF), ((n, TREES * 32, 128), BF), ((n, TREES * 32, 256), BF),
        ((4, 2) + trees, BF), ((4, 2) + stat, F32), ((2, 2) + trees, BF), ((2, 2) + stat, F32),
        ((2,) + trees, BF), ((2,) + stat, F32), ((2,) + trees, BF), ((2,) + stat, F32),
        (trees, BF), (stat, F32),
        ((TREES, 1024, 256), BF), ((n, 2 * r, 512), BF), ((n, 2, 4, 2, r, 1024), BF), ((n, 3, 3, r, 1024), BF),
        ((n, 5, r, 1024), BF),
    ]
    scratch = [pltpu.VMEM(*s) if s else pltpu.SMEM((2, 8, 128), jnp.int32) for s in shapes]
    return pl.pallas_call(
        kernel,
        out_shape=jax.ShapeDtypeStruct((2, 128, 1024), BF),
        in_specs=[anywhere] * 13,
        out_specs=vm,
        scratch_shapes=scratch
        + [pltpu.SemaphoreType.DMA((166,)), pltpu.SemaphoreType.DMA((166,)), pltpu.SemaphoreType.DMA((40,))],
        compiler_params=pltpu.CompilerParams(
            collective_id=1, has_side_effects=True, vmem_limit_bytes=61 * 2**20
        ),
        cost_estimate=pl.CostEstimate(flops=15 * 10**9, bytes_accessed=30 * 2**20, transcendentals=10**7),
    )(*operands)


def rope_tables(row_length):
    spots = row_length[None, :] + jnp.arange(2, dtype=jnp.int32)[:, None]
    ladder = jnp.arange(64, dtype=F32) * (2.0 / 128)
    frequency = jnp.power(jnp.float32(ROPE_BASE), -ladder)
    angles = spots.astype(F32)[..., None] * frequency
    cosine, sine = jnp.cos(angles), jnp.sin(angles)
    return cosine, sine


def body(
    hidden,
    norm_gain,
    w_query,
    key_weight,
    value_weight,
    w_out,
    key_cache,
    value_cache,
    tree_pages,
    page_fill,
    row_depth,
    row_length,
):
    cosine, sine = rope_tables(row_length)
    pages, fill = jnp.transpose(tree_pages[0]), jnp.transpose(page_fill[0])
    return call(
        hidden, norm_gain.reshape(64, 128), cosine, sine, pages, fill, row_depth, w_query, key_weight, value_weight, w_out,
        key_cache.reshape(128, 64, 128), value_cache.reshape(128, 64, 128),
    )


def solution(mesh):
    in_specs = (
        P(None, "cache", "head"),
        P(),
        P(None, "head"),
        P(None, "head"),
        P(None, "head"),
        P("head", None),
        P("cache", None, "head", None),
        P("cache", None, "head", None),
        P("cache", None, None),
        P("cache", None, None),
        P("cache", None),
        P("cache"),
    )
    out_specs = P(None, "cache", "head")
    return jax.shard_map(body, mesh=mesh, in_specs=in_specs, out_specs=out_specs, check_vma=False)
```

```python
import math

import jax
import jax.numpy as jnp
from jax import lax
from jax.experimental import pallas as pl
from jax.experimental.pallas import tpu as pltpu
from jax.sharding import PartitionSpec as P

MESH = pl.DeviceIdType.MESH
ROPE_BASE = 500000.0
EPSILON = 1e-05
LOW_SCORE = -1e30
LOW_MAX = -1e29
EXP_SCALE = math.log2(math.e) / math.sqrt(128.0)
BF, F32 = jnp.bfloat16, jnp.float32
CHUNKS = 2
ROWS = 128 // CHUNKS
TREES = 8 // CHUNKS
FIRST = 80
SPOTS = [(dy, dz) for dy in range(4) for dz in range(2)]
ORDER = [(0, 0), (1, 0), (3, 0), (0, 1), (2, 0), (1, 1), (3, 1), (2, 1)]


def kernel(
    hidden_hbm, gain_hbm, cosine_hbm, sine_hbm, pages_in, fill_hbm, depth_hbm, w_query, key_weight, value_weight,
    w_out_hbm, key_hbm, value_hbm,
    out,
    gain_in, gain, cosine, sine, fill, depth,
    held, sums, scale, weight, total, w_out, keys, values, filled, bias, bias_away, pages_away, pages,
    q_all, key_new, value_new, part, part_stat, got, got_stat, relay, relay_stat, joined_stat, rowed, rowed_stat, fresh, fresh_stat,
    vals, att, sent, got_y, got_z,
    send_sem, recv_sem, load_sem,
):
    c, h = lax.axis_index("cache"), lax.axis_index("head")
    x, zl, core = c // 4, lax.rem(c // 2, 2), lax.rem(c, 2)
    y, zh = h // 2, lax.rem(h, 2)

    def in_head(dy, dz):
        return lax.rem(y + dy, 4) * 2 + (zh if dz == 0 else 1 - zh)

    def in_cache(dx, dz):
        return lax.rem(x + dx, 4) * 4 + (zl if dz == 0 else 1 - zl) * 2 + core

    y_up, y_down, z_far = (c, in_head(1, 0)), (c, in_head(3, 0)), (c, in_head(0, 1))
    x_up, x_down, z_near = (in_cache(1, 0), h), (in_cache(3, 0), h), (in_cache(0, 1), h)
    twin = (c + 1 - 2 * core, h)

    loads = {}

    def load(name, src, dst):
        loads[name] = pltpu.make_async_copy(src, dst, load_sem.at[len(loads)])
        loads[name].start()

    def fetched(*names):
        for name in names:
            loads[name].wait()

    for half in range(CHUNKS):
        for p in range(2):
            rows = pl.ds(half * ROWS, ROWS)
            load(("own", half, p), hidden_hbm.at[p, rows], held.at[half, 0, 0, pl.ds(p * ROWS, ROWS)])
    load("gain", gain_hbm, gain_in)
    load("pages", pages_in, pages.at[0])
    load("fill", fill_hbm, fill)
    load("depth", depth_hbm, depth)
    load("cosine", cosine_hbm, cosine)
    load("sine", sine_hbm, sine)
    for number, spot in enumerate(ORDER):
        rows = pl.ds(pl.multiple_of(in_head(*spot) * 1024, 1024), 1024)
        load(("q", number), w_query.at[rows], weight.at[number, :, pl.ds(0, 512)])
        load(("k", number), key_weight.at[rows], weight.at[number, :, pl.ds(512, 128)])
        load(("v", number), value_weight.at[rows], weight.at[number, :, pl.ds(640, 128)])
    load("keys", key_hbm, keys.at[pl.ds(0, 128)])
    load("values", value_hbm, values.at[pl.ds(0, 128)])
    load("out", w_out_hbm, w_out)

    barrier = pltpu.get_barrier_semaphore()
    others = [(c, in_head(*spot)) for spot in SPOTS[1:]] + [x_up, x_down, z_near, twin]
    for device in others:
        pl.semaphore_signal(barrier, inc=1, device_id=device, device_id_type=MESH)
    pl.semaphore_wait(barrier, len(others))

    made = {}
    done = set()

    def send(name, src, dst, device):
        number = len(made)
        made[name] = pltpu.make_async_remote_copy(
            src_ref=src, dst_ref=dst, send_sem=send_sem.at[number], recv_sem=recv_sem.at[number],
            device_id=device, device_id_type=MESH,
        )
        made[name].start()

    def arrived(*names):
        for name in names:
            if name not in done:
                done.add(name)
                made[name].wait_recv()


    group = (pl.ds(0, FIRST), pl.ds(FIRST, 2 * ROWS - FIRST))
    ups = (pl.ds(0, 48), pl.ds(80, 16))
    downs = (pl.ds(48, 32), pl.ds(96, 32))

    def g_start(half, p):
        if ("own", half) not in done:
            done.add(("own", half))
            fetched(("own", half, 0), ("own", half, 1))
        for name, to, dy, dz in (("01", z_far, 0, 1), ("30", y_up, 3, 0), ("10", y_down, 1, 0)):
            send(f"a{half}{p}{name}", held.at[half, 0, 0, group[p]], held.at[half, dy, dz, group[p]], to)

    def g_z(half):
        arrived(f"a{half}001")
        send(f"a{half}031", held.at[half, 0, 1, group[0]], held.at[half, 3, 1, group[0]], y_up)
        send(f"a{half}011", held.at[half, 0, 1, group[0]], held.at[half, 1, 1, group[0]], y_down)

    def g_up(half, p, dz):
        a = f"a{half}{p}"
        arrived(f"{a}3{dz}")
        if p == 1:
            send(f"a{half}131", held.at[half, 3, 0, group[1]], held.at[half, 3, 1, group[1]], z_far)
        send(f"{a}2{dz}u", held.at[half, 3, dz, ups[p]], held.at[half, 2, dz, ups[p]], y_up)

    def g_down(half, p, dz):
        a = f"a{half}{p}"
        arrived(f"{a}1{dz}")
        if p == 1:
            send(f"a{half}111", held.at[half, 1, 0, group[1]], held.at[half, 1, 1, group[1]], z_far)
        send(f"{a}2{dz}d", held.at[half, 1, dz, downs[p]], held.at[half, 2, dz, downs[p]], y_down)

    def g_far(half, n):
        rows = ups[1] if n == "u" else downs[1]
        arrived(f"a{half}120{n}")
        send(f"a{half}121{n}", held.at[half, 2, 0, rows], held.at[half, 2, 1, rows], z_far)

    ready = set()

    def multiply(half, dy, dz):
        number = ORDER.index((dy, dz))
        if number not in ready:
            for array in "qkv":
                fetched((array, number))
            ready.add(number)
        if (dy, dz) != (0, 0):
            for p in range(2):
                a = f"a{half}{p}{dy}{dz}"
                arrived(*([a + "u", a + "d"] if dy == 2 else [a]))
        block = held[half, dy, dz]
        normed = block.astype(F32) * scale[half][:, 0:1] * gain[in_head(dy, dz)]
        product = jnp.dot(normed.astype(BF), weight[number], preferred_element_type=F32)
        if (dy, dz) == (0, 0):
            total[half] = product
        else:
            total[half] += product

    def project_end(half):
        rows = pl.ds(half * ROWS, ROWS)
        cos = jnp.concatenate([cosine[0, rows], cosine[1, rows]], axis=0)
        sin = jnp.concatenate([sine[0, rows], sine[1, rows]], axis=0)
        cos, sin = jnp.concatenate([cos, cos], axis=1), jnp.concatenate([-sin, sin], axis=1)

        def turned(u):
            return (u * cos + pltpu.roll(u, 64, 1) * sin).astype(BF)

        k = turned(total[half, :, 512:640])
        v = total[half, :, 640:768].astype(BF)
        for head in range(4):
            q = turned(total[half, :, head * 128 : (head + 1) * 128])
            for p in range(2):
                for u in range(TREES):
                    low = (p * 4 + head) * 16
                    q_all[0, 0, half, u, low : low + 16] = q[p * ROWS + u * 16 : p * ROWS + u * 16 + 16]
        for p in range(2):
            for u in range(TREES):
                low, there = p * ROWS + u * 16, u * 32 + p * 16
                key_new[half, there : there + 16] = k[low : low + 16]
                value_new[half, there : there + 16, 0:128] = v[low : low + 16]
        name = f"q{half}"
        send(name + "30", q_all.at[0, 0, half], q_all.at[3, 0, half], x_up)
        send(name + "10", q_all.at[0, 0, half], q_all.at[1, 0, half], x_down)
        send(name + "01", q_all.at[0, 0, half], q_all.at[0, 1, half], z_near)


    low_trees, high_trees = pl.ds(0, TREES // 2), pl.ds(TREES // 2, TREES // 2)

    def q_up(half):
        arrived(f"q{half}30")
        send(f"q{half}20u", q_all.at[3, 0, half, low_trees], q_all.at[2, 0, half, low_trees], x_up)

    def q_down(half):
        arrived(f"q{half}10")
        send(f"q{half}20d", q_all.at[1, 0, half, high_trees], q_all.at[2, 0, half, high_trees], x_down)

    def q_cross(half, n):
        trees = low_trees if n == "u" else high_trees
        arrived(f"q{half}20{n}")
        send(f"q{half}21{n}", q_all.at[2, 0, half, trees], q_all.at[2, 1, half, trees], z_near)

    def q_z(half):
        q = f"q{half}"
        arrived(q + "01")
        send(q + "31", q_all.at[0, 1, half], q_all.at[3, 1, half], x_up)
        send(q + "11", q_all.at[0, 1, half], q_all.at[1, 1, half], x_down)


    lane = lax.broadcasted_iota(jnp.int32, (128, 128), 1)
    new_lane = lax.broadcasted_iota(jnp.int32, (128, TREES * 32), 1)
    new_row = lax.broadcasted_iota(jnp.int32, (128, TREES * 32), 0)

    def fresh_tokens(half):
        stats = jnp.zeros((128, 128), F32)
        for u in range(TREES):
            seen = (new_lane // 32 == u) & (new_lane % 16 == new_row % 16)
            seen = seen & ((new_lane % 32) // 16 <= new_row // 64)
            s = lax.dot_general(
                q_all[0, 0, half, u], key_new[half], (((1,), (1,)), ((), ())), preferred_element_type=F32
            )
            s = jnp.where(seen, s, LOW_SCORE)
            m = jnp.max(s, axis=1, keepdims=True)
            p = jnp.exp2((s - m) * EXP_SCALE).astype(BF)
            o = jnp.dot(p, value_new[half], preferred_element_type=F32)
            fresh[half, u] = o[:, 0:128].astype(BF)
            stats = jnp.where(lane == u, m, stats)
            stats = jnp.where(lane == u + 4, o[:, 128:256], stats)
        fresh_stat[half] = jnp.transpose(stats)[0:8]

    def block(half, dx, dz):
        owner = lax.rem(x + dx, 4) * 2 + (zl if dz == 0 else 1 - zl)
        if (dx, dz) != (0, 0):
            q = f"q{half}{dx}{dz}"
            arrived(*([q + "u", q + "d"] if dx == 2 else [q]))
        stats = jnp.zeros((128, 128), F32)
        for u in range(TREES):
            tree = owner * 8 + half * TREES + u
            among = (owner * 2 + core) * 8 + half * TREES + u
            numbers = [pages[b, i, among] + b * 128 for b in range(2) for i in range(8)]
            k = jnp.concatenate([keys[n] for n in numbers], axis=0)
            s = lax.dot_general(
                q_all[dx, dz, half, u], k, (((1,), (1,)), ((), ())), preferred_element_type=F32
            )
            hide = jnp.concatenate([bias[0, tree], bias[1, tree]], axis=1).astype(F32)
            s = jnp.concatenate([s[i * 16 : (i + 1) * 16] + hide for i in range(8)], axis=0)
            m = jnp.maximum(jnp.max(s, axis=1, keepdims=True), LOW_MAX)
            p = jnp.exp2((s - m) * EXP_SCALE).astype(BF)
            for i in range(16):
                vals[u, i * 64 : (i + 1) * 64, 0:128] = values[numbers[i]]
            o = jnp.dot(p, vals[u], preferred_element_type=F32)
            part[dx, dz, half, u] = o[:, 0:128].astype(BF)
            stats = jnp.where(lane == u, m, stats)
            stats = jnp.where(lane == u + 4, o[:, 128:256], stats)
        part_stat[dx, dz, half] = jnp.transpose(stats)[0:8]
        if dx == 2:
            send_part(half, 2, dz, relay.at[dz, half], relay_stat.at[dz, half], x_up if dz == 0 else x_down)
        if (dx, dz) == (1, 1):
            send_part(half, 1, 1, got.at[0, 1, half], got_stat.at[0, 1, half], x_up)
        if (dx, dz) == (3, 0):
            send_part(half, 3, 0, got.at[1, 0, half], got_stat.at[1, 0, half], x_down)

    def send_trees(name, k, src, dst, device):
        trees = low_trees if k == 0 else high_trees
        send(f"{name}{k}", src.at[trees], dst.at[trees], device)

    def send_part(half, dx, dz, to, to_stat, device):
        send(f"s{half}{dx}{dz}", part_stat.at[dx, dz, half], to_stat, device)
        for k in range(2):
            send_trees(f"o{half}{dx}{dz}", k, part.at[dx, dz, half], to, device)

    def some_trees(k):
        return range(k * TREES // 2, (k + 1) * TREES // 2)

    def c_join(half, dz, k):
        arrived(f"o{half}2{dz}{k}", f"s{half}2{dz}")
        dx, slot, device = (1, 0, x_up) if dz == 0 else (3, 1, x_down)
        outs = [part.at[dx, dz, half], relay.at[dz, half]]
        top, weights, summed = weigh([part_stat[dx, dz, half], relay_stat[dz, half]])
        columns = columns_of(weights)
        if k == 0:
            joined_stat[dz, half] = jnp.concatenate([top, summed], axis=0)
            send(f"s{half}{dx}{dz}", joined_stat.at[dz, half], got_stat.at[slot, dz, half], device)
        for u in some_trees(k):
            part[dx, dz, half, u] = mixed(columns, outs, u).astype(BF)
        send_trees(f"o{half}{dx}{dz}", k, part.at[dx, dz, half], got.at[slot, dz, half], device)

    def weigh(stats):
        tops = [s[0:4] for s in stats]
        top = tops[0]
        for other in tops[1:]:
            top = jnp.maximum(top, other)
        weights = [jnp.exp2((m - top) * EXP_SCALE) for m in tops]
        summed = jnp.zeros((4, 128), F32)
        for w, s in zip(weights, stats):
            summed = summed + w * s[4:8]
        return top, weights, summed

    def columns_of(weights):
        stacked = jnp.concatenate(weights + [jnp.zeros((128 - 4 * len(weights), 128), F32)], axis=0)
        return jnp.transpose(stacked)

    def mixed(columns, outs, u):
        o = jnp.zeros((128, 128), F32)
        for i, ref in enumerate(outs):
            o = o + columns[:, i * 4 + u : i * 4 + u + 1] * ref[u].astype(F32)
        return o

    def received(half, dz, k):
        for dx in (1, 3):
            arrived(f"s{half}{dx}{dz}", f"o{half}{dx}{dz}{k}")
        outs = [part.at[0, dz, half]] + [got.at[i, dz, half] for i in range(2)]
        return outs, [part_stat[0, dz, half]] + [got_stat[i, dz, half] for i in range(2)]

    def plane_merge(half, k):
        outs, stats = received(half, 1, k)
        top, weights, summed = weigh(stats)
        columns = columns_of(weights)
        if k == 0:
            rowed_stat[0, half] = jnp.concatenate([top, summed], axis=0)
            send(f"zs{half}", rowed_stat.at[0, half], rowed_stat.at[1, half], z_near)
        for u in some_trees(k):
            rowed[0, half, u] = mixed(columns, outs, u).astype(BF)
        send_trees(f"zo{half}", k, rowed.at[0, half], rowed.at[1, half], z_near)

    def last_merge(half, k):
        outs, stats = received(half, 0, k)
        arrived(f"zs{half}", f"zo{half}{k}")
        top, weights, summed = weigh(stats + [rowed_stat[1, half], fresh_stat[half]])
        columns = columns_of([w / summed for w in weights])
        for u in some_trees(k):
            o = mixed(columns, outs + [rowed.at[1, half], fresh.at[half]], u).astype(BF)
            for p in range(2):
                for head in range(4):
                    low, there = (p * 4 + head) * 16, p * ROWS + u * 16
                    att[half, there : there + 16, head * 128 : (head + 1) * 128] = o[low : low + 16]


    rings = {"p": (0, 0, 1), "q": (1, 0, 0), "r": (2, 1, 0)}

    def product(half, dy, dz):
        if "out" not in done:
            done.add("out")
            fetched("out")
        features = pl.ds(pl.multiple_of(in_head(dy, dz) * 1024, 1024), 1024)
        r = jnp.dot(att[half], w_out[:, features], preferred_element_type=F32).astype(BF)
        sent[half, dz, dy] = r

    def over_z(half, dy):
        send(f"z{half}{dy}", sent.at[half, 1, dy, group[1]], got_z.at[half, dy, group[1]], z_far)

    def add_z(half, dy):
        arrived(f"z{half}{dy}")
        rows = group[1]
        sent[half, 0, dy, rows] = (sent[half, 0, dy, rows].astype(F32) + got_z[half, dy, rows].astype(F32)).astype(BF)

    def ring_far(half, name):
        ring, p, dz = rings[name]
        for rows, to, n in ((ups[p], y_up, "u"), (downs[p], y_down, "d")):
            send(f"{name}f{half}{n}", sent.at[half, dz, 2, rows], got_y.at[half, ring, 0, rows], to)

    def ring_near(half, name, dy):
        ring, p, dz = rings[name]
        rows, to, n, slot = (downs[p], y_up, "u", 2) if dy == 1 else (ups[p], y_down, "d", 1)
        send(f"{name}n{half}{n}", sent.at[half, dz, dy, rows], got_y.at[half, ring, slot, rows], to)

    def d_join(half, name, dy):
        ring, p, dz = rings[name]
        rows, to, n, slot = (ups[p], y_up, "u", 2) if dy == 1 else (downs[p], y_down, "d", 1)
        arrived(f"{name}f{half}{n}")
        summed = sent[half, dz, dy, rows].astype(F32) + got_y[half, ring, 0, rows].astype(F32)
        sent[half, dz, dy, rows] = summed.astype(BF)
        send(f"{name}j{half}{n}", sent.at[half, dz, dy, rows], got_y.at[half, ring, slot, rows], to)

    def ring_end(half, name):
        ring, p, dz = rings[name]
        arrived(*[f"{name}{s}{half}{n}" for s in "nj" for n in "ud"])
        rows = group[p]
        r = sent[half, dz, 0, rows].astype(F32)
        return r + got_y[half, ring, 1, rows].astype(F32) + got_y[half, ring, 2, rows].astype(F32)

    def d_far(half, dz):
        product(half, 2, dz)
        ring_far(half, "p" if dz else "q")
        if dz:
            over_z(half, 2)

    def d_near(half, dy, dz):
        product(half, dy, dz)
        if dz:
            over_z(half, dy)
        ring_near(half, "p" if dz else "q", dy)

    def d_own(half, dz):
        product(half, 0, dz)
        if dz:
            over_z(half, 0)

    def r_far(half):
        add_z(half, 2)
        ring_far(half, "r")

    def r_near(half, dy):
        add_z(half, dy)
        ring_near(half, "r", dy)

    def d_cross(half):
        sent[half, 1, 0, group[0]] = ring_end(half, "p").astype(BF)
        send(f"y{half}", sent.at[half, 1, 0, group[0]], got_z.at[half, 4, group[0]], z_far)

    def d_end(half, p):
        low = half * ROWS
        if p == 0:
            first = ring_end(half, "q")
            arrived(f"y{half}")
            first = (first + got_z[half, 4, group[0]].astype(F32)).astype(BF)
            out[0, low : low + ROWS] = first[0:ROWS]
            out[1, low : low + FIRST - ROWS] = first[ROWS:FIRST]
        else:
            add_z(half, 0)
            out[1, low + FIRST - ROWS : low + ROWS] = ring_end(half, "r").astype(BF)


    def exchange_start():
        send("pages", pages_in, pages_away, twin)
        send("keys", key_hbm, keys.at[pl.ds(128, 128)], twin)
        send("values", value_hbm, values.at[pl.ds(128, 128)], twin)

    def squares_start():
        for half in range(CHUNKS):
            if ("own", half) not in done:
                done.add(("own", half))
                fetched(("own", half, 0), ("own", half, 1))
        fetched("gain")
        for i in range(64):
            gain[i // 8, :, i % 8 * 128 : i % 8 * 128 + 128] = gain_in[i : i + 1].astype(F32)
        for p in range(2):
            rows = slice(p * ROWS, (p + 1) * ROWS)
            wide = jnp.concatenate([held[half, 0, 0, rows] for half in range(CHUNKS)], axis=0).astype(F32)
            squares = jnp.sum(wide * wide, axis=-1, keepdims=True)
            sums[0, 0, pl.ds(p, 1)] = jnp.transpose(jnp.broadcast_to(squares, (128, 128)))[0:1]
        for dy, dz in SPOTS[1:]:
            send(f"t{dy}{dz}", sums.at[0, 0], sums.at[(4 - dy) % 4, dz], (c, in_head(dy, dz)))

    def squares_end():
        arrived(*[f"t{dy}{dz}" for dy, dz in SPOTS[1:]])
        for p in range(2):
            s = sums[0, 0, pl.ds(p, 1)]
            for dy, dz in SPOTS[1:]:
                s = s + sums[dy, dz, pl.ds(p, 1)]
            s = jnp.transpose(jnp.broadcast_to(lax.rsqrt(s * (1.0 / 8192) + EPSILON), (128, 128)))
            for half in range(CHUNKS):
                scale[half, p * ROWS : (p + 1) * ROWS] = s[half * ROWS : (half + 1) * ROWS]

    def visibility():
        slot_row = lax.broadcasted_iota(jnp.int32, (128, 512), 0)
        slot_lane = lax.broadcasted_iota(jnp.int32, (128, 512), 1) // 64
        spread = jnp.where(slot_row == slot_lane, 1.0, 0.0).astype(BF)
        fetched("fill")
        fetched("depth")
        fills_t = jnp.concatenate([fill[...].astype(F32), jnp.zeros((120, 128), F32)], axis=0)
        filled[...] = jnp.dot(jnp.transpose(fills_t).astype(BF), spread, preferred_element_type=F32)
        column = lax.broadcasted_iota(jnp.int32, (16, 512), 1)
        slot_of, token_of = (column // 64).astype(F32), (column % 64).astype(F32)

        def group(target, j, e):
            depth_row = depth[:, pl.ds(pl.multiple_of(e * 128, 128), 128)].astype(F32)
            depths = jnp.transpose(jnp.broadcast_to(depth_row, (128, 128)))
            fills = filled[pl.ds(pl.multiple_of(e * 8, 8), 8)]
            for t in range(8):
                d = jnp.concatenate([depths[t * 16 : t * 16 + 16]] * 4, axis=1)
                visible = (slot_of < d) & (token_of < fills[t : t + 1])
                target[j * 8 + t] = jnp.where(visible, 0.0, LOW_SCORE).astype(BF)

        def away(j, _):
            group(bias_away, j, j * 2 + 1 - core)
            return 0

        def here(j, _):
            group(bias.at[0], j, j * 2 + core)
            return 0

        lax.fori_loop(0, 8, away, 0)
        send("bias", bias_away, bias.at[1], twin)
        lax.fori_loop(0, 8, here, 0)

    def exchange_end():
        arrived("pages")
        load("pages_away", pages_away, pages.at[1])
        for u in range(TREES):
            vals[u, :, 128:256] = jnp.ones((1024, 128), BF)
        for half in range(CHUNKS):
            value_new[half, :, 128:256] = jnp.ones((TREES * 32, 128), BF)
        fetched("pages", "pages_away", "keys", "values", "cosine", "sine")
        arrived("keys", "values", "bias")

    g_start(1, 1)
    squares_start()
    g_start(1, 0)
    exchange_start()
    visibility()
    exchange_end()
    g_down(1, 1, 0)
    g_up(1, 1, 0)
    squares_end()
    multiply(0, 0, 0)
    g_start(0, 1)
    multiply(1, 0, 0)
    g_z(1)
    multiply(1, 3, 0)
    multiply(1, 1, 0)
    g_up(1, 0, 0)
    g_down(1, 0, 0)
    g_far(1, "u")
    g_far(1, "d")
    multiply(1, 0, 1)
    g_up(1, 0, 1)
    g_down(1, 0, 1)
    g_start(0, 0)
    g_down(0, 1, 0)
    multiply(1, 1, 1)
    multiply(1, 3, 1)
    multiply(1, 2, 0)
    multiply(1, 2, 1)
    project_end(1)
    g_up(0, 1, 0)
    g_z(0)
    multiply(0, 0, 1)
    block(1, 0, 0)
    g_far(0, "u")
    g_far(0, "d")
    g_up(0, 0, 0)
    fresh_tokens(1)
    g_down(0, 0, 0)
    multiply(0, 3, 0)
    q_up(1)
    q_down(1)
    multiply(0, 1, 0)
    block(1, 3, 0)
    g_up(0, 0, 1)
    multiply(0, 1, 1)
    g_down(0, 0, 1)
    block(1, 0, 1)
    q_cross(1, "d")
    q_z(1)
    multiply(0, 3, 1)
    q_cross(1, "u")
    multiply(0, 2, 0)
    block(1, 1, 0)
    multiply(0, 2, 1)
    project_end(0)
    block(1, 2, 0)
    block(1, 2, 1)
    block(1, 3, 1)
    fresh_tokens(0)
    q_up(0)
    q_down(0)
    block(1, 1, 1)
    c_join(1, 1, 0)
    block(0, 0, 1)
    c_join(1, 1, 1)
    q_cross(0, "u")
    q_z(0)
    q_cross(0, "d")
    c_join(1, 0, 0)
    c_join(1, 0, 1)
    block(0, 2, 0)
    plane_merge(1, 0)
    plane_merge(1, 1)
    block(0, 1, 0)
    block(0, 2, 1)
    block(0, 1, 1)
    last_merge(1, 0)
    last_merge(1, 1)
    d_far(1, 1)
    d_near(1, 3, 1)
    d_near(1, 1, 0)
    block(0, 3, 1)
    c_join(0, 1, 0)
    c_join(0, 1, 1)
    d_far(1, 0)
    c_join(0, 0, 0)
    c_join(0, 0, 1)
    d_near(1, 1, 1)
    d_join(1, "p", 1)
    r_far(1)
    d_join(1, "p", 3)
    block(0, 3, 0)
    plane_merge(0, 0)
    plane_merge(0, 1)
    d_near(1, 3, 0)
    r_near(1, 3)
    d_own(1, 0)
    d_join(1, "r", 3)
    d_join(1, "q", 1)
    r_near(1, 1)
    d_own(1, 1)
    d_join(1, "q", 3)
    block(0, 0, 0)
    d_cross(1)
    last_merge(0, 0)
    d_join(1, "r", 1)
    last_merge(0, 1)
    d_own(0, 0)
    d_far(0, 1)
    d_near(0, 1, 1)
    d_near(0, 3, 1)
    d_far(0, 0)
    d_own(0, 1)
    d_join(0, "p", 1)
    d_join(0, "p", 3)
    r_far(0)
    d_near(0, 3, 0)
    d_join(0, "q", 3)
    d_near(0, 1, 0)
    d_end(1, 1)
    r_near(0, 1)
    d_cross(0)
    d_end(1, 0)
    d_join(0, "r", 1)
    d_join(0, "q", 1)
    r_near(0, 3)
    d_join(0, "r", 3)
    d_end(0, 1)
    d_end(0, 0)
    for copy in made.values():
        copy.wait_send()


def call(*operands):
    vm = pl.BlockSpec(memory_space=pltpu.VMEM)
    anywhere = pl.BlockSpec(memory_space=pl.ANY)
    n, r = CHUNKS, ROWS
    trees, tile = (n, TREES, 128, 128), (8, 128)
    stat = (n,) + tile
    shapes = [
        ((64, 128), BF), ((8, 1, 1024), F32), ((2, 128, 64), F32), ((2, 128, 64), F32),
        (tile, jnp.int32), ((1, 2048), jnp.int32),
        ((n, 4, 2, 2 * r, 1024), BF), ((4, 2) + tile, F32), ((n, 2 * r, 128), F32), ((8, 1024, 768), BF),
        ((n, 2 * r, 768), F32), ((512, 8192), BF), ((256, 64, 128), BF), ((256, 64, 128), BF), ((128, 512), F32),
        ((2, 64, 16, 512), BF), ((64, 16, 512), BF), (tile, jnp.int32), None,
        ((4, 2) + trees, BF), ((n, TREES * 32, 128), BF), ((n, TREES * 32, 256), BF),
        ((4, 2) + trees, BF), ((4, 2) + stat, F32), ((2, 2) + trees, BF), ((2, 2) + stat, F32),
        ((2,) + trees, BF), ((2,) + stat, F32), ((2,) + stat, F32), ((2,) + trees, BF), ((2,) + stat, F32),
        (trees, BF), (stat, F32),
        ((TREES, 1024, 256), BF), ((n, 2 * r, 512), BF), ((n, 2, 4, 2 * r, 1024), BF),
        ((n, 3, 3, 2 * r, 1024), BF), ((n, 5, 2 * r, 1024), BF),
    ]
    scratch = [pltpu.VMEM(*s) if s else pltpu.SMEM((2, 8, 128), jnp.int32) for s in shapes]
    return pl.pallas_call(
        kernel,
        out_shape=jax.ShapeDtypeStruct((2, 128, 1024), BF),
        in_specs=[anywhere] * 13,
        out_specs=vm,
        scratch_shapes=scratch
        + [pltpu.SemaphoreType.DMA((196,)), pltpu.SemaphoreType.DMA((196,)), pltpu.SemaphoreType.DMA((40,))],
        compiler_params=pltpu.CompilerParams(
            collective_id=1, has_side_effects=True, vmem_limit_bytes=60 * 2**20
        ),
        cost_estimate=pl.CostEstimate(flops=15 * 10**9, bytes_accessed=30 * 2**20, transcendentals=10**7),
    )(*operands)


def rope_tables(row_length):
    spots = row_length[None, :] + jnp.arange(2, dtype=jnp.int32)[:, None]
    ladder = jnp.arange(64, dtype=F32) * (2.0 / 128)
    frequency = jnp.power(jnp.float32(ROPE_BASE), -ladder)
    angles = spots.astype(F32)[..., None] * frequency
    cosine, sine = jnp.cos(angles), jnp.sin(angles)
    return cosine, sine


def body(
    hidden,
    norm_gain,
    w_query,
    key_weight,
    value_weight,
    w_out,
    key_cache,
    value_cache,
    tree_pages,
    page_fill,
    row_depth,
    row_length,
):
    cosine, sine = rope_tables(row_length)
    pages, fill = jnp.transpose(tree_pages[0]), jnp.transpose(page_fill[0])
    return call(
        hidden, norm_gain.reshape(64, 128), cosine, sine, pages, fill, row_depth, w_query, key_weight, value_weight, w_out,
        key_cache.reshape(128, 64, 128), value_cache.reshape(128, 64, 128),
    )


def solution(mesh):
    in_specs = (
        P(None, "cache", "head"),
        P(),
        P(None, "head"),
        P(None, "head"),
        P(None, "head"),
        P("head", None),
        P("cache", None, "head", None),
        P("cache", None, "head", None),
        P("cache", None, None),
        P("cache", None, None),
        P("cache", None),
        P("cache"),
    )
    out_specs = P(None, "cache", "head")
    return jax.shard_map(body, mesh=mesh, in_specs=in_specs, out_specs=out_specs, check_vma=False)
```

```python
import math

import jax
import jax.numpy as jnp
import numpy as np
from jax import lax
from jax.experimental import pallas as pl
from jax.experimental.pallas import tpu as pltpu
from jax.sharding import PartitionSpec as P

MESH = pl.DeviceIdType.MESH
ROPE_BASE = 500000.0
EPSILON = 1e-05
LOW_SCORE = -1e30
LOW_MAX = -1e29
EXP_SCALE = math.log2(math.e) / math.sqrt(128.0)
BF, F32 = jnp.bfloat16, jnp.float32
CHUNKS = 2
ROWS = 128 // CHUNKS
TREES = 8 // CHUNKS
FIRST = 80
SPOTS = [(dy, dz) for dy in range(4) for dz in range(2)]
ORDER = [(0, 0), (1, 0), (3, 0), (0, 1), (2, 0), (1, 1), (3, 1), (2, 1)]


def kernel(
    hidden_hbm, gain_hbm, lengths_hbm, frequency_hbm, pages_in, fill_hbm, depth_hbm, w_query, key_weight, value_weight,
    w_out_hbm, key_hbm, value_hbm,
    out,
    gain_in, gain, lengths, frequency, cosine, sine, fill, depth,
    held, sums, scale, weight, total, w_out, keys, values, filled, bias, bias_away, pages_away, pages,
    q_all, key_new, value_new, part, part_stat, got, got_stat, relay, relay_stat, joined_stat, rowed, rowed_stat, fresh, fresh_stat,
    vals, att, sent, got_y, got_z,
    send_sem, recv_sem, load_sem,
):
    c, h = lax.axis_index("cache"), lax.axis_index("head")
    x, zl, core = c // 4, lax.rem(c // 2, 2), lax.rem(c, 2)
    y, zh = h // 2, lax.rem(h, 2)

    def in_head(dy, dz):
        return lax.rem(y + dy, 4) * 2 + (zh if dz == 0 else 1 - zh)

    def in_cache(dx, dz):
        return lax.rem(x + dx, 4) * 4 + (zl if dz == 0 else 1 - zl) * 2 + core

    y_up, y_down, z_far = (c, in_head(1, 0)), (c, in_head(3, 0)), (c, in_head(0, 1))
    x_up, x_down, z_near = (in_cache(1, 0), h), (in_cache(3, 0), h), (in_cache(0, 1), h)
    twin = (c + 1 - 2 * core, h)

    loads = {}

    def load(name, src, dst):
        loads[name] = pltpu.make_async_copy(src, dst, load_sem.at[len(loads)])
        loads[name].start()

    def fetched(*names):
        for name in names:
            loads[name].wait()

    for half in range(CHUNKS):
        for p in range(2):
            rows = pl.ds(half * ROWS, ROWS)
            load(("own", half, p), hidden_hbm.at[p, rows], held.at[half, 0, 0, pl.ds(p * ROWS, ROWS)])
    load("gain", gain_hbm, gain_in)
    load("pages", pages_in, pages.at[0])
    load("fill", fill_hbm, fill)
    load("depth", depth_hbm, depth)
    load("lengths", lengths_hbm, lengths)
    load("frequency", frequency_hbm, frequency)
    for number, spot in enumerate(ORDER):
        rows = pl.ds(pl.multiple_of(in_head(*spot) * 1024, 1024), 1024)
        load(("q", number), w_query.at[rows], weight.at[number, :, pl.ds(0, 512)])
        load(("k", number), key_weight.at[rows], weight.at[number, :, pl.ds(512, 128)])
        load(("v", number), value_weight.at[rows], weight.at[number, :, pl.ds(640, 128)])
    load("keys", key_hbm, keys.at[pl.ds(0, 128)])
    load("values", value_hbm, values.at[pl.ds(0, 128)])
    load("out", w_out_hbm, w_out)

    barrier = pltpu.get_barrier_semaphore()
    others = [(c, in_head(*spot)) for spot in SPOTS[1:]] + [x_up, x_down, z_near, twin]
    for device in others:
        pl.semaphore_signal(barrier, inc=1, device_id=device, device_id_type=MESH)
    pl.semaphore_wait(barrier, len(others))

    made = {}
    done = set()

    def send(name, src, dst, device):
        number = len(made)
        made[name] = pltpu.make_async_remote_copy(
            src_ref=src, dst_ref=dst, send_sem=send_sem.at[number], recv_sem=recv_sem.at[number],
            device_id=device, device_id_type=MESH,
        )
        made[name].start()

    def arrived(*names):
        for name in names:
            if name not in done:
                done.add(name)
                made[name].wait_recv()


    group = (pl.ds(0, FIRST), pl.ds(FIRST, 2 * ROWS - FIRST))
    ups = (pl.ds(0, 48), pl.ds(80, 16))
    downs = (pl.ds(48, 32), pl.ds(96, 32))

    def g_start(half, p):
        if ("own", half) not in done:
            done.add(("own", half))
            fetched(("own", half, 0), ("own", half, 1))
        for name, to, dy, dz in (("01", z_far, 0, 1), ("30", y_up, 3, 0), ("10", y_down, 1, 0)):
            send(f"a{half}{p}{name}", held.at[half, 0, 0, group[p]], held.at[half, dy, dz, group[p]], to)

    def g_z(half):
        arrived(f"a{half}001")
        send(f"a{half}031", held.at[half, 0, 1, group[0]], held.at[half, 3, 1, group[0]], y_up)
        send(f"a{half}011", held.at[half, 0, 1, group[0]], held.at[half, 1, 1, group[0]], y_down)

    def g_up(half, p, dz):
        a = f"a{half}{p}"
        arrived(f"{a}3{dz}")
        if p == 1:
            send(f"a{half}131", held.at[half, 3, 0, group[1]], held.at[half, 3, 1, group[1]], z_far)
        send(f"{a}2{dz}u", held.at[half, 3, dz, ups[p]], held.at[half, 2, dz, ups[p]], y_up)

    def g_down(half, p, dz):
        a = f"a{half}{p}"
        arrived(f"{a}1{dz}")
        if p == 1:
            send(f"a{half}111", held.at[half, 1, 0, group[1]], held.at[half, 1, 1, group[1]], z_far)
        send(f"{a}2{dz}d", held.at[half, 1, dz, downs[p]], held.at[half, 2, dz, downs[p]], y_down)

    def g_far(half, n):
        rows = ups[1] if n == "u" else downs[1]
        arrived(f"a{half}120{n}")
        send(f"a{half}121{n}", held.at[half, 2, 0, rows], held.at[half, 2, 1, rows], z_far)

    ready = set()

    def multiply(half, dy, dz):
        number = ORDER.index((dy, dz))
        if number not in ready:
            for array in "qkv":
                fetched((array, number))
            ready.add(number)
        if (dy, dz) != (0, 0):
            for p in range(2):
                a = f"a{half}{p}{dy}{dz}"
                arrived(*([a + "u", a + "d"] if dy == 2 else [a]))
        block = held[half, dy, dz]
        normed = block.astype(F32) * scale[half][:, 0:1] * gain[in_head(dy, dz)]
        product = jnp.dot(normed.astype(BF), weight[number], preferred_element_type=F32)
        if (dy, dz) == (0, 0):
            total[half] = product
        else:
            total[half] += product

    low_trees, high_trees = pl.ds(0, TREES // 2), pl.ds(TREES // 2, TREES // 2)

    def project_end(half):
        rows = pl.ds(half * ROWS, ROWS)
        cos = jnp.concatenate([cosine[0, rows], cosine[1, rows]], axis=0)
        sin = jnp.concatenate([sine[0, rows], sine[1, rows]], axis=0)
        cos, sin = jnp.concatenate([cos, cos], axis=1), jnp.concatenate([-sin, sin], axis=1)

        def turned(u):
            return (u * cos + pltpu.roll(u, 64, 1) * sin).astype(BF)

        k = turned(total[half, :, 512:640])
        v = total[half, :, 640:768].astype(BF)
        for head in range(4):
            q = turned(total[half, :, head * 128 : (head + 1) * 128])
            for p in range(2):
                for u in range(TREES):
                    low = (p * 4 + head) * 16
                    q_all[0, 0, half, u, low : low + 16] = q[p * ROWS + u * 16 : p * ROWS + u * 16 + 16]
        for p in range(2):
            for u in range(TREES):
                low, there = p * ROWS + u * 16, u * 32 + p * 16
                key_new[half, there : there + 16] = k[low : low + 16]
                value_new[half, there : there + 16, 0:128] = v[low : low + 16]
        name = f"q{half}"
        for first, there, trees, device in (
            ("30l", 3, low_trees, x_up), ("10h", 1, high_trees, x_down),
            ("30h", 3, high_trees, x_up), ("10l", 1, low_trees, x_down),
        ):
            send(name + first, q_all.at[0, 0, half, trees], q_all.at[there, 0, half, trees], device)
        send(name + "01", q_all.at[0, 0, half], q_all.at[0, 1, half], z_near)


    def q_up(half):
        arrived(f"q{half}30l")
        send(f"q{half}20u", q_all.at[3, 0, half, low_trees], q_all.at[2, 0, half, low_trees], x_up)

    def q_down(half):
        arrived(f"q{half}10h")
        send(f"q{half}20d", q_all.at[1, 0, half, high_trees], q_all.at[2, 0, half, high_trees], x_down)

    def q_cross(half, n):
        trees = low_trees if n == "u" else high_trees
        arrived(f"q{half}20{n}")
        send(f"q{half}21{n}", q_all.at[2, 0, half, trees], q_all.at[2, 1, half, trees], z_near)

    def q_z(half):
        q = f"q{half}"
        arrived(q + "01")
        send(q + "31", q_all.at[0, 1, half], q_all.at[3, 1, half], x_up)
        send(q + "11", q_all.at[0, 1, half], q_all.at[1, 1, half], x_down)


    lane = lax.broadcasted_iota(jnp.int32, (128, 128), 1)
    new_lane = lax.broadcasted_iota(jnp.int32, (128, TREES * 32), 1)
    new_row = lax.broadcasted_iota(jnp.int32, (128, TREES * 32), 0)

    def fresh_tokens(half):
        stats = jnp.zeros((128, 128), F32)
        for u in range(TREES):
            seen = (new_lane // 32 == u) & (new_lane % 16 == new_row % 16)
            seen = seen & ((new_lane % 32) // 16 <= new_row // 64)
            s = lax.dot_general(
                q_all[0, 0, half, u], key_new[half], (((1,), (1,)), ((), ())), preferred_element_type=F32
            )
            s = jnp.where(seen, s, LOW_SCORE)
            m = jnp.max(s, axis=1, keepdims=True)
            p = jnp.exp2((s - m) * EXP_SCALE).astype(BF)
            o = jnp.dot(p, value_new[half], preferred_element_type=F32)
            fresh[half, u] = o[:, 0:128].astype(BF)
            stats = jnp.where(lane == u, m, stats)
            stats = jnp.where(lane == u + 4, o[:, 128:256], stats)
        fresh_stat[half] = jnp.transpose(stats)[0:8]

    def block(half, dx, dz):
        owner = lax.rem(x + dx, 4) * 2 + (zl if dz == 0 else 1 - zl)
        if (dx, dz) != (0, 0):
            q = f"q{half}{dx}{dz}"
            arrived(*(q + n for n in ("ud" if dx == 2 else "lh" if dz == 0 else [""])))
        stats = jnp.zeros((128, 128), F32)
        for u in range(TREES):
            tree = owner * 8 + half * TREES + u
            among = (owner * 2 + core) * 8 + half * TREES + u
            numbers = [pages[b, i, among] + b * 128 for b in range(2) for i in range(8)]
            k = jnp.concatenate([keys[n] for n in numbers], axis=0)
            s = lax.dot_general(
                q_all[dx, dz, half, u], k, (((1,), (1,)), ((), ())), preferred_element_type=F32
            )
            hide = jnp.concatenate([bias[0, tree], bias[1, tree]], axis=1).astype(F32)
            s = jnp.concatenate([s[i * 16 : (i + 1) * 16] + hide for i in range(8)], axis=0)
            m = jnp.maximum(jnp.max(s, axis=1, keepdims=True), LOW_MAX)
            p = jnp.exp2((s - m) * EXP_SCALE).astype(BF)
            for i in range(16):
                vals[u, i * 64 : (i + 1) * 64, 0:128] = values[numbers[i]]
            o = jnp.dot(p, vals[u], preferred_element_type=F32)
            part[dx, dz, half, u] = o[:, 0:128].astype(BF)
            stats = jnp.where(lane == u, m, stats)
            stats = jnp.where(lane == u + 4, o[:, 128:256], stats)
        part_stat[dx, dz, half] = jnp.transpose(stats)[0:8]
        if dx == 2:
            send_part(half, 2, dz, relay.at[dz, half], relay_stat.at[dz, half], x_up if dz == 0 else x_down)
        if (dx, dz) == (1, 1):
            send_part(half, 1, 1, got.at[0, 1, half], got_stat.at[0, 1, half], x_up)
        if (dx, dz) == (3, 0):
            send_part(half, 3, 0, got.at[1, 0, half], got_stat.at[1, 0, half], x_down)

    def send_trees(name, k, src, dst, device):
        trees = low_trees if k == 0 else high_trees
        send(f"{name}{k}", src.at[trees], dst.at[trees], device)

    def send_part(half, dx, dz, to, to_stat, device):
        send(f"s{half}{dx}{dz}", part_stat.at[dx, dz, half], to_stat, device)
        for k in range(2):
            send_trees(f"o{half}{dx}{dz}", k, part.at[dx, dz, half], to, device)

    def some_trees(k):
        return range(k * TREES // 2, (k + 1) * TREES // 2)

    def c_join(half, dz, k):
        arrived(f"o{half}2{dz}{k}", f"s{half}2{dz}")
        dx, slot, device = (1, 0, x_up) if dz == 0 else (3, 1, x_down)
        outs = [part.at[dx, dz, half], relay.at[dz, half]]
        top, weights, summed = weigh([part_stat[dx, dz, half], relay_stat[dz, half]])
        columns = columns_of(weights)
        if k == 0:
            joined_stat[dz, half] = jnp.concatenate([top, summed], axis=0)
            send(f"s{half}{dx}{dz}", joined_stat.at[dz, half], got_stat.at[slot, dz, half], device)
        for u in some_trees(k):
            part[dx, dz, half, u] = mixed(columns, outs, u).astype(BF)
        send_trees(f"o{half}{dx}{dz}", k, part.at[dx, dz, half], got.at[slot, dz, half], device)

    def weigh(stats):
        tops = [s[0:4] for s in stats]
        top = tops[0]
        for other in tops[1:]:
            top = jnp.maximum(top, other)
        weights = [jnp.exp2((m - top) * EXP_SCALE) for m in tops]
        summed = jnp.zeros((4, 128), F32)
        for w, s in zip(weights, stats):
            summed = summed + w * s[4:8]
        return top, weights, summed

    def columns_of(weights):
        stacked = jnp.concatenate(weights + [jnp.zeros((128 - 4 * len(weights), 128), F32)], axis=0)
        return jnp.transpose(stacked)

    def mixed(columns, outs, u):
        o = jnp.zeros((128, 128), F32)
        for i, ref in enumerate(outs):
            o = o + columns[:, i * 4 + u : i * 4 + u + 1] * ref[u].astype(F32)
        return o

    def received(half, dz, k):
        for dx in (1, 3):
            arrived(f"s{half}{dx}{dz}", f"o{half}{dx}{dz}{k}")
        outs = [part.at[0, dz, half]] + [got.at[i, dz, half] for i in range(2)]
        return outs, [part_stat[0, dz, half]] + [got_stat[i, dz, half] for i in range(2)]

    def plane_merge(half, k):
        outs, stats = received(half, 1, k)
        top, weights, summed = weigh(stats)
        columns = columns_of(weights)
        if k == 0:
            rowed_stat[0, half] = jnp.concatenate([top, summed], axis=0)
            send(f"zs{half}", rowed_stat.at[0, half], rowed_stat.at[1, half], z_near)
        for u in some_trees(k):
            rowed[0, half, u] = mixed(columns, outs, u).astype(BF)
        send_trees(f"zo{half}", k, rowed.at[0, half], rowed.at[1, half], z_near)

    def last_merge(half, k):
        outs, stats = received(half, 0, k)
        arrived(f"zs{half}", f"zo{half}{k}")
        top, weights, summed = weigh(stats + [rowed_stat[1, half], fresh_stat[half]])
        columns = columns_of([w / summed for w in weights])
        for u in some_trees(k):
            o = mixed(columns, outs + [rowed.at[1, half], fresh.at[half]], u).astype(BF)
            for p in range(2):
                for head in range(4):
                    low, there = (p * 4 + head) * 16, p * ROWS + u * 16
                    att[half, there : there + 16, head * 128 : (head + 1) * 128] = o[low : low + 16]


    rings = {"p": (0, 0, 1), "q": (1, 0, 0), "r": (0, 1, 0)}

    def product(half, dy, dz):
        if "out" not in done:
            done.add("out")
            fetched("out")
        features = pl.ds(pl.multiple_of(in_head(dy, dz) * 1024, 1024), 1024)
        r = jnp.dot(att[half], w_out[:, features], preferred_element_type=F32).astype(BF)
        sent[half, dz, dy] = r

    def over_z(half, dy):
        send(f"z{half}{dy}", sent.at[half, 1, dy, group[1]], got_z.at[half, dy, group[1]], z_far)

    def add_z(half, dy):
        arrived(f"z{half}{dy}")
        rows = group[1]
        sent[half, 0, dy, rows] = (sent[half, 0, dy, rows].astype(F32) + got_z[half, dy, rows].astype(F32)).astype(BF)

    def ring_far(half, name):
        ring, p, dz = rings[name]
        for rows, to, n in ((ups[p], y_up, "u"), (downs[p], y_down, "d")):
            send(f"{name}f{half}{n}", sent.at[half, dz, 2, rows], got_y.at[half, ring, 0, rows], to)

    def ring_near(half, name, dy):
        ring, p, dz = rings[name]
        rows, to, n, slot = (downs[p], y_up, "u", 2) if dy == 1 else (ups[p], y_down, "d", 1)
        send(f"{name}n{half}{n}", sent.at[half, dz, dy, rows], got_y.at[half, ring, slot, rows], to)

    def d_join(half, name, dy):
        ring, p, dz = rings[name]
        rows, to, n, slot = (ups[p], y_up, "u", 2) if dy == 1 else (downs[p], y_down, "d", 1)
        arrived(f"{name}f{half}{n}")
        summed = sent[half, dz, dy, rows].astype(F32) + got_y[half, ring, 0, rows].astype(F32)
        sent[half, dz, dy, rows] = summed.astype(BF)
        send(f"{name}j{half}{n}", sent.at[half, dz, dy, rows], got_y.at[half, ring, slot, rows], to)

    def ring_end(half, name):
        ring, p, dz = rings[name]
        arrived(*[f"{name}{s}{half}{n}" for s in "nj" for n in "ud"])
        rows = group[p]
        r = sent[half, dz, 0, rows].astype(F32)
        return r + got_y[half, ring, 1, rows].astype(F32) + got_y[half, ring, 2, rows].astype(F32)

    def d_far(half, dz):
        product(half, 2, dz)
        ring_far(half, "p" if dz else "q")
        if dz:
            over_z(half, 2)

    def d_near(half, dy, dz):
        product(half, dy, dz)
        if dz:
            over_z(half, dy)
        ring_near(half, "p" if dz else "q", dy)

    def d_own(half, dz):
        product(half, 0, dz)
        if dz:
            over_z(half, 0)

    def r_far(half):
        add_z(half, 2)
        ring_far(half, "r")

    def r_near(half, dy):
        add_z(half, dy)
        ring_near(half, "r", dy)

    def d_cross(half):
        sent[half, 1, 0, group[0]] = ring_end(half, "p").astype(BF)
        send(f"y{half}", sent.at[half, 1, 0, group[0]], got_z.at[half, 0, group[0]], z_far)

    def d_end(half, p):
        low = half * ROWS
        if p == 0:
            first = ring_end(half, "q")
            arrived(f"y{half}")
            first = (first + got_z[half, 0, group[0]].astype(F32)).astype(BF)
            out[0, low : low + ROWS] = first[0:ROWS]
            out[1, low : low + FIRST - ROWS] = first[ROWS:FIRST]
        else:
            add_z(half, 0)
            out[1, low + FIRST - ROWS : low + ROWS] = ring_end(half, "r").astype(BF)


    def exchange_start():
        send("pages", pages_in, pages_away, twin)
        send("keys", key_hbm, keys.at[pl.ds(128, 128)], twin)
        send("values", value_hbm, values.at[pl.ds(128, 128)], twin)

    def squares_start():
        for half in range(CHUNKS):
            if ("own", half) not in done:
                done.add(("own", half))
                fetched(("own", half, 0), ("own", half, 1))
        fetched("gain")
        for i in range(64):
            gain[i // 8, :, i % 8 * 128 : i % 8 * 128 + 128] = gain_in[i : i + 1].astype(F32)
        for p in range(2):
            rows = slice(p * ROWS, (p + 1) * ROWS)
            wide = jnp.concatenate([held[half, 0, 0, rows] for half in range(CHUNKS)], axis=0).astype(F32)
            squares = jnp.sum(wide * wide, axis=-1, keepdims=True)
            sums[0, 0, pl.ds(p, 1)] = jnp.transpose(jnp.broadcast_to(squares, (128, 128)))[0:1]
        for dy, dz in SPOTS[1:]:
            send(f"t{dy}{dz}", sums.at[0, 0], sums.at[(4 - dy) % 4, dz], (c, in_head(dy, dz)))

    def squares_end():
        arrived(*[f"t{dy}{dz}" for dy, dz in SPOTS[1:]])
        for p in range(2):
            s = sums[0, 0, pl.ds(p, 1)]
            for dy, dz in SPOTS[1:]:
                s = s + sums[dy, dz, pl.ds(p, 1)]
            s = jnp.transpose(jnp.broadcast_to(lax.rsqrt(s * (1.0 / 8192) + EPSILON), (128, 128)))
            for half in range(CHUNKS):
                scale[half, p * ROWS : (p + 1) * ROWS] = s[half * ROWS : (half + 1) * ROWS]

    def visibility():
        slot_row = lax.broadcasted_iota(jnp.int32, (128, 512), 0)
        slot_lane = lax.broadcasted_iota(jnp.int32, (128, 512), 1) // 64
        spread = jnp.where(slot_row == slot_lane, 1.0, 0.0).astype(BF)
        fetched("fill")
        fetched("depth")
        fills_t = jnp.concatenate([fill[...].astype(F32), jnp.zeros((120, 128), F32)], axis=0)
        filled[...] = jnp.dot(jnp.transpose(fills_t).astype(BF), spread, preferred_element_type=F32)
        column = lax.broadcasted_iota(jnp.int32, (16, 512), 1)
        slot_of, token_of = (column // 64).astype(F32), (column % 64).astype(F32)

        def group(target, j, e):
            depth_row = depth[:, pl.ds(pl.multiple_of(e * 128, 128), 128)].astype(F32)
            depths = jnp.transpose(jnp.broadcast_to(depth_row, (128, 128)))
            fills = filled[pl.ds(pl.multiple_of(e * 8, 8), 8)]
            for t in range(8):
                d = jnp.concatenate([depths[t * 16 : t * 16 + 16]] * 4, axis=1)
                visible = (slot_of < d) & (token_of < fills[t : t + 1])
                target[j * 8 + t] = jnp.where(visible, 0.0, LOW_SCORE).astype(BF)

        def away(j, _):
            group(bias_away, j, j * 2 + 1 - core)
            return 0

        def here(j, _):
            group(bias.at[0], j, j * 2 + core)
            return 0

        lax.fori_loop(0, 8, away, 0)
        send("bias", bias_away, bias.at[1], twin)
        lax.fori_loop(0, 8, here, 0)
        fetched("lengths", "frequency")
        spots = jnp.transpose(jnp.broadcast_to(lengths[...].astype(F32), (128, 128)))[:, 0:64]
        for p in range(2):
            angles = (spots + float(p)) * frequency[...]
            cosine[p] = jnp.cos(angles)
            sine[p] = jnp.sin(angles)

    def exchange_end():
        arrived("pages")
        load("pages_away", pages_away, pages.at[1])
        for u in range(TREES):
            vals[u, :, 128:256] = jnp.ones((1024, 128), BF)
        for half in range(CHUNKS):
            value_new[half, :, 128:256] = jnp.ones((TREES * 32, 128), BF)
        fetched("pages", "pages_away", "keys", "values")
        arrived("keys", "values", "bias")

    g_start(1, 1)
    squares_start()
    exchange_start()
    g_start(1, 0)
    g_start(0, 1)
    visibility()
    g_down(1, 1, 0)
    g_up(1, 1, 0)
    g_z(1)
    squares_end()
    multiply(1, 0, 0)
    multiply(1, 1, 0)
    multiply(0, 0, 0)
    g_up(1, 0, 0)
    g_far(1, "d")
    g_far(1, "u")
    g_down(1, 0, 0)
    multiply(1, 0, 1)
    g_up(1, 0, 1)
    g_down(1, 0, 1)
    g_start(0, 0)
    g_up(0, 1, 0)
    exchange_end()
    multiply(1, 3, 1)
    multiply(1, 1, 1)
    multiply(1, 3, 0)
    multiply(1, 2, 0)
    multiply(1, 2, 1)
    project_end(1)
    g_down(0, 1, 0)
    fresh_tokens(1)
    g_z(0)
    block(1, 0, 0)
    multiply(0, 0, 1)
    g_far(0, "u")
    g_up(0, 0, 0)
    q_up(1)
    q_down(1)
    g_far(0, "d")
    g_down(0, 0, 0)
    multiply(0, 1, 0)
    multiply(0, 3, 0)
    block(1, 3, 0)
    g_up(0, 0, 1)
    q_z(1)
    q_cross(1, "u")
    g_down(0, 0, 1)
    multiply(0, 3, 1)
    q_cross(1, "d")
    multiply(0, 1, 1)
    block(1, 2, 0)
    multiply(0, 2, 0)
    block(1, 0, 1)
    multiply(0, 2, 1)
    project_end(0)
    block(1, 2, 1)
    block(1, 3, 1)
    block(1, 1, 0)
    q_up(0)
    q_down(0)
    block(1, 1, 1)
    c_join(1, 0, 0)
    c_join(1, 0, 1)
    c_join(1, 1, 0)
    block(0, 0, 1)
    q_cross(0, "u")
    c_join(1, 1, 1)
    q_z(0)
    q_cross(0, "d")
    block(0, 2, 0)
    plane_merge(1, 0)
    block(0, 1, 0)
    plane_merge(1, 1)
    fresh_tokens(0)
    block(0, 2, 1)
    last_merge(1, 0)
    block(0, 1, 1)
    last_merge(1, 1)
    d_far(1, 1)
    d_far(1, 0)
    d_near(1, 3, 1)
    block(0, 3, 1)
    c_join(0, 1, 0)
    c_join(0, 0, 0)
    d_near(1, 1, 1)
    c_join(0, 1, 1)
    d_join(1, "p", 3)
    d_near(1, 1, 0)
    block(0, 3, 0)
    d_join(1, "p", 1)
    r_far(1)
    d_near(1, 3, 0)
    d_join(1, "q", 3)
    plane_merge(0, 0)
    d_join(1, "q", 1)
    c_join(0, 0, 1)
    plane_merge(0, 1)
    block(0, 0, 0)
    d_own(1, 1)
    r_near(1, 1)
    d_own(1, 0)
    r_near(1, 3)
    d_join(1, "r", 3)
    last_merge(0, 0)
    d_cross(1)
    d_join(1, "r", 1)
    last_merge(0, 1)
    d_own(0, 0)
    d_far(0, 1)
    d_far(0, 0)
    d_near(0, 1, 1)
    d_end(1, 1)
    d_near(0, 3, 1)
    d_join(0, "p", 3)
    d_end(1, 0)
    d_own(0, 1)
    d_join(0, "p", 1)
    r_far(0)
    d_near(0, 3, 0)
    d_join(0, "q", 3)
    d_near(0, 1, 0)
    r_near(0, 1)
    d_cross(0)
    d_join(0, "r", 1)
    d_join(0, "q", 1)
    r_near(0, 3)
    d_join(0, "r", 3)
    d_end(0, 1)
    d_end(0, 0)
    for copy in made.values():
        copy.wait_send()


def call(*operands):
    vm = pl.BlockSpec(memory_space=pltpu.VMEM)
    anywhere = pl.BlockSpec(memory_space=pl.ANY)
    n, r = CHUNKS, ROWS
    trees, tile = (n, TREES, 128, 128), (8, 128)
    stat = (n,) + tile
    shapes = [
        ((64, 128), BF), ((8, 1, 1024), F32), ((1, 128), jnp.int32), ((1, 64), F32), ((2, 128, 64), F32), ((2, 128, 64), F32),
        (tile, jnp.int32), ((1, 2048), jnp.int32),
        ((n, 4, 2, 2 * r, 1024), BF), ((4, 2) + tile, F32), ((n, 2 * r, 128), F32), ((8, 1024, 768), BF),
        ((n, 2 * r, 768), F32), ((512, 8192), BF), ((256, 64, 128), BF), ((256, 64, 128), BF), ((128, 512), F32),
        ((2, 64, 16, 512), BF), ((64, 16, 512), BF), (tile, jnp.int32), None,
        ((4, 2) + trees, BF), ((n, TREES * 32, 128), BF), ((n, TREES * 32, 256), BF),
        ((4, 2) + trees, BF), ((4, 2) + stat, F32), ((2, 2) + trees, BF), ((2, 2) + stat, F32),
        ((2,) + trees, BF), ((2,) + stat, F32), ((2,) + stat, F32), ((2,) + trees, BF), ((2,) + stat, F32),
        (trees, BF), (stat, F32),
        ((TREES, 1024, 256), BF), ((n, 2 * r, 512), BF), ((n, 2, 4, 2 * r, 1024), BF),
        ((n, 2, 3, 2 * r, 1024), BF), ((n, 4, 2 * r, 1024), BF),
    ]
    scratch = [pltpu.VMEM(*s) if s else pltpu.SMEM((2, 8, 128), jnp.int32) for s in shapes]
    return pl.pallas_call(
        kernel,
        out_shape=jax.ShapeDtypeStruct((2, 128, 1024), BF),
        in_specs=[anywhere] * 13,
        out_specs=vm,
        scratch_shapes=scratch
        + [pltpu.SemaphoreType.DMA((196,)), pltpu.SemaphoreType.DMA((196,)), pltpu.SemaphoreType.DMA((40,))],
        compiler_params=pltpu.CompilerParams(
            collective_id=1, has_side_effects=True, vmem_limit_bytes=60 * 2**20
        ),
        cost_estimate=pl.CostEstimate(flops=15 * 10**9, bytes_accessed=30 * 2**20, transcendentals=10**7),
    )(*operands)


def body(
    hidden,
    norm_gain,
    w_query,
    key_weight,
    value_weight,
    w_out,
    key_cache,
    value_cache,
    tree_pages,
    page_fill,
    row_depth,
    row_length,
):
    ladder = np.arange(64, dtype=np.float32) * np.float32(2.0 / 128)
    frequency = jnp.asarray(np.power(np.float32(ROPE_BASE), -ladder)[None, :])
    pages, fill = jnp.transpose(tree_pages[0]), jnp.transpose(page_fill[0])
    return call(
        hidden, norm_gain.reshape(64, 128), row_length[None, :], frequency, pages, fill, row_depth, w_query, key_weight, value_weight, w_out,
        key_cache.reshape(128, 64, 128), value_cache.reshape(128, 64, 128),
    )


def solution(mesh):
    in_specs = (
        P(None, "cache", "head"),
        P(),
        P(None, "head"),
        P(None, "head"),
        P(None, "head"),
        P("head", None),
        P("cache", None, "head", None),
        P("cache", None, "head", None),
        P("cache", None, None),
        P("cache", None, None),
        P("cache", None),
        P("cache"),
    )
    out_specs = P(None, "cache", "head")
    return jax.shard_map(body, mesh=mesh, in_specs=in_specs, out_specs=out_specs, check_vma=False)
```

```python
import math

import jax
import jax.numpy as jnp
import numpy as np
from jax import lax
from jax.experimental import pallas as pl
from jax.experimental.pallas import tpu as pltpu
from jax.sharding import PartitionSpec as P

MESH = pl.DeviceIdType.MESH
ROPE_BASE = 500000.0
EPSILON = 1e-05
LOW_SCORE = -1e30
LOW_MAX = -1e29
EXP_SCALE = math.log2(math.e) / math.sqrt(128.0)
BF, F32 = jnp.bfloat16, jnp.float32
CHUNKS = 2
ROWS = 128 // CHUNKS
TREES = 8 // CHUNKS
FIRST = 80
SPOTS = [(dy, dz) for dy in range(4) for dz in range(2)]
ORDER = [(0, 0), (1, 0), (3, 0), (0, 1), (2, 0), (1, 1), (3, 1), (2, 1)]


def kernel(
    hidden_hbm, gain_hbm, lengths_hbm, frequency_hbm, pages_in, fill_hbm, depth_hbm, w_query, key_weight, value_weight,
    w_out_hbm, key_hbm, value_hbm,
    out,
    gain_in, gain, lengths, frequency, cosine, sine, fill, depth,
    held, sums, scale, weight, total, w_out, keys, values, filled, bias, bias_away, pages_away, pages,
    q_all, key_new, value_new, part, part_stat, got, got_stat, relay, relay_stat, joined_stat, rowed, rowed_stat, fresh, fresh_stat,
    vals, att, sent, got_y, got_z,
    send_sem, recv_sem, load_sem,
):
    c, h = lax.axis_index("cache"), lax.axis_index("head")
    x, zl, core = c // 4, lax.rem(c // 2, 2), lax.rem(c, 2)
    y, zh = h // 2, lax.rem(h, 2)

    def in_head(dy, dz):
        return lax.rem(y + dy, 4) * 2 + (zh if dz == 0 else 1 - zh)

    def in_cache(dx, dz):
        return lax.rem(x + dx, 4) * 4 + (zl if dz == 0 else 1 - zl) * 2 + core

    y_up, y_down, z_far = (c, in_head(1, 0)), (c, in_head(3, 0)), (c, in_head(0, 1))
    x_up, x_down, z_near = (in_cache(1, 0), h), (in_cache(3, 0), h), (in_cache(0, 1), h)
    twin = (c + 1 - 2 * core, h)

    barrier = pltpu.get_barrier_semaphore()
    others = [(c, in_head(*spot)) for spot in SPOTS[1:]] + [x_up, x_down, z_near, twin]
    for device in others:
        pl.semaphore_signal(barrier, inc=1, device_id=device, device_id_type=MESH)

    loads = {}

    def load(name, src, dst):
        loads[name] = pltpu.make_async_copy(src, dst, load_sem.at[len(loads)])
        loads[name].start()

    def fetched(*names):
        for name in names:
            loads[name].wait()

    for half in range(CHUNKS):
        for p in range(2):
            rows = pl.ds(half * ROWS, ROWS)
            load(("own", half, p), hidden_hbm.at[p, rows], held.at[half, 0, 0, pl.ds(p * ROWS, ROWS)])
    load("gain", gain_hbm, gain_in)
    load("pages", pages_in, pages.at[0])
    load("fill", fill_hbm, fill)
    load("depth", depth_hbm, depth)
    load("lengths", lengths_hbm, lengths)
    load("frequency", frequency_hbm, frequency)

    def start_loads():
        for number, spot in enumerate(ORDER):
            rows = pl.ds(pl.multiple_of(in_head(*spot) * 1024, 1024), 1024)
            load(("q", number), w_query.at[rows], weight.at[number, :, pl.ds(0, 512)])
            load(("k", number), key_weight.at[rows], weight.at[number, :, pl.ds(512, 128)])
            load(("v", number), value_weight.at[rows], weight.at[number, :, pl.ds(640, 128)])
        load("keys", key_hbm, keys.at[pl.ds(0, 128)])
        load("values", value_hbm, values.at[pl.ds(0, 128)])
        load("out", w_out_hbm, w_out)

    pl.semaphore_wait(barrier, len(others))

    made = {}
    done = set()

    def send(name, src, dst, device):
        number = len(made)
        made[name] = pltpu.make_async_remote_copy(
            src_ref=src, dst_ref=dst, send_sem=send_sem.at[number], recv_sem=recv_sem.at[number],
            device_id=device, device_id_type=MESH,
        )
        made[name].start()

    def arrived(*names):
        for name in names:
            if name not in done:
                done.add(name)
                made[name].wait_recv()


    group = (pl.ds(0, FIRST), pl.ds(FIRST, 2 * ROWS - FIRST))
    ups = (pl.ds(0, 48), pl.ds(80, 16))
    downs = (pl.ds(48, 32), pl.ds(96, 32))

    def g_start(half, p):
        if ("own", half) not in done:
            done.add(("own", half))
            fetched(("own", half, 0), ("own", half, 1))
        for name, to, dy, dz in (("01", z_far, 0, 1), ("30", y_up, 3, 0), ("10", y_down, 1, 0)):
            send(f"a{half}{p}{name}", held.at[half, 0, 0, group[p]], held.at[half, dy, dz, group[p]], to)

    def g_z(half):
        arrived(f"a{half}001")
        send(f"a{half}031", held.at[half, 0, 1, group[0]], held.at[half, 3, 1, group[0]], y_up)
        send(f"a{half}011", held.at[half, 0, 1, group[0]], held.at[half, 1, 1, group[0]], y_down)

    def g_up(half, p, dz):
        a = f"a{half}{p}"
        arrived(f"{a}3{dz}")
        if p == 1:
            send(f"a{half}131", held.at[half, 3, 0, group[1]], held.at[half, 3, 1, group[1]], z_far)
        send(f"{a}2{dz}u", held.at[half, 3, dz, ups[p]], held.at[half, 2, dz, ups[p]], y_up)

    def g_down(half, p, dz):
        a = f"a{half}{p}"
        arrived(f"{a}1{dz}")
        if p == 1:
            send(f"a{half}111", held.at[half, 1, 0, group[1]], held.at[half, 1, 1, group[1]], z_far)
        send(f"{a}2{dz}d", held.at[half, 1, dz, downs[p]], held.at[half, 2, dz, downs[p]], y_down)

    def g_far(half, n):
        rows = ups[1] if n == "u" else downs[1]
        arrived(f"a{half}120{n}")
        send(f"a{half}121{n}", held.at[half, 2, 0, rows], held.at[half, 2, 1, rows], z_far)

    ready = set()

    def multiply(half, dy, dz):
        number = ORDER.index((dy, dz))
        if number not in ready:
            for array in "qkv":
                fetched((array, number))
            ready.add(number)
        if (dy, dz) != (0, 0):
            for p in range(2):
                a = f"a{half}{p}{dy}{dz}"
                arrived(*([a + "u", a + "d"] if dy == 2 else [a]))
        block = held[half, dy, dz]
        normed = block.astype(F32) * scale[half][:, 0:1] * gain[in_head(dy, dz)]
        product = jnp.dot(normed.astype(BF), weight[number], preferred_element_type=F32)
        if (dy, dz) == (0, 0):
            total[half] = product
        else:
            total[half] += product

    low_trees, high_trees = pl.ds(0, TREES // 2), pl.ds(TREES // 2, TREES // 2)

    def project_end(half):
        rows = pl.ds(half * ROWS, ROWS)
        cos = jnp.concatenate([cosine[0, rows], cosine[1, rows]], axis=0)
        sin = jnp.concatenate([sine[0, rows], sine[1, rows]], axis=0)
        cos, sin = jnp.concatenate([cos, cos], axis=1), jnp.concatenate([-sin, sin], axis=1)

        def turned(u):
            return (u * cos + pltpu.roll(u, 64, 1) * sin).astype(BF)

        k = turned(total[half, :, 512:640])
        v = total[half, :, 640:768].astype(BF)
        for head in range(4):
            q = turned(total[half, :, head * 128 : (head + 1) * 128])
            for p in range(2):
                for u in range(TREES):
                    low = (p * 4 + head) * 16
                    q_all[0, 0, half, u, low : low + 16] = q[p * ROWS + u * 16 : p * ROWS + u * 16 + 16]
        for p in range(2):
            for u in range(TREES):
                low, there = p * ROWS + u * 16, u * 32 + p * 16
                key_new[half, there : there + 16] = k[low : low + 16]
                value_new[half, there : there + 16, 0:128] = v[low : low + 16]
        name = f"q{half}"
        for first, there, trees, device in (
            ("30l", 3, low_trees, x_up), ("10h", 1, high_trees, x_down),
            ("30h", 3, high_trees, x_up), ("10l", 1, low_trees, x_down),
        ):
            send(name + first, q_all.at[0, 0, half, trees], q_all.at[there, 0, half, trees], device)
        send(name + "01", q_all.at[0, 0, half], q_all.at[0, 1, half], z_near)


    def q_up(half):
        arrived(f"q{half}30l")
        send(f"q{half}20u", q_all.at[3, 0, half, low_trees], q_all.at[2, 0, half, low_trees], x_up)

    def q_down(half):
        arrived(f"q{half}10h")
        send(f"q{half}20d", q_all.at[1, 0, half, high_trees], q_all.at[2, 0, half, high_trees], x_down)

    def q_cross(half, n):
        trees = low_trees if n == "u" else high_trees
        arrived(f"q{half}20{n}")
        send(f"q{half}21{n}", q_all.at[2, 0, half, trees], q_all.at[2, 1, half, trees], z_near)

    def q_z(half):
        q = f"q{half}"
        arrived(q + "01")
        send(q + "31", q_all.at[0, 1, half], q_all.at[3, 1, half], x_up)
        send(q + "11", q_all.at[0, 1, half], q_all.at[1, 1, half], x_down)


    lane = lax.broadcasted_iota(jnp.int32, (128, 128), 1)
    new_lane = lax.broadcasted_iota(jnp.int32, (128, TREES * 32), 1)
    new_row = lax.broadcasted_iota(jnp.int32, (128, TREES * 32), 0)

    def fresh_tokens(half):
        stats = jnp.zeros((128, 128), F32)
        for u in range(TREES):
            seen = (new_lane // 32 == u) & (new_lane % 16 == new_row % 16)
            seen = seen & ((new_lane % 32) // 16 <= new_row // 64)
            s = lax.dot_general(
                q_all[0, 0, half, u], key_new[half], (((1,), (1,)), ((), ())), preferred_element_type=F32
            )
            s = jnp.where(seen, s, LOW_SCORE)
            m = jnp.max(s, axis=1, keepdims=True)
            p = jnp.exp2((s - m) * EXP_SCALE).astype(BF)
            o = jnp.dot(p, value_new[half], preferred_element_type=F32)
            fresh[half, u] = o[:, 0:128].astype(BF)
            stats = jnp.where(lane == u, m, stats)
            stats = jnp.where(lane == u + 4, o[:, 128:256], stats)
        fresh_stat[half] = jnp.transpose(stats)[0:8]

    def block(half, dx, dz):
        owner = lax.rem(x + dx, 4) * 2 + (zl if dz == 0 else 1 - zl)
        if (dx, dz) != (0, 0):
            q = f"q{half}{dx}{dz}"
            arrived(*(q + n for n in ("ud" if dx == 2 else "lh" if dz == 0 else [""])))
        stats = jnp.zeros((128, 128), F32)
        for u in range(TREES):
            tree = owner * 8 + half * TREES + u
            among = (owner * 2 + core) * 8 + half * TREES + u
            numbers = [pages[b, i, among] + b * 128 for b in range(2) for i in range(8)]
            k = jnp.concatenate([keys[n] for n in numbers], axis=0)
            s = lax.dot_general(
                q_all[dx, dz, half, u], k, (((1,), (1,)), ((), ())), preferred_element_type=F32
            )
            hide = jnp.concatenate([bias[0, tree], bias[1, tree]], axis=1).astype(F32)
            s = jnp.concatenate([s[i * 16 : (i + 1) * 16] + hide for i in range(8)], axis=0)
            m = jnp.maximum(jnp.max(s, axis=1, keepdims=True), LOW_MAX)
            p = jnp.exp2((s - m) * EXP_SCALE).astype(BF)
            for i in range(16):
                vals[u, i * 64 : (i + 1) * 64, 0:128] = values[numbers[i]]
            o = jnp.dot(p, vals[u], preferred_element_type=F32)
            part[dx, dz, half, u] = o[:, 0:128].astype(BF)
            stats = jnp.where(lane == u, m, stats)
            stats = jnp.where(lane == u + 4, o[:, 128:256], stats)
        part_stat[dx, dz, half] = jnp.transpose(stats)[0:8]
        if dx == 2:
            send_part(half, 2, dz, relay.at[dz, half], relay_stat.at[dz, half], x_up if dz == 0 else x_down)
        if (dx, dz) == (1, 1):
            send_part(half, 1, 1, got.at[0, 1, half], got_stat.at[0, 1, half], x_up)
        if (dx, dz) == (3, 0):
            send_part(half, 3, 0, got.at[1, 0, half], got_stat.at[1, 0, half], x_down)

    def send_trees(name, k, src, dst, device):
        trees = low_trees if k == 0 else high_trees
        send(f"{name}{k}", src.at[trees], dst.at[trees], device)

    def send_part(half, dx, dz, to, to_stat, device):
        send(f"s{half}{dx}{dz}", part_stat.at[dx, dz, half], to_stat, device)
        for k in range(2):
            send_trees(f"o{half}{dx}{dz}", k, part.at[dx, dz, half], to, device)

    def some_trees(k):
        return range(k * TREES // 2, (k + 1) * TREES // 2)

    def c_join(half, dz, k):
        arrived(f"o{half}2{dz}{k}", f"s{half}2{dz}")
        dx, slot, device = (1, 0, x_up) if dz == 0 else (3, 1, x_down)
        outs = [part.at[dx, dz, half], relay.at[dz, half]]
        top, weights, summed = weigh([part_stat[dx, dz, half], relay_stat[dz, half]])
        columns = columns_of(weights)
        if k == 0:
            joined_stat[dz, half] = jnp.concatenate([top, summed], axis=0)
            send(f"s{half}{dx}{dz}", joined_stat.at[dz, half], got_stat.at[slot, dz, half], device)
        for u in some_trees(k):
            part[dx, dz, half, u] = mixed(columns, outs, u).astype(BF)
        send_trees(f"o{half}{dx}{dz}", k, part.at[dx, dz, half], got.at[slot, dz, half], device)

    def weigh(stats):
        tops = [s[0:4] for s in stats]
        top = tops[0]
        for other in tops[1:]:
            top = jnp.maximum(top, other)
        weights = [jnp.exp2((m - top) * EXP_SCALE) for m in tops]
        summed = jnp.zeros((4, 128), F32)
        for w, s in zip(weights, stats):
            summed = summed + w * s[4:8]
        return top, weights, summed

    def columns_of(weights):
        stacked = jnp.concatenate(weights + [jnp.zeros((128 - 4 * len(weights), 128), F32)], axis=0)
        return jnp.transpose(stacked)

    def mixed(columns, outs, u):
        o = jnp.zeros((128, 128), F32)
        for i, ref in enumerate(outs):
            o = o + columns[:, i * 4 + u : i * 4 + u + 1] * ref[u].astype(F32)
        return o

    def received(half, dz, k):
        for dx in (1, 3):
            arrived(f"s{half}{dx}{dz}", f"o{half}{dx}{dz}{k}")
        outs = [part.at[0, dz, half]] + [got.at[i, dz, half] for i in range(2)]
        return outs, [part_stat[0, dz, half]] + [got_stat[i, dz, half] for i in range(2)]

    def plane_merge(half, k):
        outs, stats = received(half, 1, k)
        top, weights, summed = weigh(stats)
        columns = columns_of(weights)
        if k == 0:
            rowed_stat[0, half] = jnp.concatenate([top, summed], axis=0)
            send(f"zs{half}", rowed_stat.at[0, half], rowed_stat.at[1, half], z_near)
        for u in some_trees(k):
            rowed[0, half, u] = mixed(columns, outs, u).astype(BF)
        send_trees(f"zo{half}", k, rowed.at[0, half], rowed.at[1, half], z_near)

    def last_merge(half, k):
        outs, stats = received(half, 0, k)
        arrived(f"zs{half}", f"zo{half}{k}")
        top, weights, summed = weigh(stats + [rowed_stat[1, half], fresh_stat[half]])
        columns = columns_of([w / summed for w in weights])
        for u in some_trees(k):
            o = mixed(columns, outs + [rowed.at[1, half], fresh.at[half]], u).astype(BF)
            for p in range(2):
                for head in range(4):
                    low, there = (p * 4 + head) * 16, p * ROWS + u * 16
                    att[half, there : there + 16, head * 128 : (head + 1) * 128] = o[low : low + 16]


    rings = {"p": (0, 0, 1), "q": (1, 0, 0), "r": (0, 1, 0)}

    def product(half, dy, dz):
        if "out" not in done:
            done.add("out")
            fetched("out")
        features = pl.ds(pl.multiple_of(in_head(dy, dz) * 1024, 1024), 1024)
        r = jnp.dot(att[half], w_out[:, features], preferred_element_type=F32).astype(BF)
        sent[half, dz, dy] = r

    def over_z(half, dy):
        send(f"z{half}{dy}", sent.at[half, 1, dy, group[1]], got_z.at[half, dy, group[1]], z_far)

    def add_z(half, dy):
        arrived(f"z{half}{dy}")
        rows = group[1]
        sent[half, 0, dy, rows] = (sent[half, 0, dy, rows].astype(F32) + got_z[half, dy, rows].astype(F32)).astype(BF)

    def ring_far(half, name):
        ring, p, dz = rings[name]
        for rows, to, n in ((ups[p], y_up, "u"), (downs[p], y_down, "d")):
            send(f"{name}f{half}{n}", sent.at[half, dz, 2, rows], got_y.at[half, ring, 0, rows], to)

    def ring_near(half, name, dy):
        ring, p, dz = rings[name]
        rows, to, n, slot = (downs[p], y_up, "u", 2) if dy == 1 else (ups[p], y_down, "d", 1)
        send(f"{name}n{half}{n}", sent.at[half, dz, dy, rows], got_y.at[half, ring, slot, rows], to)

    def d_join(half, name, dy):
        ring, p, dz = rings[name]
        rows, to, n, slot = (ups[p], y_up, "u", 2) if dy == 1 else (downs[p], y_down, "d", 1)
        arrived(f"{name}f{half}{n}")
        summed = sent[half, dz, dy, rows].astype(F32) + got_y[half, ring, 0, rows].astype(F32)
        sent[half, dz, dy, rows] = summed.astype(BF)
        send(f"{name}j{half}{n}", sent.at[half, dz, dy, rows], got_y.at[half, ring, slot, rows], to)

    def ring_end(half, name):
        ring, p, dz = rings[name]
        arrived(*[f"{name}{s}{half}{n}" for s in "nj" for n in "ud"])
        rows = group[p]
        r = sent[half, dz, 0, rows].astype(F32)
        return r + got_y[half, ring, 1, rows].astype(F32) + got_y[half, ring, 2, rows].astype(F32)

    def d_far(half, dz):
        product(half, 2, dz)
        ring_far(half, "p" if dz else "q")
        if dz:
            over_z(half, 2)

    def d_near(half, dy, dz):
        product(half, dy, dz)
        if dz:
            over_z(half, dy)
        ring_near(half, "p" if dz else "q", dy)

    def d_own(half, dz):
        product(half, 0, dz)
        if dz:
            over_z(half, 0)

    def r_far(half):
        add_z(half, 2)
        ring_far(half, "r")

    def r_near(half, dy):
        add_z(half, dy)
        ring_near(half, "r", dy)

    def d_cross(half):
        sent[half, 1, 0, group[0]] = ring_end(half, "p").astype(BF)
        send(f"y{half}", sent.at[half, 1, 0, group[0]], got_z.at[half, 0, group[0]], z_far)

    def d_end(half, p):
        low = half * ROWS
        if p == 0:
            first = ring_end(half, "q")
            arrived(f"y{half}")
            first = (first + got_z[half, 0, group[0]].astype(F32)).astype(BF)
            out[0, low : low + ROWS] = first[0:ROWS]
            out[1, low : low + FIRST - ROWS] = first[ROWS:FIRST]
        else:
            add_z(half, 0)
            out[1, low + FIRST - ROWS : low + ROWS] = ring_end(half, "r").astype(BF)


    def exchange_start():
        send("pages", pages_in, pages_away, twin)
        send("keys", key_hbm, keys.at[pl.ds(128, 128)], twin)
        send("values", value_hbm, values.at[pl.ds(128, 128)], twin)

    def squares_start():
        for half in range(CHUNKS):
            if ("own", half) not in done:
                done.add(("own", half))
                fetched(("own", half, 0), ("own", half, 1))
        fetched("gain")
        for i in range(64):
            gain[i // 8, :, i % 8 * 128 : i % 8 * 128 + 128] = gain_in[i : i + 1].astype(F32)
        for p in range(2):
            rows = slice(p * ROWS, (p + 1) * ROWS)
            wide = jnp.concatenate([held[half, 0, 0, rows] for half in range(CHUNKS)], axis=0).astype(F32)
            squares = jnp.sum(wide * wide, axis=-1, keepdims=True)
            sums[0, 0, pl.ds(p, 1)] = jnp.transpose(jnp.broadcast_to(squares, (128, 128)))[0:1]
        for dy, dz in SPOTS[1:]:
            send(f"t{dy}{dz}", sums.at[0, 0], sums.at[(4 - dy) % 4, dz], (c, in_head(dy, dz)))

    def squares_end():
        arrived(*[f"t{dy}{dz}" for dy, dz in SPOTS[1:]])
        for p in range(2):
            s = sums[0, 0, pl.ds(p, 1)]
            for dy, dz in SPOTS[1:]:
                s = s + sums[dy, dz, pl.ds(p, 1)]
            s = jnp.transpose(jnp.broadcast_to(lax.rsqrt(s * (1.0 / 8192) + EPSILON), (128, 128)))
            for half in range(CHUNKS):
                scale[half, p * ROWS : (p + 1) * ROWS] = s[half * ROWS : (half + 1) * ROWS]

    def visibility():
        slot_row = lax.broadcasted_iota(jnp.int32, (128, 512), 0)
        slot_lane = lax.broadcasted_iota(jnp.int32, (128, 512), 1) // 64
        spread = jnp.where(slot_row == slot_lane, 1.0, 0.0).astype(BF)
        fetched("fill")
        fetched("depth")
        fills_t = jnp.concatenate([fill[...].astype(F32), jnp.zeros((120, 128), F32)], axis=0)
        filled[...] = jnp.dot(jnp.transpose(fills_t).astype(BF), spread, preferred_element_type=F32)
        column = lax.broadcasted_iota(jnp.int32, (16, 512), 1)
        slot_of, token_of = (column // 64).astype(F32), (column % 64).astype(F32)

        def group(target, j, e):
            depth_row = depth[:, pl.ds(pl.multiple_of(e * 128, 128), 128)].astype(F32)
            depths = jnp.transpose(jnp.broadcast_to(depth_row, (128, 128)))
            fills = filled[pl.ds(pl.multiple_of(e * 8, 8), 8)]
            for t in range(8):
                d = jnp.concatenate([depths[t * 16 : t * 16 + 16]] * 4, axis=1)
                visible = (slot_of < d) & (token_of < fills[t : t + 1])
                target[j * 8 + t] = jnp.where(visible, 0.0, LOW_SCORE).astype(BF)

        def away(j, _):
            group(bias_away, j, j * 2 + 1 - core)
            return 0

        def here(j, _):
            group(bias.at[0], j, j * 2 + core)
            return 0

        lax.fori_loop(0, 8, away, 0)
        send("bias", bias_away, bias.at[1], twin)
        lax.fori_loop(0, 8, here, 0)
        fetched("lengths", "frequency")
        spots = jnp.transpose(jnp.broadcast_to(lengths[...].astype(F32), (128, 128)))[:, 0:64]
        for p in range(2):
            angles = (spots + float(p)) * frequency[...]
            cosine[p] = jnp.cos(angles)
            sine[p] = jnp.sin(angles)

    def exchange_end():
        arrived("pages")
        load("pages_away", pages_away, pages.at[1])
        for u in range(TREES):
            vals[u, :, 128:256] = jnp.ones((1024, 128), BF)
        for half in range(CHUNKS):
            value_new[half, :, 128:256] = jnp.ones((TREES * 32, 128), BF)
        fetched("pages", "pages_away", "keys", "values")
        arrived("keys", "values", "bias")

    g_start(1, 1)
    squares_start()
    exchange_start()
    g_start(1, 0)
    start_loads()
    g_start(0, 1)
    visibility()
    g_down(1, 1, 0)
    g_up(1, 1, 0)
    g_z(1)
    squares_end()
    multiply(1, 0, 0)
    multiply(1, 1, 0)
    multiply(0, 0, 0)
    g_up(1, 0, 0)
    g_far(1, "d")
    g_far(1, "u")
    g_down(1, 0, 0)
    multiply(1, 0, 1)
    g_up(1, 0, 1)
    g_down(1, 0, 1)
    g_start(0, 0)
    g_up(0, 1, 0)
    exchange_end()
    multiply(1, 3, 1)
    multiply(1, 1, 1)
    multiply(1, 3, 0)
    multiply(1, 2, 0)
    multiply(1, 2, 1)
    project_end(1)
    g_down(0, 1, 0)
    fresh_tokens(1)
    g_z(0)
    block(1, 0, 0)
    multiply(0, 0, 1)
    g_far(0, "u")
    g_up(0, 0, 0)
    q_up(1)
    q_down(1)
    g_far(0, "d")
    g_down(0, 0, 0)
    multiply(0, 1, 0)
    multiply(0, 3, 0)
    block(1, 3, 0)
    g_up(0, 0, 1)
    q_z(1)
    q_cross(1, "u")
    g_down(0, 0, 1)
    multiply(0, 3, 1)
    q_cross(1, "d")
    multiply(0, 1, 1)
    block(1, 2, 0)
    multiply(0, 2, 0)
    block(1, 0, 1)
    multiply(0, 2, 1)
    project_end(0)
    block(1, 2, 1)
    block(1, 3, 1)
    block(1, 1, 0)
    q_up(0)
    q_down(0)
    block(1, 1, 1)
    c_join(1, 0, 0)
    c_join(1, 0, 1)
    c_join(1, 1, 0)
    block(0, 0, 1)
    q_cross(0, "u")
    c_join(1, 1, 1)
    q_z(0)
    q_cross(0, "d")
    block(0, 2, 0)
    plane_merge(1, 0)
    block(0, 1, 0)
    plane_merge(1, 1)
    fresh_tokens(0)
    block(0, 2, 1)
    last_merge(1, 0)
    block(0, 1, 1)
    last_merge(1, 1)
    d_far(1, 1)
    d_far(1, 0)
    d_near(1, 3, 1)
    block(0, 3, 1)
    c_join(0, 1, 0)
    c_join(0, 0, 0)
    d_near(1, 1, 1)
    c_join(0, 1, 1)
    d_join(1, "p", 3)
    d_near(1, 1, 0)
    block(0, 3, 0)
    d_join(1, "p", 1)
    r_far(1)
    d_near(1, 3, 0)
    d_join(1, "q", 3)
    plane_merge(0, 0)
    d_join(1, "q", 1)
    c_join(0, 0, 1)
    plane_merge(0, 1)
    block(0, 0, 0)
    d_own(1, 1)
    r_near(1, 1)
    d_own(1, 0)
    r_near(1, 3)
    d_join(1, "r", 3)
    last_merge(0, 0)
    d_cross(1)
    d_join(1, "r", 1)
    last_merge(0, 1)
    d_own(0, 0)
    d_far(0, 1)
    d_far(0, 0)
    d_near(0, 1, 1)
    d_end(1, 1)
    d_near(0, 3, 1)
    d_join(0, "p", 3)
    d_end(1, 0)
    d_own(0, 1)
    d_join(0, "p", 1)
    r_far(0)
    d_near(0, 3, 0)
    d_join(0, "q", 3)
    d_near(0, 1, 0)
    r_near(0, 1)
    d_cross(0)
    d_join(0, "r", 1)
    d_join(0, "q", 1)
    r_near(0, 3)
    d_join(0, "r", 3)
    d_end(0, 1)
    d_end(0, 0)
    for copy in made.values():
        copy.wait_send()


def call(*operands):
    vm = pl.BlockSpec(memory_space=pltpu.VMEM)
    anywhere = pl.BlockSpec(memory_space=pl.ANY)
    n, r = CHUNKS, ROWS
    trees, tile = (n, TREES, 128, 128), (8, 128)
    stat = (n,) + tile
    shapes = [
        ((64, 128), BF), ((8, 1, 1024), F32), ((1, 128), jnp.int32), ((1, 64), F32), ((2, 128, 64), F32), ((2, 128, 64), F32),
        (tile, jnp.int32), ((1, 2048), jnp.int32),
        ((n, 4, 2, 2 * r, 1024), BF), ((4, 2) + tile, F32), ((n, 2 * r, 128), F32), ((8, 1024, 768), BF),
        ((n, 2 * r, 768), F32), ((512, 8192), BF), ((256, 64, 128), BF), ((256, 64, 128), BF), ((128, 512), F32),
        ((2, 64, 16, 512), BF), ((64, 16, 512), BF), (tile, jnp.int32), None,
        ((4, 2) + trees, BF), ((n, TREES * 32, 128), BF), ((n, TREES * 32, 256), BF),
        ((4, 2) + trees, BF), ((4, 2) + stat, F32), ((2, 2) + trees, BF), ((2, 2) + stat, F32),
        ((2,) + trees, BF), ((2,) + stat, F32), ((2,) + stat, F32), ((2,) + trees, BF), ((2,) + stat, F32),
        (trees, BF), (stat, F32),
        ((TREES, 1024, 256), BF), ((n, 2 * r, 512), BF), ((n, 2, 4, 2 * r, 1024), BF),
        ((n, 2, 3, 2 * r, 1024), BF), ((n, 4, 2 * r, 1024), BF),
    ]
    scratch = [pltpu.VMEM(*s) if s else pltpu.SMEM((2, 8, 128), jnp.int32) for s in shapes]
    return pl.pallas_call(
        kernel,
        out_shape=jax.ShapeDtypeStruct((2, 128, 1024), BF),
        in_specs=[anywhere] * 13,
        out_specs=vm,
        scratch_shapes=scratch
        + [pltpu.SemaphoreType.DMA((196,)), pltpu.SemaphoreType.DMA((196,)), pltpu.SemaphoreType.DMA((40,))],
        compiler_params=pltpu.CompilerParams(
            collective_id=1, has_side_effects=True, vmem_limit_bytes=60 * 2**20
        ),
        cost_estimate=pl.CostEstimate(flops=15 * 10**9, bytes_accessed=30 * 2**20, transcendentals=10**7),
    )(*operands)


def body(
    hidden,
    norm_gain,
    w_query,
    key_weight,
    value_weight,
    w_out,
    key_cache,
    value_cache,
    tree_pages,
    page_fill,
    row_depth,
    row_length,
):
    ladder = np.arange(64, dtype=np.float32) * np.float32(2.0 / 128)
    frequency = jnp.asarray(np.power(np.float32(ROPE_BASE), -ladder)[None, :])
    pages, fill = jnp.transpose(tree_pages[0]), jnp.transpose(page_fill[0])
    return call(
        hidden, norm_gain.reshape(64, 128), row_length[None, :], frequency, pages, fill, row_depth, w_query, key_weight, value_weight, w_out,
        key_cache.reshape(128, 64, 128), value_cache.reshape(128, 64, 128),
    )


def solution(mesh):
    in_specs = (
        P(None, "cache", "head"),
        P(),
        P(None, "head"),
        P(None, "head"),
        P(None, "head"),
        P("head", None),
        P("cache", None, "head", None),
        P("cache", None, "head", None),
        P("cache", None, None),
        P("cache", None, None),
        P("cache", None),
        P("cache"),
    )
    out_specs = P(None, "cache", "head")
    return jax.shard_map(body, mesh=mesh, in_specs=in_specs, out_specs=out_specs, check_vma=False)
```
